32 devices in a mesh: dp: 8 (over z, y), mp: 4 (over x, core).
Axes of the slice: x: 2, y: 2, z: 4, core: 2. Of those that a mesh axis runs over, the one named last changes fastest.
Arguments:
- inputs: bfloat16 [8192, 1024], P(('dp', 'mp')), may hold values from -6 to 6
- teacher: bfloat16 [8192, 1024], P(('dp', 'mp')), may hold values from -6 to 6
- segments: int32 [8, 1024], P('dp'), may hold values from 0 to 7, never falling along the last dimension, each value on 1 to 768 neighbouring positions
- valid_mask: int32 [8192], P(('dp', 'mp')), may hold values from 0 to 1, as said below
- qkv_copy: bfloat16 [1024, 3, 1024], P(None, None, 'mp'), may hold values from -0.1875 to 0.1875
- out_copy: bfloat16 [1024, 1024], P('mp'), may hold values from -0.5 to 0.5
- up_copy: bfloat16 [1024, 4096], P(None, 'mp'), may hold values from -0.1875 to 0.1875
- down_copy: bfloat16 [4096, 1024], P('mp'), may hold values from -0.09375 to 0.09375
- vector_copy: bfloat16 [12, 1024], replicated
- qkv_state: float32 [3, 1024, 3, 1024], P(None, 'dp', None, 'mp'), as said below
- out_state: float32 [3, 1024, 1024], P(None, 'mp', 'dp'), as said below
- up_state: float32 [3, 1024, 4096], P(None, 'dp', 'mp'), as said below
- down_state: float32 [3, 4096, 1024], P(None, 'mp', 'dp'), as said below
- vector_state: float32 [3, 12, 1024], replicated, as said below
Outputs:
- block_out: bfloat16 [8192, 1024], P(('dp', 'mp'))
- input_grad: float32 [8192, 1024], P(('dp', 'mp'))
- qkv_grad: float32 [1024, 3, 1024], P('dp', None, 'mp')
- out_grad: float32 [1024, 1024], P('mp', 'dp')
- up_grad: float32 [1024, 4096], P('dp', 'mp')
- down_grad: float32 [4096, 1024], P('mp', 'dp')
- vector_grad: float32 [12, 1024], replicated
- qkv_state_new: float32 [3, 1024, 3, 1024], P(None, 'dp', None, 'mp')
- out_state_new: float32 [3, 1024, 1024], P(None, 'mp', 'dp')
- up_state_new: float32 [3, 1024, 4096], P(None, 'dp', 'mp')
- down_state_new: float32 [3, 4096, 1024], P(None, 'mp', 'dp')
- vector_state_new: float32 [3, 12, 1024], replicated
- qkv_copy_new: bfloat16 [1024, 3, 1024], P(None, None, 'mp')
- out_copy_new: bfloat16 [1024, 1024], P('mp')
- up_copy_new: bfloat16 [1024, 4096], P(None, 'mp')
- down_copy_new: bfloat16 [4096, 1024], P('mp')
- vector_copy_new: bfloat16 [12, 1024], replicated
The draws below stay inside these ranges and needn't reach their ends.
Inputs may be any that keep to these rules, and one draw needn't show every extreme that they name: `segments`: ids never fall along a sequence. `valid_mask`: the first token of every sequence is 1. `qkv_state`: row 2 is positive. `out_state`: row 2 is positive. `up_state`: row 2 is positive. `down_state`: row 2 is positive. `vector_state`: row 2 is positive.
All inputs are finite; a program needn't handle non-finite values.
Results may differ from the reference program's by a relative error of at most 0.007.
The reference program's roundings to bfloat16 on the way count: a program that leaves them out, or rounds other values in their place, can miss the bound.
Values may be sent and summed in bfloat16 or wider, within the bound.
A program may use at most 128 MiB of HBM per device.

```python
import math
import jax
import jax.numpy as jnp
import numpy as np
from jax import lax

D = 1024
HEADS = 16
HD = 64
FF = 4096
LEN = 1024
BQ = 512
NSEQ = 8
TOKENS = 8192
VROWS = 12


def second_moment(subkey, array_shape, weight_scale):
    return weight_scale * jnp.exp(jax.random.uniform(subkey, array_shape, jnp.float32, math.log(0.25), 0.0))


def vector_layout():
    row_ids = jnp.arange(VROWS, dtype=jnp.int32)
    gain_rows = (row_ids == 0) | (row_ids == 3)
    centre = jnp.where(gain_rows, 1.0, 0.0).astype(jnp.float32)
    spread = jnp.where(gain_rows, 0.1, 0.3).astype(jnp.float32)
    return (centre[:, None], spread[:, None])


def stack_state(weight, moment, subkey, array_shape, weight_scale):
    return jnp.stack([weight, moment * weight_scale, second_moment(subkey, array_shape, weight_scale)])


def draw_valid_mask(key, part):
    key = jax.random.fold_in(key, 5)
    positions = jnp.arange(TOKENS, dtype=jnp.int32)
    levels = jax.random.randint(key, (TOKENS,), 0, 1000)
    barrier = 250 + 600 * positions // TOKENS
    heads_of_rows = positions % LEN == 0
    return jnp.where(heads_of_rows | (levels < barrier), 1, 0).astype(jnp.int32)


def draw_vector_copy(key, part):
    key = jax.random.fold_in(key, 7)
    centre, spread = vector_layout()
    base = jax.random.normal(key, (VROWS, D), jnp.float32)
    return (centre + spread * base).astype(jnp.bfloat16)


def draw_vector_state(key, part):
    key = jax.random.fold_in(key, 9)
    subkeys = jax.random.split(key, 3)
    centre, spread = vector_layout()
    array_shape = (VROWS, D)
    base = jax.random.normal(subkeys[0], array_shape, jnp.float32)
    moment = jax.random.normal(subkeys[1], array_shape, jnp.float32)
    return stack_state(centre + spread * base, moment, subkeys[2], array_shape, 0.3)


def draw_qkv_state(key, part):
    key = jax.random.fold_in(key, 11)
    subkeys = jax.random.split(key, 3)
    array_shape = (D, 3, D)
    weight = jax.random.normal(subkeys[0], array_shape, jnp.float32)
    moment = jax.random.normal(subkeys[1], array_shape, jnp.float32)
    scale = D ** (-0.5)
    return stack_state(weight * scale, moment, subkeys[2], array_shape, scale)


def draw_out_state(key, part):
    key = jax.random.fold_in(key, 13)
    subkeys = jax.random.split(key, 3)
    array_shape = (D, D)
    weight = jax.random.normal(subkeys[0], array_shape, jnp.float32)
    moment = jax.random.normal(subkeys[1], array_shape, jnp.float32)
    scale = (D // 8) ** (-0.5)
    return stack_state(weight * scale, moment, subkeys[2], array_shape, scale)


def draw_up_state(key, part):
    key = jax.random.fold_in(key, 17)
    subkeys = jax.random.split(key, 3)
    array_shape = (D, FF)
    weight = jax.random.normal(subkeys[0], array_shape, jnp.float32)
    moment = jax.random.normal(subkeys[1], array_shape, jnp.float32)
    scale = D ** (-0.5)
    return stack_state(weight * scale, moment, subkeys[2], array_shape, scale)


def draw_down_state(key, part):
    key = jax.random.fold_in(key, 19)
    subkeys = jax.random.split(key, 3)
    array_shape = (FF, D)
    weight = jax.random.normal(subkeys[0], array_shape, jnp.float32)
    moment = jax.random.normal(subkeys[1], array_shape, jnp.float32)
    scale = FF ** (-0.5)
    return stack_state(weight * scale, moment, subkeys[2], array_shape, scale)


def strengthened(values, own_key, source, target, parts, factor):
    def block_of(dim):
        return (jnp.arange(values.shape[dim]) // (values.shape[dim] // parts)).reshape((-1,) + (1,) * (values.ndim - 1 - dim))

    one_side = jax.random.permutation(own_key, parts)[block_of(target)]
    far = (block_of(target) + parts // 2) % parts
    return jnp.where((block_of(source) == one_side) | (block_of(source) == far), factor * values, values)


def block_scale(own_key, extent, shards, least, largest):
    def one(position, parts):
        draws = jax.random.uniform(jax.random.fold_in(jax.random.fold_in(own_key, 6), position), (parts,), jnp.float32, least / len(shards), largest / len(shards))
        return jnp.repeat(jnp.exp(draws), extent[position] // parts).reshape((-1,) + (1,) * (len(extent) - position - 1))

    level = one(*shards[0])
    for cut in shards[1:]:
        level = level * one(*cut)
    return level


def length_profile(number_of, total, bound, skew):
    weights = [(1 << 20) // math.isqrt(rank ** skew) + 1 for rank in range(2, number_of + 1)]
    surplus, holding = total - bound - (number_of - 1), [1] * (number_of - 1)
    while surplus > 0:
        movable = [i for i in range(number_of - 1) if holding[i] < bound]
        pool, left = sum([weights[i] for i in movable]), surplus
        for i in movable:
            addition = min(bound - holding[i], max(1, left * weights[i] // pool), surplus)
            holding[i] = holding[i] + addition
            surplus = surplus - addition
    return np.array([bound] + holding)


def ragged(own_key, number_of, total, reach, slope):
    if number_of == 2:
        one = jax.random.randint(own_key, (), max(1, total - reach), min(reach, total - 1) + 1)
        return jnp.stack([one, total - one])
    lengths = jnp.asarray(length_profile(number_of, total, reach, slope), jnp.int32)
    couples = (number_of - 1) // 2
    source_of, receiver = lengths[1:1 + 2 * couples:2], lengths[2:2 + 2 * couples:2]
    slack = jnp.minimum(source_of - 1, reach - receiver)
    passed = jax.random.randint(jax.random.fold_in(own_key, 1), (couples,), 0, 1 << 20) % (slack + 1)
    lengths = lengths.at[1:1 + 2 * couples:2].set(source_of - passed).at[2:2 + 2 * couples:2].set(receiver + passed)
    return lengths[jax.random.permutation(jax.random.fold_in(own_key, 2), number_of)]


def noise(rng, dims, width, bound, cuts=(), held_as=jnp.bfloat16):
    drawn = jax.random.normal(rng, dims, jnp.float32) * width
    if len(cuts) > 0:
        drawn = block_scale(rng, dims, cuts, -0.22, 0.18) * drawn
    return jnp.clip(drawn, min=-bound, max=bound).astype(held_as)


def gaussian_with(key, extent, width, most, pieces, heavy, held_as=jnp.bfloat16):
    entries = width * jax.random.normal(key, extent, jnp.float32)
    if pieces:
        entries = entries * block_scale(key, extent, pieces, -0.22, 0.18)
    return jnp.clip(strengthened(entries, jax.random.fold_in(key, 3), *heavy), -most, most).astype(held_as)


def setup_inputs(seed: int = 0) -> dict:
    seeds = jax.random.split(jax.random.key(seed), 15)
    return {
        "inputs": noise(seeds[0], (TOKENS, D), 1.0, 6.0, ((0, 32),)),
        "teacher": gaussian_with(seeds[1], (TOKENS, D), 1.0, 6.0, ((0, 32),), (0, 1, 32, 2.75)),
        "segments": jax.vmap(lambda own: jnp.searchsorted(jnp.cumsum(ragged(own, 8, LEN, 3 * LEN // 4, 2)), jnp.arange(LEN), side="right"))(jax.random.split(seeds[2], NSEQ)).reshape((NSEQ, LEN)).astype(jnp.int32),
        "valid_mask": draw_valid_mask(jax.random.fold_in(seeds[14], 71), 0),
        "qkv_copy": noise(seeds[4], (D, 3, D), D ** -0.5, 0.1875, ((2, 4),)),
        "out_copy": noise(seeds[5], (D, D), (D // 8) ** -0.5, 0.5, ((0, 4),)),
        "up_copy": noise(seeds[6], (D, FF), D ** -0.5, 0.1875, ((1, 4),)),
        "down_copy": noise(seeds[7], (FF, D), FF ** -0.5, 0.09375, ((0, 4),)),
        "vector_copy": draw_vector_copy(jax.random.fold_in(seeds[14], 71), 0),
        "qkv_state": draw_qkv_state(jax.random.fold_in(seeds[14], 71), 0),
        "out_state": draw_out_state(jax.random.fold_in(seeds[14], 71), 0),
        "up_state": draw_up_state(jax.random.fold_in(seeds[14], 71), 0),
        "down_state": draw_down_state(jax.random.fold_in(seeds[14], 71), 0),
        "vector_state": draw_vector_state(jax.random.fold_in(seeds[14], 71), 0),
    }


@jax.custom_vjp
def low(v):
    return lax.optimization_barrier(v.astype(jnp.bfloat16)).astype(jnp.float32)

@jax.custom_vjp
def low_back(v):
    return v

def low_keep(v):
    return (low(v), None)

def low_pass(kept, grad):
    return (grad,)

def back_keep(v):
    return (v, None)

def back_low(kept, grad):
    return (low(grad),)
low.defvjp(low_keep, low_pass)
low_back.defvjp(back_keep, back_low)
highest = lax.Precision.HIGHEST
norm_eps = 1e-05
beta_one = 0.9
beta_two = 0.95
adam_eps = 1e-08
learn_rate = 0.001
decay_rate = 0.1
correction_one = 1.0 - (0.9 ** 10) ** 10
correction_two = 1.0 - (0.95 ** 10) ** 10
masked_value = -1e+30

def gelu_tanh(operand):
    return 0.5 * operand * (1.0 + jnp.tanh(0.7978845608 * (operand + 0.044715 * operand * operand * operand)))

def layer_norm(operand, gain_row, shift_row):
    centred = operand - lax.optimization_barrier(jnp.mean(operand, -1, keepdims=True))
    inverse = lax.rsqrt(lax.optimization_barrier(jnp.mean(centred * centred, -1, keepdims=True)) + norm_eps)
    return centred * inverse * gain_row + shift_row

def attend_block(block_query, key_heads, value_heads, block_segments, segment_ids, first_row, slopes):
    score_scale = 1.0 / math.sqrt(HD)
    raw_scores = low_back(jnp.einsum('qhd,khd->hqk', block_query, key_heads, precision=highest))
    query_rows = first_row + jnp.arange(block_query.shape[0], dtype=jnp.int32)
    key_rows = jnp.arange(key_heads.shape[0], dtype=jnp.int32)
    distance = query_rows[:, None] - key_rows[None, :]
    allowed = (distance >= 0) & (block_segments[:, None] == segment_ids[None, :])
    scores = raw_scores * score_scale - slopes[:, None, None] * distance.astype(jnp.float32)[None]
    scores = jnp.where(allowed[None], scores, masked_value)
    row_top = lax.optimization_barrier(jnp.max(scores, -1, keepdims=True))
    exponent = jnp.exp(scores - row_top)
    probability = low(exponent / lax.optimization_barrier(jnp.sum(exponent, -1, keepdims=True)))
    return jnp.einsum('hqk,khd->qhd', probability, value_heads, precision=highest)

def attend_sequence(queries, key_heads, value_heads, segment_ids, slopes):
    block_count = LEN // BQ
    block_items = (queries.reshape(block_count, BQ, HEADS, HD), segment_ids.reshape(block_count, BQ), jnp.arange(block_count, dtype=jnp.int32) * BQ)

    def one_block(block_item):
        return jax.checkpoint(attend_block)(block_item[0], key_heads, value_heads, block_item[1], segment_ids, block_item[2], slopes)
    return lax.map(one_block, block_items).reshape(LEN, HEADS, HD)

def split_heads(operand, group_size):
    return operand.reshape(group_size, LEN, HEADS, HD)

def block_forward(weights, source_rows, segment_rows, slopes):
    qkv_weight, out_weight, up_weight, down_weight, vectors = weights
    row_count = source_rows.shape[0]
    group_size = row_count // LEN
    norm_one = low(layer_norm(source_rows, vectors[0], vectors[1]))
    projected = jnp.einsum('rd,dce->rce', norm_one, qkv_weight, precision=highest)
    queries = low(low_back(projected[:, 0] + vectors[6]))
    key_heads = low(low_back(projected[:, 1]))
    value_heads = low(low_back(projected[:, 2] + vectors[7]))

    def attend_group(seq_item):
        return attend_sequence(seq_item[0], seq_item[1], seq_item[2], seq_item[3], slopes)
    mixture = lax.map(attend_group, (split_heads(queries, group_size), split_heads(key_heads, group_size), split_heads(value_heads, group_size), segment_rows))
    mixture = low(low_back(mixture.reshape(row_count, D)))
    hidden = source_rows + low_back(jnp.dot(mixture, out_weight, precision=highest)) + vectors[2]
    norm_two = low(layer_norm(hidden, vectors[3], vectors[4]))
    up_value = low_back(jnp.dot(norm_two, up_weight, precision=highest) + vectors[8:].reshape(FF))
    activated = low(gelu_tanh(up_value))
    return hidden + low_back(jnp.dot(activated, down_weight, precision=highest)) + vectors[5]

def adam_update(gradient, stored, decay_factor, token_total):
    weight = stored[0]
    mean_grad = gradient / token_total
    moment_one = beta_one * stored[1] + (1.0 - beta_one) * mean_grad
    moment_two = beta_two * stored[2] + (1.0 - beta_two) * mean_grad * mean_grad
    update = moment_one / correction_one / (jnp.sqrt(moment_two / correction_two) + adam_eps) + decay_factor * weight
    weight = weight - learn_rate * update
    return (jnp.stack([weight, moment_one, moment_two]), weight.astype(jnp.bfloat16))

def reference(inputs, teacher, segments, valid_mask, qkv_copy, out_copy, up_copy, down_copy, vector_copy, qkv_state, out_state, up_state, down_state, vector_state):
    valid_float = valid_mask.astype(jnp.float32)
    token_count = jnp.sum(valid_float)
    loss_scale = TOKENS / token_count
    slopes = jnp.exp2(-8.0 * (jnp.arange(HEADS).astype(jnp.float32) + 1.0) / HEADS)
    group_size = math.gcd(NSEQ, max(1, 4096 // LEN))
    step_total = NSEQ // group_size
    rows_step = group_size * LEN
    teacher_steps = teacher.astype(jnp.float32).reshape(step_total, rows_step, D)
    segment_steps = segments.reshape(step_total, group_size, LEN)
    valid_steps = valid_float.reshape(step_total, rows_step)

    def total_loss(weights, source):

        def one_step(carried, step_item):
            source_rows, teacher_rows, segment_rows, valid_rows = step_item
            output = jax.checkpoint(block_forward)(weights, source_rows, segment_rows, slopes)
            differ = output - teacher_rows
            return (carried + 0.5 * loss_scale * jnp.sum(valid_rows[:, None] * differ * differ), output)
        loss_value, outputs = lax.scan(one_step, jnp.zeros((), jnp.float32), (source.reshape(step_total, rows_step, D), teacher_steps, segment_steps, valid_steps))
        return (loss_value, outputs.reshape(TOKENS, D))
    weights = (qkv_copy.astype(jnp.float32), out_copy.astype(jnp.float32), up_copy.astype(jnp.float32), down_copy.astype(jnp.float32), vector_copy.astype(jnp.float32))
    loss_value, pullback, output = jax.vjp(total_loss, weights, inputs.astype(jnp.float32), has_aux=True)
    weight_grads, input_grad = pullback(jnp.ones((), jnp.float32))
    qkv_grad, out_grad, up_grad, down_grad, vector_grad = weight_grads
    qkv_new, qkv_low = adam_update(qkv_grad, qkv_state, decay_rate, TOKENS)
    out_new, out_low = adam_update(out_grad, out_state, decay_rate, TOKENS)
    up_new, up_low = adam_update(up_grad, up_state, decay_rate, TOKENS)
    down_new, down_low = adam_update(down_grad, down_state, decay_rate, TOKENS)
    vector_new, vector_low = adam_update(vector_grad, vector_state, 0.0, TOKENS)
    return (output.astype(jnp.bfloat16), input_grad, qkv_grad, out_grad, up_grad, down_grad, vector_grad, qkv_new, out_new, up_new, down_new, vector_new, qkv_low, out_low, up_low, down_low, vector_low)
```

```python
import functools
import math

import jax
import jax.numpy as jnp
from jax import lax
from jax.experimental import pallas as pl
from jax.experimental.pallas import tpu as pltpu
from jax.sharding import PartitionSpec as P

HEADS = 16
HD = 64

norm_eps = 1e-05
beta_one = 0.9
beta_two = 0.95
adam_eps = 1e-08
learn_rate = 0.001
decay_rate = 0.1
correction_one = 1.0 - (0.9**10) ** 10
correction_two = 1.0 - (0.95**10) ** 10
log2_e = 1.4426950408889634

CHUNKS = 2
BQ = 256
TILE = 256
MESH = pl.DeviceIdType.MESH
F32 = jnp.float32
BF16 = jnp.bfloat16
NN = ((1,), (0,))
NT = ((1,), (1,))
TN = ((0,), (0,))


def mm(a, b, dims):
    return lax.dot_general(a, b, (dims, ((), ())), preferred_element_type=F32)


def gelu_both(v):
    c = 0.7978845608
    v2 = v * v
    th = jnp.tanh(c * (v + 0.044715 * v2 * v))
    half = 0.5 * (1.0 + th)
    back = half + 0.5 * v * (1.0 - th * th) * (c * (1.0 + 3.0 * 0.044715 * v2))
    return v * half, back


def norm_rows(v):
    centred = v - jnp.mean(v, -1, keepdims=True)
    inverse = lax.rsqrt(jnp.mean(centred * centred, -1, keepdims=True) + norm_eps)
    return centred * inverse, inverse


def norm_backward(grad_out, normed, inverse, gain_row):
    scaled = grad_out * gain_row
    return inverse * (
        scaled
        - jnp.mean(scaled, -1, keepdims=True)
        - normed * jnp.mean(scaled * normed, -1, keepdims=True)
    )


def block_kernel(
    sizes,
    x_ref, t_ref, segr_ref, segc_ref, valid_ref, vec_ref,
    wqkv_hbm, wout_hbm, wup_hbm, wdown_hbm,
    bo_ref, ig_ref, vg_ref, dqkv_hbm, dout_hbm, dup_hbm, ddown_hbm,
    wqkv, wout, wup, wdown, w_sem,
    g1, g2, g3, g4, qkv, qT, kT, vT, mixT, mix, lse, dist,
    hidden, n1, n2, inv1, inv2, go, act, gelub, gup,
    gm, gmT, gk, gv, gqT, st,
    tmp, keep, rs_cs, rs_cr, rs_xs, rs_xr,
    cnt, cnt_r, stage, stage_sem,
    ag_ss, ag_rs, rs_ss, rs_rs, cnt_ss, cnt_rs,
):
    dp_size, mp_size = sizes
    dp = lax.axis_index("dp")
    m = lax.axis_index("mp")
    core = lax.rem(m, 2)
    chip = m // 2
    mc = m + 1 - 2 * core
    mx = lax.rem(m + 2, 4)
    md = mc + mx - m
    C = CHUNKS
    R, D = x_ref.shape
    rc = R // C
    T = mp_size * R
    HW = wout.shape[0]
    FU = wup.shape[1]

    bits = []
    for b in range(mp_size.bit_length() - 1):
        bits.append(("mp", b))
    for b in range(dp_size.bit_length() - 1):
        bits.append(("dp", b))

    def flip(v, b):
        w = 1 << b
        return v + w - 2 * w * lax.rem(v // w, 2)

    def bit_partner(item):
        axis, b = item
        if axis == "mp":
            return (dp, flip(m, b))
        return (flip(dp, b), m)

    to_core = (dp, mc)
    to_x = (dp, mx)

    weights = [
        pltpu.make_async_copy(src, dst, w_sem.at[i])
        for i, (src, dst) in enumerate(
            [(wqkv_hbm, wqkv), (wout_hbm, wout), (wup_hbm, wup), (wdown_hbm, wdown)]
        )
    ]
    for w in weights:
        w.start()

    barrier = pltpu.get_barrier_semaphore()
    for item in bits:
        pl.semaphore_signal(barrier, inc=1, device_id=bit_partner(item), device_id_type=MESH)
    pl.semaphore_wait(barrier, len(bits))

    def small_copy(step, src, dst):
        return pltpu.make_async_remote_copy(
            src_ref=src, dst_ref=dst, send_sem=cnt_ss.at[step], recv_sem=cnt_rs.at[step],
            device_id=bit_partner(bits[step]), device_id_type=MESH,
        )

    cnt[0] = jnp.zeros((8, 128), F32) + jnp.sum(valid_ref[...])

    count_copies = []

    def count_send(step):
        cp = small_copy(step, cnt.at[step], cnt_r.at[step])
        cp.start()
        count_copies.append(cp)

    def count_next(step):
        count_copies[step].wait()
        cnt[step + 1] = cnt[step] + cnt_r[step]
        if step + 1 < len(bits):
            count_send(step + 1)

    count_send(0)

    def ag_copy(site, j, kind, ref, block, device):
        part = ref.at[block, pl.ds(j * rc, rc)]
        return pltpu.make_async_remote_copy(
            src_ref=part, dst_ref=part, send_sem=ag_ss.at[site, j, kind],
            recv_sem=ag_rs.at[site, j, kind], device_id=device, device_id_type=MESH,
        )

    def ag_start(site, j, ref, value):
        ref[m, pl.ds(j * rc, rc), :] = value
        cx = ag_copy(site, j, 0, ref, m, to_x)
        cx.start()
        cc = ag_copy(site, j, 1, ref, m, to_core)
        cc.start()
        return cx, cc

    def ag_forward(site, j, ref):
        cf = ag_copy(site, j, 2, ref, mx, to_core)
        cf.start()
        return cf

    def rs_copy(site, j, kind, src, dst, device):
        return pltpu.make_async_remote_copy(
            src_ref=src, dst_ref=dst, send_sem=rs_ss.at[site, j, kind],
            recv_sem=rs_rs.at[site, j, kind], device_id=device, device_id_type=MESH,
        )

    def rs_start(site, j, lhs_of, rhs_of):
        def product(first, slot):
            lhs = lhs_of(first)

            def tile_body(n, carry):
                lanes = pl.ds(pl.multiple_of(n * TILE, TILE), TILE)
                rhs, dims = rhs_of(lanes)
                tmp[slot, :, :, lanes] = mm(lhs, rhs, dims).reshape(2, rc, TILE)
                return carry

            lax.fori_loop(0, D // TILE, tile_body, 0)

        product(2 * (1 - chip), 0)
        rs_cs[j, 0] = tmp[0, 1 - core].astype(BF16)
        c0 = rs_copy(site, j, 0, rs_cs.at[j, 0], rs_cr.at[j, 0], to_core)
        c0.start()
        product(2 * chip, 1)
        rs_cs[j, 1] = tmp[1, 1 - core].astype(BF16)
        c1 = rs_copy(site, j, 1, rs_cs.at[j, 1], rs_cr.at[j, 1], to_core)
        c1.start()
        keep[j] = tmp[1, core]
        c0.wait()
        rs_xs[j] = (tmp[0, core] + rs_cr[j, 0].astype(F32)).astype(BF16)
        cx = rs_copy(site, j, 2, rs_xs.at[j], rs_xr.at[j], to_x)
        cx.start()
        return c1, cx

    def rs_finish(j, copies):
        for cp in copies:
            cp.wait()
        return keep[j] + rs_cr[j, 1].astype(F32) + rs_xr[j].astype(F32)

    vg_ref[...] = jnp.zeros(vg_ref.shape, F32)
    ag = {}
    for j in range(C):
        rows = slice(j * rc, (j + 1) * rc)
        normed, inverse = norm_rows(x_ref[rows, :].astype(F32))
        n1[rows, :] = normed
        inv1[rows, :] = inverse
        ag[j] = ag_start(0, j, g1, (normed * vec_ref[0:1, :] + vec_ref[1:2, :]).astype(BF16))

    head_lanes = pl.ds(pl.multiple_of(m * HW, HW), HW)
    weights[0].wait()

    def project(o):
        p = mm(g1[o], wqkv[...], NN)
        at = pl.ds(pl.multiple_of(o * R, R), R)
        q = (p[:, :HW] + vec_ref[6:7, head_lanes]).astype(BF16)
        k = p[:, HW : 2 * HW].astype(BF16)
        v = (p[:, 2 * HW :] + vec_ref[7:8, head_lanes]).astype(BF16)
        qkv[at, 0:HW] = q
        qkv[at, HW : 2 * HW] = k
        qkv[at, 2 * HW :] = v
        qT[:, at] = q.T
        kT[:, at] = k.T
        vT[:, at] = v.T

    project(m)
    count_next(0)
    for j in range(C):
        ag[j][1].wait()
    project(mc)
    count_next(1)
    fw = {}
    for j in range(C):
        ag[j][0].wait()
        fw[j] = ag_forward(0, j, g1)
    project(mx)
    for j in range(C):
        fw[j].wait()
    project(md)

    pair_row = lax.broadcasted_iota(jnp.int32, (2 * HD, BQ), 0) // HD
    pair_lane = lax.broadcasted_iota(jnp.int32, (BQ, 2 * HD), 1) // HD
    scale2 = log2_e / math.sqrt(HD)

    def make_dist(i, ke):
        key = lax.broadcasted_iota(jnp.int32, (ke, BQ), 0)
        query = lax.broadcasted_iota(jnp.int32, (ke, BQ), 1) + i * BQ
        apart = query - key
        allowed = (apart >= 0) & (segc_ref[0:ke, :] == segr_ref[:, i * BQ : (i + 1) * BQ])
        dist[0:ke, :] = jnp.where(allowed, apart.astype(F32), jnp.inf)

    def head_slope(h):
        head = jnp.zeros((1, BQ), jnp.int32) + (m * (HW // HD) + h + 1)
        return jnp.exp2(head.astype(F32) * (-8.0 / HEADS)) * log2_e

    def head_scores(i, ke, h):
        lanes = pl.ds(pl.multiple_of((h // 2) * 2 * HD, 2 * HD), 2 * HD)
        k_lanes = pl.ds(pl.multiple_of(HW + (h // 2) * 2 * HD, 2 * HD), 2 * HD)
        mask = (pair_row == lax.rem(h, 2)).astype(F32).astype(BF16)
        q_cols = qT[lanes, i * BQ : (i + 1) * BQ] * mask
        raw = mm(qkv[0:ke, k_lanes], q_cols, NN)
        return raw * scale2 - head_slope(h) * dist[0:ke, :]

    n_blocks = T // BQ
    for i in range(n_blocks):
        ke = (i + 1) * BQ
        make_dist(i, ke)

        def head_body(h, carry):
            s = head_scores(i, ke, h)
            top = jnp.max(s, 0, keepdims=True)
            e = jnp.exp2(s - top)
            total = jnp.sum(e, 0, keepdims=True)
            p = (e * (1.0 / total)).astype(BF16)
            lse[h, :, i * BQ : (i + 1) * BQ] = top + jnp.log2(total)
            at = pl.ds(pl.multiple_of(h * HD, HD), HD)
            mixT[at, i * BQ : (i + 1) * BQ] = mm(vT[at, 0:ke], p, NN).astype(BF16)
            return carry

        lax.fori_loop(0, HW // HD, head_body, 0)
        mix[i * BQ : (i + 1) * BQ, :] = mixT[:, i * BQ : (i + 1) * BQ].T
        if i < len(bits) - 2:
            count_next(i + 2)
    for step in range(2 + n_blocks, len(bits)):
        count_next(step)

    def rows4(ref, j):
        v = ref[:, pl.ds(j * rc, rc), :]
        return v.reshape(v.shape[0] * rc, v.shape[2])

    def pair_rows(ref, j):
        def of(first):
            v = ref[pl.ds(first, 2), pl.ds(j * rc, rc), :]
            return v.reshape(2 * rc, v.shape[2])

        return of

    def pair_mix(j):
        def of(first):
            a = mix[pl.ds(pl.multiple_of(first * R + j * rc, rc), rc), :]
            b = mix[pl.ds(pl.multiple_of(first * R + R + j * rc, rc), rc), :]
            return jnp.concatenate([a, b], 0)

        return of

    weights[1].wait()
    rs = {}
    for j in range(C):
        rs[j] = rs_start(0, j, pair_mix(j), lambda lanes: (wout[:, lanes], NN))
    for j in range(C):
        rows = slice(j * rc, (j + 1) * rc)
        hid = x_ref[rows, :].astype(F32) + rs_finish(j, rs[j]) + vec_ref[2:3, :]
        hidden[rows, :] = hid
        normed, inverse = norm_rows(hid)
        n2[rows, :] = normed
        inv2[rows, :] = inverse
        ag[j] = ag_start(1, j, g2, (normed * vec_ref[3:4, :] + vec_ref[4:5, :]).astype(BF16))

    def ag_finish(site, j, ref):
        ag[j][0].wait()
        cf = ag_forward(site, j, ref)
        ag[j][1].wait()
        cf.wait()

    weights[2].wait()
    weights[3].wait()
    for j in range(C):
        ag_finish(1, j, g2)
        rows = rows4(g2, j)

        def up_body(n, carry):
            lanes = pl.ds(pl.multiple_of(n * TILE, TILE), TILE)
            u = mm(rows, wup[:, lanes], NN) + vec_ref[pl.ds(8 + m, 1), lanes]
            a, b = gelu_both(u)
            act[:, pl.ds(j * rc, rc), lanes] = a.astype(BF16).reshape(mp_size, rc, TILE)
            gelub[:, pl.ds(j * rc, rc), lanes] = b.reshape(mp_size, rc, TILE)
            return carry

        lax.fori_loop(0, FU // TILE, up_body, 0)
        rs[j] = rs_start(1, j, pair_rows(act, j), lambda lanes: (wdown[:, lanes], NN))

    loss_scale = float(dp_size * mp_size * R) / cnt[len(bits), 0:1, 0:1]
    for j in range(C):
        rows = slice(j * rc, (j + 1) * rc)
        out = hidden[rows, :] + rs_finish(j, rs[j]) + vec_ref[5:6, :]
        bo_ref[rows, :] = out.astype(BF16)
        grad = valid_ref[rows, :] * (out - t_ref[rows, :].astype(F32)) * loss_scale
        go[rows, :] = grad
        ag[j] = ag_start(2, j, g3, grad.astype(BF16))
        vg_ref[5:6, :] += jnp.sum(grad, 0, keepdims=True)

    for j in range(C):
        ag_finish(2, j, g3)
        rows = rows4(g3, j)

        def act_body(n, carry):
            lanes = pl.ds(pl.multiple_of(n * TILE, TILE), TILE)
            ga = mm(rows, wdown[lanes, :], NT)
            gu = ga * gelub[:, pl.ds(j * rc, rc), lanes].reshape(mp_size * rc, TILE)
            gup[:, pl.ds(j * rc, rc), lanes] = gu.astype(BF16).reshape(mp_size, rc, TILE)
            return carry

        lax.fori_loop(0, FU // TILE, act_body, 0)
        rs[j] = rs_start(2, j, pair_rows(gup, j), lambda lanes: (wup[lanes, :], NT))

    def put_out(src, dst):
        cp = pltpu.make_async_copy(src, dst, stage_sem)
        cp.start()
        cp.wait()

    def down_body(n, carry):
        lanes = pl.ds(pl.multiple_of(n * TILE, TILE), TILE)
        left = act[:, :, lanes].reshape(T, TILE)
        stage[...] = mm(left, g3[...].reshape(T, D), TN)
        put_out(stage, ddown_hbm.at[lanes, :])
        return carry

    lax.fori_loop(0, FU // TILE, down_body, 0)

    for j in range(C):
        rows = slice(j * rc, (j + 1) * rc)
        gs = rs_finish(j, rs[j])
        gh = go[rows, :] + norm_backward(gs, n2[rows, :], inv2[rows, :], vec_ref[3:4, :])
        hidden[rows, :] = gh
        ag[j] = ag_start(3, j, g4, gh.astype(BF16))
        vg_ref[2:3, :] += jnp.sum(gh, 0, keepdims=True)
        vg_ref[3:4, :] += jnp.sum(gs * n2[rows, :], 0, keepdims=True)
        vg_ref[4:5, :] += jnp.sum(gs, 0, keepdims=True)

    def up_grad_body(n, carry):
        lanes = pl.ds(pl.multiple_of(n * TILE, TILE), TILE)
        left = g2[:, :, lanes].reshape(T, TILE)
        stage[...] = mm(left, gup[...].reshape(T, FU), TN)
        put_out(stage, dup_hbm.at[lanes, :])
        return carry

    lax.fori_loop(0, D // TILE, up_grad_body, 0)
    vg_ref[pl.ds(8 + m, 1), :] = jnp.sum(gup[...].reshape(T, FU).astype(F32), 0, keepdims=True)

    for j in range(C):
        ag_finish(3, j, g4)

    def gm_body(o, carry):
        at = pl.ds(pl.multiple_of(o * R, R), R)
        gmx = mm(g4[o], wout[...], NT).astype(BF16)
        gm[at, :] = gmx
        gmT[:, at] = gmx.T
        return carry

    lax.fori_loop(0, mp_size, gm_body, 0)

    gk[...] = jnp.zeros(gk.shape, F32)
    gv[...] = jnp.zeros(gv.shape, F32)
    for i in range(n_blocks):
        ke = (i + 1) * BQ
        block = slice(i * BQ, (i + 1) * BQ)
        make_dist(i, ke)

        def back_body(h, carry):
            lanes = pl.ds(pl.multiple_of((h // 2) * 2 * HD, 2 * HD), 2 * HD)
            v_lanes = pl.ds(pl.multiple_of(2 * HW + (h // 2) * 2 * HD, 2 * HD), 2 * HD)
            row_mask = (pair_row == lax.rem(h, 2)).astype(F32).astype(BF16)
            lane_mask = (pair_lane == lax.rem(h, 2)).astype(F32).astype(BF16)
            p = jnp.exp2(head_scores(i, ke, h) - lse[h, :, block])
            gp = mm(qkv[0:ke, v_lanes], gmT[lanes, block] * row_mask, NN)
            inner = jnp.sum(p * gp, 0, keepdims=True)
            raw = (p * (gp - inner)).astype(BF16)
            gv[0:ke, lanes] += mm(p.astype(BF16), gm[block, lanes] * lane_mask, NN)
            gk[0:ke, lanes] += mm(raw, qkv[block, lanes] * lane_mask, NN)
            at = pl.ds(pl.multiple_of(h * HD, HD), HD)
            gqT[at, block] = mm(kT[at, 0:ke], raw, NN) * (1.0 / math.sqrt(HD))
            return carry

        lax.fori_loop(0, HW // HD, back_body, 0)
        st[block, 0:HW] = gqT[:, block].T.astype(BF16)
    st[:, HW : 2 * HW] = (gk[...] * (1.0 / math.sqrt(HD))).astype(BF16)
    st[:, 2 * HW :] = gv[...].astype(BF16)
    vg_ref[6:7, head_lanes] = jnp.sum(st[:, 0:HW].astype(F32), 0, keepdims=True)
    vg_ref[7:8, head_lanes] = jnp.sum(st[:, 2 * HW :].astype(F32), 0, keepdims=True)

    def pair_st(j):
        def of(first):
            a = st[pl.ds(pl.multiple_of(first * R + j * rc, rc), rc), :]
            b = st[pl.ds(pl.multiple_of(first * R + R + j * rc, rc), rc), :]
            return jnp.concatenate([a, b], 0)

        return of

    for j in range(C):
        rs[j] = rs_start(3, j, pair_st(j), lambda lanes: (wqkv[lanes, :], NT))

    def out_grad_body(n, carry):
        lanes = pl.ds(pl.multiple_of(n * TILE, TILE), TILE)
        stage[...] = mm(mix[:, lanes], g4[...].reshape(T, D), TN)
        put_out(stage, dout_hbm.at[lanes, :])
        return carry

    lax.fori_loop(0, HW // TILE, out_grad_body, 0)

    def qkv_grad_body(n, carry):
        lanes = pl.ds(pl.multiple_of(n * TILE, TILE), TILE)
        left = g1[:, :, lanes].reshape(T, TILE)
        stage[:, 0 : 3 * HW] = mm(left, st[...], TN)
        put_out(stage.at[:, 0 : 3 * HW], dqkv_hbm.at[lanes, :])
        return carry

    lax.fori_loop(0, D // TILE, qkv_grad_body, 0)

    for j in range(C):
        rows = slice(j * rc, (j + 1) * rc)
        gf = rs_finish(j, rs[j])
        ig_ref[rows, :] = hidden[rows, :] + norm_backward(
            gf, n1[rows, :], inv1[rows, :], vec_ref[0:1, :]
        )
        vg_ref[0:1, :] += jnp.sum(gf * n1[rows, :], 0, keepdims=True)
        vg_ref[1:2, :] += jnp.sum(gf, 0, keepdims=True)


def block_call(sizes, x, teacher, segments, valid, vectors, wqkv, wout, wup, wdown):
    dp_size, mp_size = sizes
    R, D = x.shape
    T = mp_size * R
    HW = wout.shape[0]
    FU = wup.shape[1]
    C = CHUNKS
    rc = R // C
    n_bits = (dp_size * mp_size).bit_length() - 1
    vmem = pl.BlockSpec(memory_space=pltpu.VMEM)
    anywhere = pl.BlockSpec(memory_space=pl.ANY)
    dma = pltpu.SemaphoreType.DMA
    V = pltpu.VMEM
    scratch = [
        V((D, 3 * HW), BF16), V((HW, D), BF16), V((D, FU), BF16), V((FU, D), BF16), dma((4,)),
        V((mp_size, R, D), BF16), V((mp_size, R, D), BF16), V((mp_size, R, D), BF16), V((mp_size, R, D), BF16),
        V((T, 3 * HW), BF16), V((HW, T), BF16), V((HW, T), BF16), V((HW, T), BF16),
        V((HW, T), BF16), V((T, HW), BF16), V((HW // HD, 1, T), F32), V((T, BQ), F32),
        V((R, D), F32), V((R, D), F32), V((R, D), F32), V((R, 1), F32), V((R, 1), F32), V((R, D), F32),
        V((mp_size, R, FU), BF16), V((mp_size, R, FU), F32), V((mp_size, R, FU), BF16),
        V((T, HW), BF16), V((HW, T), BF16), V((T, HW), F32), V((T, HW), F32), V((HW, T), F32), V((T, 3 * HW), BF16),
        V((2, 2, rc, D), F32), V((C, rc, D), F32),
        V((C, 2, rc, D), BF16), V((C, 2, rc, D), BF16), V((C, rc, D), BF16), V((C, rc, D), BF16),
        V((n_bits + 1, 8, 128), F32), V((n_bits, 8, 128), F32), V((TILE, D), F32), dma,
        dma((4, C, 3)), dma((4, C, 3)), dma((4, C, 3)), dma((4, C, 3)), dma((n_bits,)), dma((n_bits,)),
    ]
    out_shape = [
        jax.ShapeDtypeStruct((R, D), BF16),
        jax.ShapeDtypeStruct((R, D), F32),
        jax.ShapeDtypeStruct((16, D), F32),
        jax.ShapeDtypeStruct((D, 3 * HW), F32),
        jax.ShapeDtypeStruct((HW, D), F32),
        jax.ShapeDtypeStruct((D, FU), F32),
        jax.ShapeDtypeStruct((FU, D), F32),
    ]
    return pl.pallas_call(
        functools.partial(block_kernel, sizes),
        out_shape=out_shape,
        in_specs=[vmem] * 6 + [anywhere] * 4,
        out_specs=[vmem] * 3 + [anywhere] * 4,
        scratch_shapes=scratch,
        compiler_params=pltpu.CompilerParams(
            collective_id=0, has_side_effects=True, vmem_limit_bytes=60 << 20
        ),
        name="block",
    )(
        x, teacher, segments.reshape(1, T), segments.reshape(T, 1),
        valid.reshape(R, 1), vectors, wqkv, wout, wup, wdown,
    )


def adam_update(gradient, stored, decay_factor, token_total):
    weight = stored[0]
    mean_grad = gradient / token_total
    moment_one = beta_one * stored[1] + (1.0 - beta_one) * mean_grad
    moment_two = beta_two * stored[2] + (1.0 - beta_two) * mean_grad * mean_grad
    update = (
        moment_one / correction_one / (jnp.sqrt(moment_two / correction_two) + adam_eps)
        + decay_factor * weight
    )
    weight = weight - learn_rate * update
    return (jnp.stack([weight, moment_one, moment_two]), weight.astype(jnp.bfloat16))


def shards(
    inputs,
    teacher,
    segments,
    valid_mask,
    qkv_copy,
    out_copy,
    up_copy,
    down_copy,
    vector_copy,
    qkv_state,
    out_state,
    up_state,
    down_state,
    vector_state,
):
    sizes = (lax.axis_size("dp"), lax.axis_size("mp"))
    token_total = inputs.shape[0] * sizes[0] * sizes[1]
    width = inputs.shape[1]
    head_width = qkv_copy.shape[2]
    block_out, input_grad, vector_local, qkv_local, out_local, up_local, down_local = block_call(
        sizes,
        inputs,
        teacher,
        segments,
        valid_mask.astype(F32),
        vector_copy.astype(F32),
        qkv_copy.reshape(width, 3 * head_width),
        out_copy,
        up_copy,
        down_copy,
    )
    qkv_local = qkv_local.reshape(width, 3, head_width)
    vector_grad = lax.psum(vector_local[: vector_copy.shape[0]], ("dp", "mp"))
    qkv_grad, out_grad, up_grad, down_grad = (
        lax.psum_scatter(qkv_local, "dp", scatter_dimension=0, tiled=True),
        lax.psum_scatter(out_local, "dp", scatter_dimension=1, tiled=True),
        lax.psum_scatter(up_local, "dp", scatter_dimension=0, tiled=True),
        lax.psum_scatter(down_local, "dp", scatter_dimension=1, tiled=True),
    )
    qkv_new, qkv_low = adam_update(qkv_grad, qkv_state, decay_rate, token_total)
    out_new, out_low = adam_update(out_grad, out_state, decay_rate, token_total)
    up_new, up_low = adam_update(up_grad, up_state, decay_rate, token_total)
    down_new, down_low = adam_update(down_grad, down_state, decay_rate, token_total)
    vector_new, vector_low = adam_update(vector_grad, vector_state, 0.0, token_total)
    qkv_full, out_full, up_full, down_full = (
        lax.all_gather(qkv_low, "dp", axis=0, tiled=True),
        lax.all_gather(out_low, "dp", axis=1, tiled=True),
        lax.all_gather(up_low, "dp", axis=0, tiled=True),
        lax.all_gather(down_low, "dp", axis=1, tiled=True),
    )
    return (
        block_out,
        input_grad,
        qkv_grad,
        out_grad,
        up_grad,
        down_grad,
        vector_grad,
        qkv_new,
        out_new,
        up_new,
        down_new,
        vector_new,
        qkv_full,
        out_full,
        up_full,
        down_full,
        vector_low,
    )


def solution(mesh):
    in_specs = (
        P(("dp", "mp"), None),
        P(("dp", "mp"), None),
        P("dp", None),
        P(("dp", "mp")),
        P(None, None, "mp"),
        P("mp", None),
        P(None, "mp"),
        P("mp", None),
        P(),
        P(None, "dp", None, "mp"),
        P(None, "mp", "dp"),
        P(None, "dp", "mp"),
        P(None, "mp", "dp"),
        P(),
    )
    out_specs = (
        P(("dp", "mp"), None),
        P(("dp", "mp"), None),
        P("dp", None, "mp"),
        P("mp", "dp"),
        P("dp", "mp"),
        P("mp", "dp"),
        P(),
        P(None, "dp", None, "mp"),
        P(None, "mp", "dp"),
        P(None, "dp", "mp"),
        P(None, "mp", "dp"),
        P(),
        P(None, None, "mp"),
        P("mp", None),
        P(None, "mp"),
        P("mp", None),
        P(),
    )
    return jax.shard_map(shards, mesh=mesh, in_specs=in_specs, out_specs=out_specs, check_vma=False)
```

```python
import functools
import math
import types

import jax
import jax.numpy as jnp
from jax import lax
from jax.experimental import pallas as pl
from jax.experimental.pallas import tpu as pltpu
from jax.sharding import PartitionSpec as P

HEADS = 16
HD = 64

norm_eps = 1e-05
beta_one = 0.9
beta_two = 0.95
adam_eps = 1e-08
learn_rate = 0.001
decay_rate = 0.1
correction_one = 1.0 - (0.9**10) ** 10
correction_two = 1.0 - (0.95**10) ** 10
log2_e = 1.4426950408889634

CHUNKS = 2
BQ = 256
TILE = 256
MESH = pl.DeviceIdType.MESH
F32 = jnp.float32
BF16 = jnp.bfloat16
NN = ((1,), (0,))
NT = ((1,), (1,))
TN = ((0,), (0,))


def mm(a, b, dims):
    return lax.dot_general(a, b, (dims, ((), ())), preferred_element_type=F32)


def gelu_both(v):
    c = 0.7978845608
    v2 = v * v
    th = jnp.tanh(c * (v + 0.044715 * v2 * v))
    half = 0.5 * (1.0 + th)
    back = half + 0.5 * v * (1.0 - th * th) * (c * (1.0 + 3.0 * 0.044715 * v2))
    return v * half, back


def norm_rows(v):
    centred = v - jnp.mean(v, -1, keepdims=True)
    inverse = lax.rsqrt(jnp.mean(centred * centred, -1, keepdims=True) + norm_eps)
    return centred * inverse, inverse


def norm_backward(grad_out, normed, inverse, gain_row):
    scaled = grad_out * gain_row
    return inverse * (
        scaled
        - jnp.mean(scaled, -1, keepdims=True)
        - normed * jnp.mean(scaled * normed, -1, keepdims=True)
    )


def adam_step(gradient, weight, first, second, decay_factor, token_total):
    mean_grad = gradient / token_total
    moment_one = beta_one * first + (1.0 - beta_one) * mean_grad
    moment_two = beta_two * second + (1.0 - beta_two) * mean_grad * mean_grad
    update = (
        moment_one / correction_one / (jnp.sqrt(moment_two / correction_two) + adam_eps)
        + decay_factor * weight
    )
    return weight - learn_rate * update, moment_one, moment_two


def block_kernel(sizes, fast, names, *refs):
    r = types.SimpleNamespace(**dict(zip(names, refs)))
    dp_size, mp_size = sizes
    dp = lax.axis_index("dp")
    m = lax.axis_index("mp")
    core = lax.rem(m, 2)
    chip = m // 2
    mc = m + 1 - 2 * core
    mx = lax.rem(m + 2, 4)
    md = mc + mx - m
    C = CHUNKS
    R, D = r.x.shape
    rc = R // C
    T = mp_size * R
    HW = r.wout.shape[0]
    FU = r.wup.shape[1]
    LOCAL_HEADS = HW // HD
    token_total = float(dp_size * T)

    bits = [("mp", b) for b in range(mp_size.bit_length() - 1)]
    bits += [("dp", b) for b in range(dp_size.bit_length() - 1)]

    def flip(v, b):
        w = 1 << b
        return v + w - 2 * w * lax.rem(v // w, 2)

    def bit_partner(item):
        axis, b = item
        if axis == "mp":
            return (dp, flip(m, b))
        return (flip(dp, b), m)

    to_core = (dp, mc)
    to_x = (dp, mx)

    NZ = dp_size // 2
    z = dp // 2
    y = lax.rem(dp, 2)
    to_y = (dp + 1 - 2 * y, m)

    def line(direction):
        place = z + direction * (NZ - 1 - 2 * z)
        return place, (dp + 2 - 4 * direction, m)

    def local_copy(src, dst, sem):
        cp = pltpu.make_async_copy(src, dst, sem)
        cp.start()
        return cp

    weights = [
        local_copy(src, dst, r.w_sem.at[i])
        for i, (src, dst) in enumerate(
            [(r.wqkv_hbm, r.wqkv), (r.wout_hbm, r.wout), (r.wup_hbm, r.wup), (r.wdown_hbm, r.wdown)]
        )
    ]
    if fast:
        parts = {
            "d": (0, r.g3, r.act, FU, True),
            "u": (1, r.g2, r.gup, FU, False),
            "o": (2, r.g4, r.mix, HW, True),
            "q": (3, r.g1, r.st, 3 * HW, False),
        }
        states = {
            "d": r.sd,
            "u": r.big.at[0:3, 0:SHARE, :],
            "o": r.so,
            "q": r.big.at[0:3, SHARE : 2 * SHARE, 0 : 3 * HW],
        }
        state_in = {}

        def fetch_state(name):
            state_in[name] = local_copy(
                getattr(r, "s%s_hbm" % name), states[name], r.s_sem.at[parts[name][0]]
            )

        fetch_state("d")
        fetch_state("o")

    barrier = pltpu.get_barrier_semaphore()
    for item in bits:
        pl.semaphore_signal(barrier, inc=1, device_id=bit_partner(item), device_id_type=MESH)
    greetings = len(bits)
    if fast:
        for direction in range(2):
            place, following = line(direction)

            @pl.when(place < NZ - 1)
            def _():
                pl.semaphore_signal(barrier, inc=1, device_id=following, device_id_type=MESH)

        greetings = greetings + (z > 0).astype(jnp.int32) + (z < NZ - 1).astype(jnp.int32)
    pl.semaphore_wait(barrier, greetings)

    def doubling(values, received, send_sems, recv_sems):
        copies = []

        def send(step):
            cp = pltpu.make_async_remote_copy(
                src_ref=values.at[step], dst_ref=received.at[step],
                send_sem=send_sems.at[step], recv_sem=recv_sems.at[step],
                device_id=bit_partner(bits[step]), device_id_type=MESH,
            )
            cp.start()
            copies.append(cp)

        def following():
            step = len(copies) - 1
            copies[step].wait()
            values[step + 1] = values[step] + received[step]
            if step + 1 < len(bits):
                send(step + 1)

        return send, following

    count_send, count_next = doubling(r.cnt, r.cnt_r, r.cnt_ss, r.cnt_rs)
    r.cnt[0] = jnp.zeros((8, 128), F32) + jnp.sum(r.valid[...])
    count_send(0)

    def ag_copy(site, j, kind, ref, block, device):
        part = ref.at[block, pl.ds(j * rc, rc)]
        return pltpu.make_async_remote_copy(
            src_ref=part, dst_ref=part, send_sem=r.ag_ss.at[site, j, kind],
            recv_sem=r.ag_rs.at[site, j, kind], device_id=device, device_id_type=MESH,
        )

    def ag_start(site, j, ref, value):
        ref[m, pl.ds(j * rc, rc), :] = value
        cx = ag_copy(site, j, 0, ref, m, to_x)
        cx.start()
        cc = ag_copy(site, j, 1, ref, m, to_core)
        cc.start()
        return cx, cc

    def ag_forward(site, j, ref):
        cf = ag_copy(site, j, 2, ref, mx, to_core)
        cf.start()
        return cf

    def rs_copy(site, j, kind, src, dst, device):
        return pltpu.make_async_remote_copy(
            src_ref=src, dst_ref=dst, send_sem=r.rs_ss.at[site, j, kind],
            recv_sem=r.rs_rs.at[site, j, kind], device_id=device, device_id_type=MESH,
        )

    def rs_start(site, j, lhs_of, rhs_of):
        def product(first, slot, kept_ref):
            lhs = lhs_of(first)

            def tile_body(n, carry):
                lanes = pl.ds(pl.multiple_of(n * TILE, TILE), TILE)
                rhs, dims = rhs_of(lanes)
                both = mm(lhs, rhs, dims)
                low, high = both[:rc], both[rc:]
                r.rs_cs[j, slot, :, lanes] = jnp.where(core == 0, high, low).astype(BF16)
                kept_ref[j, :, lanes] = jnp.where(core == 0, low, high)
                return carry

            lax.fori_loop(0, D // TILE, tile_body, 0)

        product(2 * (1 - chip), 0, r.pass_on)
        c0 = rs_copy(site, j, 0, r.rs_cs.at[j, 0], r.rs_cr.at[j, 0], to_core)
        c0.start()
        product(2 * chip, 1, r.keep)
        c1 = rs_copy(site, j, 1, r.rs_cs.at[j, 1], r.rs_cr.at[j, 1], to_core)
        c1.start()
        c0.wait()
        r.rs_xs[j] = (r.pass_on[j] + r.rs_cr[j, 0].astype(F32)).astype(BF16)
        cx = rs_copy(site, j, 2, r.rs_xs.at[j], r.rs_xr.at[j], to_x)
        cx.start()
        return c1, cx

    def rs_finish(j, copies):
        for cp in copies:
            cp.wait()
        return r.keep[j] + r.rs_cr[j, 1].astype(F32) + r.rs_xr[j].astype(F32)

    def share_rows(ref, share):
        lanes = pl.ds(pl.multiple_of(share * SHARE, SHARE), SHARE)
        return ref[:, :, lanes].reshape(T, SHARE).T

    def right_tile(ref, lanes):
        if len(ref.shape) == 3:
            return ref[:, :, lanes].reshape(T, TILE)
        return ref[:, lanes]

    def y_copy(name, i):
        p = parts[name][0]
        return pltpu.make_async_remote_copy(
            src_ref=getattr(r, "ys" + name).at[i], dst_ref=getattr(r, "yr" + name).at[i],
            send_sem=r.y_ss.at[p, i], recv_sem=r.y_rs.at[p, i], device_id=to_y, device_id_type=MESH,
        )

    def y_start(name):
        _, left, right, width, _ = parts[name]
        out = getattr(r, "ys" + name)

        def pair_body(i, carry):
            lhs = jnp.concatenate(
                [share_rows(left, 4 * i + 1 - y), share_rows(left, 4 * i + 3 - y)], 0
            )

            def tile_body(n, inner):
                lanes = pl.ds(pl.multiple_of(n * TILE, TILE), TILE)
                both = mm(lhs, right_tile(right, lanes), NN).astype(BF16)
                out[2 * i, :, lanes] = both[:SHARE]
                out[2 * i + 1, :, lanes] = both[SHARE:]
                return inner

            lax.fori_loop(0, width // TILE, tile_body, 0)
            y_copy(name, 2 * i).start()
            y_copy(name, 2 * i + 1).start()
            return carry

        lax.fori_loop(0, NZ // 2, pair_body, 0)

    def share_sum(name, target, put):
        _, left, right, width, _ = parts[name]
        got = getattr(r, "yr" + name)
        y_copy(name, target).wait_recv()
        lhs = share_rows(left, 2 * target + y)

        def tile_body(n, carry):
            lanes = pl.ds(pl.multiple_of(n * TILE, TILE), TILE)
            put(lanes, mm(lhs, right_tile(right, lanes), NN) + got[target, :, lanes].astype(F32))
            return carry

        lax.fori_loop(0, width // TILE, tile_body, 0)

    def z_copy(name, direction, step, device):
        p = parts[name][0]
        return pltpu.make_async_remote_copy(
            src_ref=getattr(r, "zs" + name).at[direction],
            dst_ref=getattr(r, "zr" + name).at[direction, step],
            send_sem=r.z_ss.at[p, direction, step], recv_sem=r.z_rs.at[p, direction, step],
            device_id=device, device_id_type=MESH,
        )

    def chain_step(name, step):
        out = getattr(r, "zs" + name)
        got = getattr(r, "zr" + name)

        def one(direction, carry):
            place, following = line(direction)

            @pl.when(place <= step)
            def _():
                mirrored = NZ - 1 - step + place
                target = mirrored + direction * (NZ - 1 - 2 * mirrored)

                def put(lanes, value):
                    r.acc[:, lanes] = value

                share_sum(name, target, put)
                if step > 0:

                    @pl.when(place < step)
                    def _():
                        z_copy(name, direction, step - 1, following).wait_send()

                    @pl.when(place > 0)
                    def _():
                        z_copy(name, direction, step - 1, following).wait_recv()
                        r.acc[:, 0 : out.shape[2]] += got[direction, step - 1].astype(F32)

                out[direction] = r.acc[:, 0 : out.shape[2]].astype(BF16)
                z_copy(name, direction, step, following).start()

            return carry

        lax.fori_loop(0, 2, one, 0)

    gathered = {}

    def a_src(name, share):
        ref = getattr(r, name + "_full")
        at = pl.ds(pl.multiple_of(share * SHARE, SHARE), SHARE)
        if parts[name][4]:
            return ref.at[:, at]
        return ref.at[at, :]

    def az_copy(name, direction, step, share, src, device):
        p = parts[name][0]
        return pltpu.make_async_remote_copy(
            src_ref=src, dst_ref=a_src(name, share), send_sem=r.az_ss.at[p, direction, step],
            recv_sem=r.az_rs.at[p, direction, step], device_id=device, device_id_type=MESH,
        )

    def ay_copy(name, place, src):
        p = parts[name][0]
        return pltpu.make_async_remote_copy(
            src_ref=src, dst_ref=a_src(name, 2 * place + y), send_sem=r.ay_ss.at[p, place],
            recv_sem=r.ay_rs.at[p, place], device_id=to_y, device_id_type=MESH,
        )

    local_out = []

    def finish_share(name):
        p, _, _, width, turned = parts[name]
        got = getattr(r, "zr" + name)
        state = states[name]
        grad_out = getattr(r, "gr" + name)
        fresh = getattr(r, "nc" + name)

        def put(lanes, value):
            r.acc[:, lanes] = value

        share_sum(name, z, put)

        def one(direction, carry):
            place, _ = line(direction)

            @pl.when(place > 0)
            def _():
                z_copy(name, direction, NZ - 2, (dp, m)).wait_recv()
                r.acc[:, 0:width] += got[direction, NZ - 2].astype(F32)

            return carry

        lax.fori_loop(0, 2, one, 0)
        state_in[name].wait()

        def adam_body(n, carry):
            cols = pl.ds(pl.multiple_of(n * SHARE, SHARE), SHARE)
            grad = r.acc[:, cols]
            if turned:
                grad = grad.T
                at = (cols, slice(None))
            else:
                at = (slice(None), cols)
            grad_out[at] = grad
            w, a, b = adam_step(
                grad, state[(0,) + at], state[(1,) + at], state[(2,) + at], decay_rate, token_total
            )
            state[(0,) + at] = w
            state[(1,) + at] = a
            state[(2,) + at] = b
            fresh[at] = w.astype(BF16)
            return carry

        lax.fori_loop(0, width // SHARE, adam_body, 0)
        for direction in range(2):
            place, following = line(direction)

            @pl.when(place < NZ - 1)
            def _():
                az_copy(name, direction, 0, 2 * z + y, fresh, following).start()

        ay_copy(name, z, fresh).start()
        local_out.append(local_copy(fresh, a_src(name, 2 * z + y), r.o_sem.at[p, 0]))
        local_out.append(local_copy(grad_out, getattr(r, name + "_grad"), r.o_sem.at[p, 1]))
        local_out.append(local_copy(state, getattr(r, name + "_new"), r.o_sem.at[p, 2]))

    def gather_step(name, step):
        for direction in range(2):
            place, following = line(direction)

            @pl.when(place >= step)
            def _():
                source = z - step + 2 * step * direction
                part = a_src(name, 2 * source + y)
                az_copy(name, direction, step - 1, 2 * source + y, part, following).wait_recv()
                if step < NZ - 1:

                    @pl.when(place < NZ - 1)
                    def _():
                        az_copy(name, direction, step, 2 * source + y, part, following).start()

                ay_copy(name, source, part).start()

    def gather_end(name):
        def one(direction, carry):
            place, following = line(direction)
            part = a_src(name, 2 * z + y)

            @pl.when(place <= NZ - 2)
            def _():
                z_copy(name, direction, NZ - 2, following).wait_send()

            for step in range(NZ - 1):

                @pl.when((place >= step) & (place < NZ - 1))
                def _():
                    az_copy(name, direction, step, 2 * z + y, part, following).wait_send()

            return carry

        lax.fori_loop(0, 2, one, 0)

        def y_body(i, carry):
            y_copy(name, i).wait_send()
            part = a_src(name, 2 * i + y)
            ay_copy(name, i, part).wait_send()
            ay_copy(name, i, part).wait_recv()
            return carry

        lax.fori_loop(0, NZ, y_body, 0)

    def put_out(src, dst):
        cp = pltpu.make_async_copy(src, dst, r.stage_sem)
        cp.start()
        cp.wait()

    r.vg[...] = jnp.zeros(r.vg.shape, F32)
    ag = {}
    for j in range(C):
        rows = slice(j * rc, (j + 1) * rc)
        normed, inverse = norm_rows(r.x[rows, :].astype(F32))
        ag[j] = ag_start(0, j, r.g1, (normed * r.vec[0:1, :] + r.vec[1:2, :]).astype(BF16))

    head_lanes = pl.ds(pl.multiple_of(m * HW, HW), HW)
    weights[0].wait()

    def project(o):
        p = mm(r.g1[o], r.wqkv[...], NN)
        at = pl.ds(pl.multiple_of(o * R, R), R)
        q = (p[:, :HW] + r.vec[6:7, head_lanes]).astype(BF16)
        k = p[:, HW : 2 * HW].astype(BF16)
        v = (p[:, 2 * HW :] + r.vec[7:8, head_lanes]).astype(BF16)
        r.qkv[at, 0:HW] = q
        r.qkv[at, HW : 2 * HW] = k
        r.qkv[at, 2 * HW :] = v
        r.qT[:, at] = q.T
        r.kT[:, at] = k.T
        r.vT[:, at] = v.T

    project(m)
    count_next()
    for j in range(C):
        ag[j][1].wait()
    project(mc)
    count_next()
    fw = {}
    for j in range(C):
        ag[j][0].wait()
        fw[j] = ag_forward(0, j, r.g1)
    project(mx)
    for j in range(C):
        fw[j].wait()
    project(md)

    pair_row = lax.broadcasted_iota(jnp.int32, (2 * HD, BQ), 0) // HD
    pair_lane = lax.broadcasted_iota(jnp.int32, (BQ, 2 * HD), 1) // HD
    scale2 = log2_e / math.sqrt(HD)
    K_AT, V_AT, Q_AT, DIST = 0, HW, 2 * HW, 3 * HW

    def make_dist(i):
        def one(b, carry):
            key = lax.broadcasted_iota(jnp.int32, (BQ, BQ), 0) + b * BQ
            query = lax.broadcasted_iota(jnp.int32, (BQ, BQ), 1) + i * BQ
            apart = query - key
            key_seg = r.segr[:, pl.ds(pl.multiple_of(b * BQ, BQ), BQ)]
            key_seg = jnp.broadcast_to(key_seg, (BQ, BQ)).T
            same = key_seg == r.segr[:, i * BQ : (i + 1) * BQ]
            r.big[b, :, DIST : DIST + BQ] = jnp.where((apart >= 0) & same, apart.astype(F32), jnp.inf)
            return carry

        lax.fori_loop(0, i + 1, one, 0)

    def head_slope(h):
        head = jnp.zeros((1, BQ), jnp.int32) + (m * LOCAL_HEADS + h + 1)
        return jnp.exp2(head.astype(F32) * (-8.0 / HEADS)) * log2_e

    def pair_lanes(h, start):
        return pl.ds(pl.multiple_of(start + (h // 2) * 2 * HD, 2 * HD), 2 * HD)

    def head_scores(i, ke, h):
        mask = (pair_row == lax.rem(h, 2)).astype(F32).astype(BF16)
        q_cols = r.qT[pair_lanes(h, 0), i * BQ : (i + 1) * BQ] * mask
        raw = mm(r.qkv[0:ke, pair_lanes(h, HW)], q_cols, NN)
        return raw * scale2 - head_slope(h) * r.big[0 : i + 1, :, DIST : DIST + BQ].reshape(ke, BQ)

    n_blocks = T // BQ
    for i in range(n_blocks):
        ke = (i + 1) * BQ
        block = slice(i * BQ, (i + 1) * BQ)
        make_dist(i)

        def head_body(h, carry):
            s = head_scores(i, ke, h)
            top = jnp.max(s, 0, keepdims=True)
            e = jnp.exp2(s - top)
            total = jnp.sum(e, 0, keepdims=True)
            p = (e * (1.0 / total)).astype(BF16)
            r.lse[h, :, block] = top + jnp.log2(total)
            at = pl.ds(pl.multiple_of(h * HD, HD), HD)
            r.mixT[at, :] = mm(r.vT[at, 0:ke], p, NN).astype(BF16)
            return carry

        lax.fori_loop(0, LOCAL_HEADS, head_body, 0)
        r.mix[block, :] = r.mixT[...].T
        if i < len(bits) - 2:
            count_next()
    for _ in range(2 + n_blocks, len(bits)):
        count_next()

    def rows4(ref, j):
        v = ref[:, pl.ds(j * rc, rc), :]
        return v.reshape(v.shape[0] * rc, v.shape[2])

    def pair_rows(ref, j):
        def of(first):
            v = ref[pl.ds(first, 2), pl.ds(j * rc, rc), :]
            return v.reshape(2 * rc, v.shape[2])

        return of

    def pair_flat(ref, j):
        def of(first):
            a = ref[pl.ds(pl.multiple_of(first * R + j * rc, rc), rc), :]
            b = ref[pl.ds(pl.multiple_of(first * R + R + j * rc, rc), rc), :]
            return jnp.concatenate([a, b], 0)

        return of

    def ag_finish(site, j, ref):
        ag[j][0].wait()
        cf = ag_forward(site, j, ref)
        ag[j][1].wait()
        cf.wait()

    weights[1].wait()
    rs = {}
    for j in range(C):
        rs[j] = rs_start(0, j, pair_flat(r.mix, j), lambda lanes: (r.wout[:, lanes], NN))
    for j in range(C):
        rows = slice(j * rc, (j + 1) * rc)
        hid = r.x[rows, :].astype(F32) + rs_finish(j, rs[j]) + r.vec[2:3, :]
        r.hidden[rows, :] = hid
        normed, inverse = norm_rows(hid)
        r.n2[rows, :] = normed
        r.inv2[rows, :] = inverse
        ag[j] = ag_start(1, j, r.g2, (normed * r.vec[3:4, :] + r.vec[4:5, :]).astype(BF16))

    weights[2].wait()
    weights[3].wait()
    for j in range(C):
        ag_finish(1, j, r.g2)
        rows = rows4(r.g2, j)

        def up_body(n, carry):
            lanes = pl.ds(pl.multiple_of(n * TILE, TILE), TILE)
            u = mm(rows, r.wup[:, lanes], NN) + r.vec[pl.ds(8 + m, 1), lanes]
            a, b = gelu_both(u)
            r.act[:, pl.ds(j * rc, rc), lanes] = a.astype(BF16).reshape(mp_size, rc, TILE)
            r.big[:, pl.ds(j * rc, rc), lanes] = b.reshape(mp_size, rc, TILE)
            return carry

        lax.fori_loop(0, FU // TILE, up_body, 0)
        rs[j] = rs_start(1, j, pair_rows(r.act, j), lambda lanes: (r.wdown[:, lanes], NN))

    loss_scale = token_total / r.cnt[len(bits), 0:1, 0:1]
    for j in range(C):
        rows = slice(j * rc, (j + 1) * rc)
        out = r.hidden[rows, :] + rs_finish(j, rs[j]) + r.vec[5:6, :]
        r.bo[rows, :] = out.astype(BF16)
        grad = r.valid[rows, :] * (out - r.t[rows, :].astype(F32)) * loss_scale
        r.ig[rows, :] = grad
        ag[j] = ag_start(2, j, r.g3, grad.astype(BF16))
        r.vg[5:6, :] += jnp.sum(grad, 0, keepdims=True)

    for j in range(C):
        ag_finish(2, j, r.g3)
        if fast and j == C - 1:
            y_start("d")
        rows = rows4(r.g3, j)

        def act_body(n, carry):
            lanes = pl.ds(pl.multiple_of(n * TILE, TILE), TILE)
            ga = mm(rows, r.wdown[lanes, :], NT)
            gu = ga * r.big[:, pl.ds(j * rc, rc), lanes].reshape(mp_size * rc, TILE)
            r.gup[:, pl.ds(j * rc, rc), lanes] = gu.astype(BF16).reshape(mp_size, rc, TILE)
            return carry

        lax.fori_loop(0, FU // TILE, act_body, 0)
        rs[j] = rs_start(2, j, pair_rows(r.gup, j), lambda lanes: (r.wup[lanes, :], NT))

    def whole_grad(left, right, width, dst):
        def body(n, carry):
            lanes = pl.ds(pl.multiple_of(n * TILE, TILE), TILE)
            r.stage[:, 0:width] = mm(right_tile(left, lanes), right[...].reshape(T, width), TN)
            put_out(r.stage.at[:, 0:width], dst.at[lanes, :])
            return carry

        lax.fori_loop(0, dst.shape[0] // TILE, body, 0)

    if not fast:
        whole_grad(r.act, r.g3, D, r.d_grad)

    for j in range(C):
        rows = slice(j * rc, (j + 1) * rc)
        gs = rs_finish(j, rs[j])
        gh = r.ig[rows, :] + norm_backward(gs, r.n2[rows, :], r.inv2[rows, :], r.vec[3:4, :])
        r.hidden[rows, :] = gh
        ag[j] = ag_start(3, j, r.g4, gh.astype(BF16))
        r.vg[2:3, :] += jnp.sum(gh, 0, keepdims=True)
        r.vg[3:4, :] += jnp.sum(gs * r.n2[rows, :], 0, keepdims=True)
        r.vg[4:5, :] += jnp.sum(gs, 0, keepdims=True)

    if fast:
        y_start("u")
    else:
        whole_grad(r.g2, r.gup, FU, r.u_grad)
    r.vg[pl.ds(8 + m, 1), :] = jnp.sum(r.gup[...].reshape(T, FU).astype(F32), 0, keepdims=True)

    for j in range(C):
        ag_finish(3, j, r.g4)

    def gm_body(o, carry):
        at = pl.ds(pl.multiple_of(o * R, R), R)
        gmx = mm(r.g4[o], r.wout[...], NT).astype(BF16)
        r.gm[at, :] = gmx
        r.vT[:, at] = gmx.T
        return carry

    lax.fori_loop(0, mp_size, gm_body, 0)
    if fast:
        y_start("o")

    r.big[:, :, K_AT : K_AT + HW] = jnp.zeros((mp_size, R, HW), F32)
    r.big[:, :, V_AT : V_AT + HW] = jnp.zeros((mp_size, R, HW), F32)
    for i in range(n_blocks):
        ke = (i + 1) * BQ
        block = slice(i * BQ, (i + 1) * BQ)
        make_dist(i)

        def back_body(h, carry):
            lanes = pair_lanes(h, 0)
            row_mask = (pair_row == lax.rem(h, 2)).astype(F32).astype(BF16)
            lane_mask = (pair_lane == lax.rem(h, 2)).astype(F32).astype(BF16)
            p = jnp.exp2(head_scores(i, ke, h) - r.lse[h, :, block])
            gp = mm(r.qkv[0:ke, pair_lanes(h, 2 * HW)], r.vT[lanes, block] * row_mask, NN)
            inner = jnp.sum(p * gp, 0, keepdims=True)
            raw = (p * (gp - inner)).astype(BF16)
            low = p.astype(BF16)
            r.big[0 : i + 1, :, pair_lanes(h, V_AT)] += mm(
                low, r.gm[block, lanes] * lane_mask, NN
            ).reshape(i + 1, BQ, 2 * HD)
            r.big[0 : i + 1, :, pair_lanes(h, K_AT)] += mm(
                raw, r.qkv[block, lanes] * lane_mask, NN
            ).reshape(i + 1, BQ, 2 * HD)
            at = pl.ds(pl.multiple_of(h * HD, HD), HD)
            r.big[i, at, Q_AT : Q_AT + BQ] = mm(r.kT[at, 0:ke], raw, NN) * (1.0 / math.sqrt(HD))
            return carry

        lax.fori_loop(0, LOCAL_HEADS, back_body, 0)
        r.st[block, 0:HW] = r.big[i, 0:HW, Q_AT : Q_AT + BQ].T.astype(BF16)
        if fast and i >= 1:
            chain_step("d", i - 1)
    r.st[:, HW : 2 * HW] = (
        r.big[:, :, K_AT : K_AT + HW].reshape(T, HW) * (1.0 / math.sqrt(HD))
    ).astype(BF16)
    r.st[:, 2 * HW :] = r.big[:, :, V_AT : V_AT + HW].reshape(T, HW).astype(BF16)
    r.vg[6:7, head_lanes] = jnp.sum(r.st[:, 0:HW].astype(F32), 0, keepdims=True)
    r.vg[7:8, head_lanes] = jnp.sum(r.st[:, 2 * HW :].astype(F32), 0, keepdims=True)

    if fast:
        fetch_state("u")
        fetch_state("q")

    for j in range(C):
        rs[j] = rs_start(3, j, pair_flat(r.st, j), lambda lanes: (r.wqkv[lanes, :], NT))

    if fast:
        y_start("q")
        chain_step("u", 0)
        finish_share("d")
    else:
        whole_grad(r.mix, r.g4, D, r.o_grad)
        whole_grad(r.g1, r.st, 3 * HW, r.q_grad)

    for j in range(C):
        rows = slice(j * rc, (j + 1) * rc)
        gf = rs_finish(j, rs[j])
        normed, inverse = norm_rows(r.x[rows, :].astype(F32))
        r.ig[rows, :] = r.hidden[rows, :] + norm_backward(gf, normed, inverse, r.vec[0:1, :])
        r.vg[0:1, :] += jnp.sum(gf * normed, 0, keepdims=True)
        r.vg[1:2, :] += jnp.sum(gf, 0, keepdims=True)

    vector_send, vector_next = doubling(r.vs, r.vs_r, r.vs_ss, r.vs_rs)
    r.vs[0] = r.vg[...]
    vector_send(0)
    if fast:
        chain_step("u", 1)
        chain_step("o", 0)
        vector_next()
        gather_step("d", 1)
        chain_step("u", 2)
        chain_step("o", 1)
        chain_step("q", 0)
        vector_next()
        finish_share("u")
        gather_step("d", 2)
        chain_step("o", 2)
        chain_step("q", 1)
        vector_next()
        finish_share("o")
        gather_step("d", 3)
        gather_step("u", 1)
        chain_step("q", 2)
        gather_step("o", 1)
        vector_next()
        finish_share("q")
        gather_step("u", 2)
        gather_step("o", 2)
        gather_step("q", 1)
        gather_step("u", 3)
        gather_step("o", 3)
        gather_step("q", 2)
        vector_next()
        gather_step("q", 3)
        for name in ("d", "u", "o", "q"):
            gather_end(name)
        for cp in local_out:
            cp.wait()
    else:
        for _ in bits:
            vector_next()
    r.vsum[...] = r.vs[len(bits)]


SHARE = 128


def block_call(sizes, x, teacher, segments, valid, vectors, copies, states):
    dp_size, mp_size = sizes
    R, D = x.shape
    T = mp_size * R
    wqkv, wout, wup, wdown = copies
    HW = wout.shape[0]
    FU = wup.shape[1]
    C = CHUNKS
    rc = R // C
    n_bits = (dp_size * mp_size).bit_length() - 1
    NZ = dp_size // 2
    fast = D == dp_size * SHARE
    dma = pltpu.SemaphoreType.DMA
    V = pltpu.VMEM
    S = jax.ShapeDtypeStruct
    vmem = pl.BlockSpec(memory_space=pltpu.VMEM)
    anywhere = pl.BlockSpec(memory_space=pl.ANY)

    ins = {
        "x": (x, vmem),
        "t": (teacher, vmem),
        "segr": (segments.reshape(1, T), vmem),
        "valid": (valid.reshape(R, 1), vmem),
        "vec": (vectors, vmem),
        "wqkv_hbm": (wqkv, anywhere),
        "wout_hbm": (wout, anywhere),
        "wup_hbm": (wup, anywhere),
        "wdown_hbm": (wdown, anywhere),
    }
    outs = {
        "bo": (S((R, D), BF16), vmem),
        "ig": (S((R, D), F32), vmem),
        "vsum": (S((16, D), F32), vmem),
    }
    if fast:
        shard = {"q": (SHARE, 3 * HW), "o": (HW, SHARE), "u": (SHARE, FU), "d": (FU, SHARE)}
        whole = {"q": (D, 3 * HW), "o": (HW, D), "u": (D, FU), "d": (FU, D)}
        for name, state in zip("qoud", states):
            ins["s%s_hbm" % name] = (state, anywhere)
        for name in "qoud":
            outs[name + "_grad"] = (S(shard[name], F32), anywhere)
        for name in "qoud":
            outs[name + "_new"] = (S((3,) + shard[name], F32), anywhere)
        for name in "qoud":
            outs[name + "_full"] = (S(whole[name], BF16), anywhere)
    else:
        outs["q_grad"] = (S((D, 3 * HW), F32), anywhere)
        outs["o_grad"] = (S((HW, D), F32), anywhere)
        outs["u_grad"] = (S((D, FU), F32), anywhere)
        outs["d_grad"] = (S((FU, D), F32), anywhere)
    scratch = {
        "wqkv": V((D, 3 * HW), BF16),
        "wout": V((HW, D), BF16),
        "wup": V((D, FU), BF16),
        "wdown": V((FU, D), BF16),
        "w_sem": dma((4,)),
        "g1": V((mp_size, R, D), BF16),
        "g2": V((mp_size, R, D), BF16),
        "g3": V((mp_size, R, D), BF16),
        "g4": V((mp_size, R, D), BF16),
        "qkv": V((T, 3 * HW), BF16),
        "qT": V((HW, T), BF16),
        "kT": V((HW, T), BF16),
        "vT": V((HW, T), BF16),
        "mixT": V((HW, BQ), BF16),
        "mix": V((T, HW), BF16),
        "lse": V((HW // HD, 1, T), F32),
        "hidden": V((R, D), F32),
        "n2": V((R, D), F32),
        "inv2": V((R, 1), F32),
        "act": V((mp_size, R, FU), BF16),
        "big": V((mp_size, R, FU), F32),
        "gup": V((mp_size, R, FU), BF16),
        "gm": V((T, HW), BF16),
        "st": V((T, 3 * HW), BF16),
        "pass_on": V((C, rc, D), F32),
        "keep": V((C, rc, D), F32),
        "rs_cs": V((C, 2, rc, D), BF16),
        "rs_cr": V((C, 2, rc, D), BF16),
        "rs_xs": V((C, rc, D), BF16),
        "rs_xr": V((C, rc, D), BF16),
        "cnt": V((n_bits + 1, 8, 128), F32),
        "cnt_r": V((n_bits, 8, 128), F32),
        "vg": V((16, D), F32),
        "vs": V((n_bits + 1, 16, D), F32),
        "vs_r": V((n_bits, 16, D), F32),
        "ag_ss": dma((4, C, 3)),
        "ag_rs": dma((4, C, 3)),
        "rs_ss": dma((4, C, 3)),
        "rs_rs": dma((4, C, 3)),
        "cnt_ss": dma((n_bits,)),
        "cnt_rs": dma((n_bits,)),
        "vs_ss": dma((n_bits,)),
        "vs_rs": dma((n_bits,)),
    }
    if fast:
        wide = {"q": 3 * HW, "o": HW, "u": FU, "d": FU}
        for name in "qoud":
            w = wide[name]
            scratch["ys" + name] = V((NZ, SHARE, w), BF16)
            scratch["yr" + name] = V((NZ, SHARE, w), BF16)
            scratch["zs" + name] = V((2, SHARE, w), BF16)
            scratch["zr" + name] = V((2, NZ - 1, SHARE, w), BF16)
            if name in "od":
                scratch["s" + name] = V((3,) + shard[name], F32)
            scratch["gr" + name] = V(shard[name], F32)
            scratch["nc" + name] = V(shard[name], BF16)
        scratch["acc"] = V((SHARE, FU), F32)
        scratch["s_sem"] = dma((4,))
        scratch["o_sem"] = dma((4, 3))
        scratch["y_ss"] = dma((4, NZ))
        scratch["y_rs"] = dma((4, NZ))
        scratch["z_ss"] = dma((4, 2, NZ - 1))
        scratch["z_rs"] = dma((4, 2, NZ - 1))
        scratch["az_ss"] = dma((4, 2, NZ - 1))
        scratch["az_rs"] = dma((4, 2, NZ - 1))
        scratch["ay_ss"] = dma((4, NZ))
        scratch["ay_rs"] = dma((4, NZ))
    else:
        scratch["stage"] = V((TILE, D), F32)
        scratch["stage_sem"] = dma
    names = list(ins) + list(outs) + list(scratch)
    results = pl.pallas_call(
        functools.partial(block_kernel, sizes, fast, names),
        out_shape=[v[0] for v in outs.values()],
        in_specs=[v[1] for v in ins.values()],
        out_specs=[v[1] for v in outs.values()],
        scratch_shapes=list(scratch.values()),
        compiler_params=pltpu.CompilerParams(
            collective_id=0, has_side_effects=True, vmem_limit_bytes=62 << 20
        ),
        name="block",
    )(*[v[0] for v in ins.values()])
    return dict(zip(outs, results)), fast


def adam_update(gradient, stored, decay_factor, token_total):
    new = adam_step(gradient, stored[0], stored[1], stored[2], decay_factor, token_total)
    return (jnp.stack(new), new[0].astype(jnp.bfloat16))


def shards(
    inputs,
    teacher,
    segments,
    valid_mask,
    qkv_copy,
    out_copy,
    up_copy,
    down_copy,
    vector_copy,
    qkv_state,
    out_state,
    up_state,
    down_state,
    vector_state,
):
    sizes = (lax.axis_size("dp"), lax.axis_size("mp"))
    token_total = inputs.shape[0] * sizes[0] * sizes[1]
    width = inputs.shape[1]
    head_width = qkv_copy.shape[2]
    outs, fast = block_call(
        sizes,
        inputs,
        teacher,
        segments,
        valid_mask.astype(F32),
        vector_copy.astype(F32),
        (qkv_copy.reshape(width, 3 * head_width), out_copy, up_copy, down_copy),
        (
            qkv_state.reshape(qkv_state.shape[:2] + (3 * head_width,)),
            out_state,
            up_state,
            down_state,
        ),
    )
    vector_grad = outs["vsum"][: vector_copy.shape[0]]
    vector_new, vector_low = adam_update(vector_grad, vector_state, 0.0, token_total)
    if fast:
        qkv_grad = outs["q_grad"].reshape(qkv_state.shape[1:])
        out_grad, up_grad, down_grad = (outs[n + "_grad"] for n in "oud")
        qkv_new = outs["q_new"].reshape(qkv_state.shape)
        out_new, up_new, down_new = (outs[n + "_new"] for n in "oud")
        qkv_full = outs["q_full"].reshape(qkv_copy.shape)
        out_full, up_full, down_full = (outs[n + "_full"] for n in "oud")
    else:
        qkv_local = outs["q_grad"].reshape(width, 3, head_width)
        qkv_grad, out_grad, up_grad, down_grad = (
            lax.psum_scatter(qkv_local, "dp", scatter_dimension=0, tiled=True),
            lax.psum_scatter(outs["o_grad"], "dp", scatter_dimension=1, tiled=True),
            lax.psum_scatter(outs["u_grad"], "dp", scatter_dimension=0, tiled=True),
            lax.psum_scatter(outs["d_grad"], "dp", scatter_dimension=1, tiled=True),
        )
        qkv_new, qkv_low = adam_update(qkv_grad, qkv_state, decay_rate, token_total)
        out_new, out_low = adam_update(out_grad, out_state, decay_rate, token_total)
        up_new, up_low = adam_update(up_grad, up_state, decay_rate, token_total)
        down_new, down_low = adam_update(down_grad, down_state, decay_rate, token_total)
        qkv_full, out_full, up_full, down_full = (
            lax.all_gather(qkv_low, "dp", axis=0, tiled=True),
            lax.all_gather(out_low, "dp", axis=1, tiled=True),
            lax.all_gather(up_low, "dp", axis=0, tiled=True),
            lax.all_gather(down_low, "dp", axis=1, tiled=True),
        )
    return (
        outs["bo"],
        outs["ig"],
        qkv_grad,
        out_grad,
        up_grad,
        down_grad,
        vector_grad,
        qkv_new,
        out_new,
        up_new,
        down_new,
        vector_new,
        qkv_full,
        out_full,
        up_full,
        down_full,
        vector_low,
    )


def solution(mesh):
    in_specs = (
        P(("dp", "mp"), None),
        P(("dp", "mp"), None),
        P("dp", None),
        P(("dp", "mp")),
        P(None, None, "mp"),
        P("mp", None),
        P(None, "mp"),
        P("mp", None),
        P(),
        P(None, "dp", None, "mp"),
        P(None, "mp", "dp"),
        P(None, "dp", "mp"),
        P(None, "mp", "dp"),
        P(),
    )
    out_specs = (
        P(("dp", "mp"), None),
        P(("dp", "mp"), None),
        P("dp", None, "mp"),
        P("mp", "dp"),
        P("dp", "mp"),
        P("mp", "dp"),
        P(),
        P(None, "dp", None, "mp"),
        P(None, "mp", "dp"),
        P(None, "dp", "mp"),
        P(None, "mp", "dp"),
        P(),
        P(None, None, "mp"),
        P("mp", None),
        P(None, "mp"),
        P("mp", None),
        P(),
    )
    return jax.shard_map(shards, mesh=mesh, in_specs=in_specs, out_specs=out_specs, check_vma=False)
```

```python
import functools
import math
import types

import jax
import jax.numpy as jnp
from jax import lax
from jax.experimental import pallas as pl
from jax.experimental.pallas import tpu as pltpu
from jax.sharding import PartitionSpec as P

HEADS = 16
HD = 64

norm_eps = 1e-05
beta_one = 0.9
beta_two = 0.95
adam_eps = 1e-08
learn_rate = 0.001
decay_rate = 0.1
correction_one = 1.0 - (0.9**10) ** 10
correction_two = 1.0 - (0.95**10) ** 10
log2_e = 1.4426950408889634

CHUNKS = 2
BQ = 256
TILE = 256
MESH = pl.DeviceIdType.MESH
F32 = jnp.float32
BF16 = jnp.bfloat16
NN = ((1,), (0,))
NT = ((1,), (1,))
TN = ((0,), (0,))


def mm(a, b, dims):
    return lax.dot_general(a, b, (dims, ((), ())), preferred_element_type=F32)


def gelu_both(v):
    c = 0.7978845608
    v2 = v * v
    th = jnp.tanh(c * (v + 0.044715 * v2 * v))
    half = 0.5 * (1.0 + th)
    back = half + 0.5 * v * (1.0 - th * th) * (c * (1.0 + 3.0 * 0.044715 * v2))
    return v * half, back


def norm_rows(v):
    centred = v - jnp.mean(v, -1, keepdims=True)
    inverse = lax.rsqrt(jnp.mean(centred * centred, -1, keepdims=True) + norm_eps)
    return centred * inverse, inverse


def norm_backward(grad_out, normed, inverse, gain_row):
    scaled = grad_out * gain_row
    return inverse * (
        scaled
        - jnp.mean(scaled, -1, keepdims=True)
        - normed * jnp.mean(scaled * normed, -1, keepdims=True)
    )


def adam_step(gradient, weight, first, second, decay_factor, token_total):
    mean_grad = gradient / token_total
    moment_one = beta_one * first + (1.0 - beta_one) * mean_grad
    moment_two = beta_two * second + (1.0 - beta_two) * mean_grad * mean_grad
    update = (
        moment_one / correction_one / (jnp.sqrt(moment_two / correction_two) + adam_eps)
        + decay_factor * weight
    )
    return weight - learn_rate * update, moment_one, moment_two


def block_kernel(sizes, fast, names, *refs):
    r = types.SimpleNamespace(**dict(zip(names, refs)))
    dp_size, mp_size = sizes
    dp = lax.axis_index("dp")
    m = lax.axis_index("mp")
    core = lax.rem(m, 2)
    chip = m // 2
    mc = m + 1 - 2 * core
    mx = lax.rem(m + 2, 4)
    md = mc + mx - m
    C = CHUNKS
    R, D = r.x.shape
    rc = R // C
    T = mp_size * R
    HW = r.wout.shape[0]
    FU = r.wup.shape[1]
    LOCAL_HEADS = HW // HD
    PAIR = 2 * HD
    PAIRS = HW // PAIR
    token_total = float(dp_size * T)

    dp_bits = [("dp", b) for b in range(dp_size.bit_length() - 1)]
    mp_bits = [("mp", b) for b in range(mp_size.bit_length() - 1)]
    bits = dp_bits + mp_bits

    def flip(v, b):
        w = 1 << b
        return v + w - 2 * w * lax.rem(v // w, 2)

    def bit_partner(item):
        axis, b = item
        if axis == "mp":
            return (dp, flip(m, b))
        return (flip(dp, b), m)

    to_core = (dp, mc)
    to_x = (dp, mx)

    NZ = dp_size // 2
    z = dp // 2
    y = lax.rem(dp, 2)
    to_y = (dp + 1 - 2 * y, m)

    def line(direction):
        place = z + direction * (NZ - 1 - 2 * z)
        return place, (dp + 2 - 4 * direction, m)

    def local_copy(src, dst, sem):
        cp = pltpu.make_async_copy(src, dst, sem)
        cp.start()
        return cp

    def qkv_lanes(pair, kind):
        return slice((3 * pair + kind) * PAIR, (3 * pair + kind + 1) * PAIR)

    qkv_weights = [
        local_copy(
            r.wqkv_hbm.at[kind, :, pair * PAIR : (pair + 1) * PAIR],
            r.wqkv.at[:, qkv_lanes(pair, kind)],
            r.wq_sem.at[pair, kind],
        )
        for pair in range(PAIRS)
        for kind in range(3)
    ]
    weights = [
        local_copy(src, dst, r.w_sem.at[i])
        for i, (src, dst) in enumerate(
            [(r.wout_hbm, r.wout), (r.wup_hbm, r.wup), (r.wdown_hbm, r.wdown)]
        )
    ]
    if fast:
        parts = {}
        for name, width in pieces(HW, FU):
            left, right = {
                "d": (r.g3, r.act),
                "u": (r.g2, r.gup),
                "o": (r.g4, r.mix),
                "q": (r.g1, r.st),
            }[name[0]]
            parts[name] = (len(parts), left, right, width)
        state_in = {}

        def span(name):
            width = PAIR if name[0] == "q" else parts[name][3]
            return slice(int(name[1]) * width, (int(name[1]) + 1) * width)

        def piece(ref, name):
            at = span(name)
            if name[0] == "q":
                return ref.at[:, :, at]
            return ref.at[:, at] if name[0] == "u" else ref.at[at, :]

        def state_copies(name, out):
            far = getattr(r, name[0] + "_new") if out else getattr(r, "s%s_hbm" % name[0])
            at = span(name)
            if name[0] == "q":
                return [
                    (
                        far.at[:, kind, :, at],
                        r.big.at[0:3, SHARE : 2 * SHARE, kind * HW + at.start : kind * HW + at.stop],
                    )
                    for kind in range(3)
                ]
            if name[0] == "u":
                return [(far.at[:, :, at], r.big.at[0:3, 0:SHARE, at])]
            return [(far.at[:, at, :], getattr(r, "s" + name[0]).at[:, at, :])]

        def fetch_state(matrix):
            for name in parts:
                if name[0] == matrix:
                    p = parts[name][0]
                    state_in[name] = [
                        local_copy(far, near, r.s_sem.at[p, k])
                        for k, (far, near) in enumerate(state_copies(name, False))
                    ]

        fetch_state("d")
        fetch_state("o")

    barrier = pltpu.get_barrier_semaphore()
    for item in bits:
        pl.semaphore_signal(barrier, inc=1, device_id=bit_partner(item), device_id_type=MESH)
    greetings = len(bits)
    if fast:
        for direction in range(2):
            place, following = line(direction)

            @pl.when(place < NZ - 1)
            def _():
                pl.semaphore_signal(barrier, inc=1, device_id=following, device_id_type=MESH)

        greetings = greetings + (z > 0).astype(jnp.int32) + (z < NZ - 1).astype(jnp.int32)
    pl.semaphore_wait(barrier, greetings)

    def doubling(order, values, received, send_sems, recv_sems):
        copies = []

        def send(step):
            cp = pltpu.make_async_remote_copy(
                src_ref=values.at[step], dst_ref=received.at[step],
                send_sem=send_sems.at[step], recv_sem=recv_sems.at[step],
                device_id=bit_partner(order[step]), device_id_type=MESH,
            )
            cp.start()
            copies.append(cp)

        def following():
            step = len(copies) - 1
            copies[step].wait()
            values[step + 1] = values[step] + received[step]
            if step + 1 < len(order):
                send(step + 1)

        return send, following

    count_send, count_next = doubling(bits, r.cnt, r.cnt_r, r.cnt_ss, r.cnt_rs)
    r.cnt[0] = jnp.zeros((8, 128), F32) + jnp.sum(r.valid[...].astype(F32))
    count_send(0)
    r.vec[...] = r.vec_low[...].astype(F32)

    def ag_copy(site, j, kind, ref, block, device):
        part = ref.at[block, pl.ds(j * rc, rc)]
        return pltpu.make_async_remote_copy(
            src_ref=part, dst_ref=part, send_sem=r.ag_ss.at[site, j, kind],
            recv_sem=r.ag_rs.at[site, j, kind], device_id=device, device_id_type=MESH,
        )

    def ag_start(site, j, ref, value):
        ref[m, pl.ds(j * rc, rc), :] = value
        cx = ag_copy(site, j, 0, ref, m, to_x)
        cx.start()
        cc = ag_copy(site, j, 1, ref, m, to_core)
        cc.start()
        return cx, cc

    def ag_forward(site, j, ref):
        cf = ag_copy(site, j, 2, ref, mx, to_core)
        cf.start()
        return cf

    def rs_copy(site, j, kind, src, dst, device):
        return pltpu.make_async_remote_copy(
            src_ref=src, dst_ref=dst, send_sem=r.rs_ss.at[site, j, kind],
            recv_sem=r.rs_rs.at[site, j, kind], device_id=device, device_id_type=MESH,
        )

    def rs_start(site, j, lhs_of, rhs_of):
        def product(first, slot, kept_ref):
            lhs = lhs_of(first)

            def tile_body(n, carry):
                lanes = pl.ds(pl.multiple_of(n * TILE, TILE), TILE)
                rhs, dims = rhs_of(lanes)
                both = mm(lhs, rhs, dims)
                low, high = both[:rc], both[rc:]
                r.rs_cs[j, slot, :, lanes] = jnp.where(core == 0, high, low).astype(BF16)
                kept_ref[j, :, lanes] = jnp.where(core == 0, low, high)
                return carry

            lax.fori_loop(0, D // TILE, tile_body, 0)

        product(2 * (1 - chip), 0, r.pass_on)
        c0 = rs_copy(site, j, 0, r.rs_cs.at[j, 0], r.rs_cr.at[j, 0], to_core)
        c0.start()
        product(2 * chip, 1, r.keep)
        c1 = rs_copy(site, j, 1, r.rs_cs.at[j, 1], r.rs_cr.at[j, 1], to_core)
        c1.start()
        c0.wait()
        r.rs_xs[j] = (r.pass_on[j] + r.rs_cr[j, 0].astype(F32)).astype(BF16)
        cx = rs_copy(site, j, 2, r.rs_xs.at[j], r.rs_xr.at[j], to_x)
        cx.start()
        return c1, cx

    def rs_finish(j, copies):
        for cp in copies:
            cp.wait()
        return r.keep[j] + r.rs_cr[j, 1].astype(F32) + r.rs_xr[j].astype(F32)

    def share_rows(ref, share):
        lanes = pl.ds(pl.multiple_of(share * SHARE, SHARE), SHARE)
        return ref[:, :, lanes].reshape(T, SHARE).T

    def right_tile(ref, lanes):
        if len(ref.shape) == 3:
            return ref[:, :, lanes].reshape(T, lanes.size)
        return ref[:, lanes]

    def tiles(width):
        return width if width < 2 * TILE else TILE

    def part_tile(name, n, step):
        _, _, right, width = parts[name]
        lanes = pl.ds(pl.multiple_of(n * step, 128), step)
        from_lanes = pl.ds(pl.multiple_of(int(name[1]) * width + n * step, 128), step)
        return lanes, right_tile(right, from_lanes)

    def part_product(name, lhs, put):
        width = parts[name][3]
        step = tiles(width)

        def tile_body(n, carry):
            lanes, rhs = part_tile(name, n, step)
            put(lanes, mm(lhs, rhs, NN))
            return carry

        lax.fori_loop(0, width // step, tile_body, 0)

    def y_copy(name, i):
        p = parts[name][0]
        return pltpu.make_async_remote_copy(
            src_ref=getattr(r, "ys" + name).at[i], dst_ref=getattr(r, "yr" + name).at[i],
            send_sem=r.y_ss.at[p, i], recv_sem=r.y_rs.at[p, i], device_id=to_y, device_id_type=MESH,
        )

    def y_start(name):
        left = parts[name][1]
        out = getattr(r, "ys" + name)

        def pair_body(i, carry):
            lhs = jnp.concatenate(
                [share_rows(left, 4 * i + 1 - y), share_rows(left, 4 * i + 3 - y)], 0
            )

            def put(lanes, both):
                out[2 * i, :, lanes] = both[:SHARE].astype(BF16)
                out[2 * i + 1, :, lanes] = both[SHARE:].astype(BF16)

            part_product(name, lhs, put)
            y_copy(name, 2 * i).start()
            y_copy(name, 2 * i + 1).start()
            return carry

        lax.fori_loop(0, NZ // 2, pair_body, 0)

    def share_sum(name, target):
        got = getattr(r, "yr" + name)
        y_copy(name, target).wait_recv()

        def put(lanes, value):
            r.acc[0:SHARE, lanes] = value + got[target, :, lanes].astype(F32)

        part_product(name, share_rows(parts[name][1], 2 * target + y), put)

    def both_shares(name, target):
        def put(lanes, value):
            r.wide[:, lanes] = value

        left = parts[name][1]
        lanes = pl.ds(pl.multiple_of(2 * target * SHARE, 2 * SHARE), 2 * SHARE)
        part_product(name, left[:, :, lanes].reshape(T, 2 * SHARE).T, put)

    def z_copy(name, direction, step, device):
        p = parts[name][0]
        return pltpu.make_async_remote_copy(
            src_ref=getattr(r, "zs" + name).at[direction],
            dst_ref=getattr(r, "zr" + name).at[direction, step],
            send_sem=r.z_ss.at[p, direction, step], recv_sem=r.z_rs.at[p, direction, step],
            device_id=device, device_id_type=MESH,
        )

    def chain_step(name, step):
        out = getattr(r, "zs" + name)
        got = getattr(r, "zr" + name)
        width = parts[name][3]
        total = (r.wide if name in Z_FIRST else r.acc).at[:, 0:width]

        def one(direction, carry):
            place, following = line(direction)

            @pl.when(place <= step)
            def _():
                mirrored = NZ - 1 - step + place
                target = mirrored + direction * (NZ - 1 - 2 * mirrored)
                (both_shares if name in Z_FIRST else share_sum)(name, target)
                if step > 0:

                    @pl.when(place < step)
                    def _():
                        z_copy(name, direction, step - 1, following).wait_send()

                    @pl.when(place > 0)
                    def _():
                        z_copy(name, direction, step - 1, following).wait_recv()
                        total[...] += got[direction, step - 1].astype(F32)

                out[direction] = total[...].astype(BF16)
                z_copy(name, direction, step, following).start()

            return carry

        lax.fori_loop(0, 2, one, 0)

    def chain_end(name):
        got = getattr(r, "zr" + name)
        width = parts[name][3]
        total = (r.wide if name in Z_FIRST else r.acc).at[:, 0:width]
        (both_shares if name in Z_FIRST else share_sum)(name, z)

        def one(direction, carry):
            place, _ = line(direction)

            @pl.when(place > 0)
            def _():
                z_copy(name, direction, NZ - 2, (dp, m)).wait_recv()
                total[...] += got[direction, NZ - 2].astype(F32)

            return carry

        lax.fori_loop(0, 2, one, 0)

    def y_exchange(name):
        chain_end(name)
        width = parts[name][3]
        theirs = pl.ds(pl.multiple_of((1 - y) * SHARE, SHARE), SHARE)
        getattr(r, "ys" + name)[0] = r.wide[theirs, 0:width].astype(BF16)
        y_copy(name, 0).start()

    def a_src(name, share):
        ref = getattr(r, name[0] + "_full")
        at = pl.ds(pl.multiple_of(share * SHARE, SHARE), SHARE)
        if name[0] == "q":
            return ref.at[:, at, span(name)]
        return ref.at[at, span(name)] if name[0] == "u" else ref.at[span(name), at]

    def az_copy(name, side, direction, step, share, src, device):
        p = parts[name][0]
        return pltpu.make_async_remote_copy(
            src_ref=src, dst_ref=a_src(name, share), send_sem=r.az_ss.at[p, side, direction, step],
            recv_sem=r.az_rs.at[p, side, direction, step], device_id=device, device_id_type=MESH,
        )

    def ay_copy(name, place, src):
        p = parts[name][0]
        return pltpu.make_async_remote_copy(
            src_ref=src, dst_ref=a_src(name, 2 * place + y), send_sem=r.ay_ss.at[p, place],
            recv_sem=r.ay_rs.at[p, place], device_id=to_y, device_id_type=MESH,
        )

    local_out = []

    def finish_share(name):
        p, _, _, width = parts[name]
        matrix = name[0]
        at0 = span(name)
        if name in Z_FIRST:
            y_copy(name, 0).wait_recv()
            ours = pl.ds(pl.multiple_of(y * SHARE, SHARE), SHARE)
            r.acc[:, 0:width] = r.wide[ours, 0:width] + getattr(r, "yr" + name)[0].astype(F32)
        else:
            chain_end(name)
        for cp in state_in[name]:
            cp.wait()
        grad_out = getattr(r, "gr" + matrix)
        fresh = getattr(r, "nc" + matrix)

        def adam_block(cols, at, state, state_at):
            grad = r.acc[:, cols]
            if matrix in "do":
                grad = grad.T
            grad_out[at] = grad
            w, a, b = adam_step(
                grad,
                state[(0,) + state_at],
                state[(1,) + state_at],
                state[(2,) + state_at],
                decay_rate,
                token_total,
            )
            state[(0,) + state_at] = w
            state[(1,) + state_at] = a
            state[(2,) + state_at] = b
            fresh[at] = w.astype(BF16)

        if matrix == "q":
            for kind in range(3):
                adam_block(
                    slice(kind * PAIR, (kind + 1) * PAIR),
                    (kind, slice(None), at0),
                    r.big,
                    (slice(SHARE, 2 * SHARE), slice(kind * HW + at0.start, kind * HW + at0.stop)),
                )
        else:

            def adam_body(n, carry):
                cols = pl.ds(pl.multiple_of(n * SHARE, SHARE), SHARE)
                there = pl.ds(pl.multiple_of(at0.start + n * SHARE, SHARE), SHARE)
                if matrix == "u":
                    adam_block(cols, (slice(None), there), r.big, (slice(0, SHARE), there))
                else:
                    at = (there, slice(None))
                    adam_block(cols, at, getattr(r, "s" + matrix), at)
                return carry

            lax.fori_loop(0, width // SHARE, adam_body, 0)
        fresh = piece(fresh, name)
        if name in Y_FIRST:
            ay_copy(name, z, fresh).start()
        for direction in range(2):
            place, following = line(direction)

            @pl.when(place < NZ - 1)
            def _():
                az_copy(name, 0, direction, 0, 2 * z + y, fresh, following).start()

        if name not in Y_FIRST:
            ay_copy(name, z, fresh).start()
        local_out.append(local_copy(fresh, a_src(name, 2 * z + y), r.o_sem.at[p, 0]))
        local_out.append(
            local_copy(piece(grad_out, name), piece(getattr(r, matrix + "_grad"), name), r.o_sem.at[p, 1])
        )
        for k, (far, near) in enumerate(state_copies(name, True)):
            local_out.append(local_copy(near, far, r.o_sem.at[p, 2 + k]))

    def neighbour_share(name):
        part = a_src(name, 2 * z + 1 - y)
        ay_copy(name, z, part).wait_recv()
        for direction in range(2):
            place, following = line(direction)

            @pl.when(place < NZ - 1)
            def _():
                az_copy(name, 1, direction, 0, 2 * z + 1 - y, part, following).start()

    def gather_step(name, step):
        for side in range(2 if name in Y_FIRST else 1):
            for direction in range(2):
                place, following = line(direction)

                @pl.when(place >= step)
                def _():
                    source = z - step + 2 * step * direction
                    share = 2 * source + (1 - y if side else y)
                    part = a_src(name, share)
                    az_copy(name, side, direction, step - 1, share, part, following).wait_recv()
                    if step < NZ - 1:

                        @pl.when(place < NZ - 1)
                        def _():
                            az_copy(name, side, direction, step, share, part, following).start()

                    if name not in Y_FIRST:
                        ay_copy(name, source, part).start()

    def gather_end(name):
        part = a_src(name, 2 * z + y)

        def one(direction, carry):
            place, following = line(direction)

            @pl.when(place <= NZ - 2)
            def _():
                z_copy(name, direction, NZ - 2, following).wait_send()

            for step in range(NZ - 1):

                @pl.when((place >= step) & (place < NZ - 1))
                def _():
                    for side in range(2 if name in Y_FIRST else 1):
                        az_copy(name, side, direction, step, 2 * z + y, part, following).wait_send()

            return carry

        lax.fori_loop(0, 2, one, 0)
        if name in Z_FIRST:
            y_copy(name, 0).wait_send()
        if name in Y_FIRST:
            ay_copy(name, z, part).wait_send()

        def y_body(i, carry):
            if name not in Z_FIRST:
                y_copy(name, i).wait_send()
            if name not in Y_FIRST:
                there = a_src(name, 2 * i + y)
                ay_copy(name, i, there).wait_send()
                ay_copy(name, i, there).wait_recv()
            return carry

        lax.fori_loop(0, NZ, y_body, 0)

    def put_out(src, dst):
        cp = pltpu.make_async_copy(src, dst, r.stage_sem)
        cp.start()
        cp.wait()

    late = {}

    def turn(point):
        if not fast:
            return
        for item in ORDER.get(point, "").split():
            kind, rest = item[0], item[1:]
            if kind == "v":
                late["vector_next"]()
            elif kind == "y":
                y_start(rest)
            elif kind == "f":
                finish_share(rest)
            elif kind == "e":
                y_exchange(rest)
            elif kind == "h":
                neighbour_share(rest)
            elif kind == "c":
                chain_step(rest[1:], int(rest[0]))
            elif kind == "g":
                gather_step(rest[1:], int(rest[0]))

    r.vg[...] = jnp.zeros(r.vg.shape, F32)
    ag = {}
    for j in range(C):
        rows = slice(j * rc, (j + 1) * rc)
        normed, inverse = norm_rows(r.x[rows, :].astype(F32))
        ag[j] = ag_start(0, j, r.g1, (normed * r.vec[0:1, :] + r.vec[1:2, :]).astype(BF16))

    head_lanes = pl.ds(pl.multiple_of(m * HW, HW), HW)
    for w in qkv_weights:
        w.wait()

    def project(o):
        p = mm(r.g1[o], r.wqkv[...], NN)
        at = pl.ds(pl.multiple_of(o * R, R), R)
        for pair in range(PAIRS):
            rows = slice(pair * PAIR, (pair + 1) * PAIR)
            lanes = pl.ds(pl.multiple_of(m * HW + pair * PAIR, PAIR), PAIR)
            q, k, v = (p[:, qkv_lanes(pair, kind)] for kind in range(3))
            q = (q + r.vec[6:7, lanes]).astype(BF16)
            k = k.astype(BF16)
            v = (v + r.vec[7:8, lanes]).astype(BF16)
            for kind, value in enumerate((q, k, v)):
                r.qkv[at, qkv_lanes(pair, kind)] = value
            r.qT[rows, at] = q.T
            r.kT[rows, at] = k.T
            r.vT[rows, at] = v.T

    project(m)
    count_next()
    for j in range(C):
        ag[j][1].wait()
    project(mc)
    for _ in range(1, dp_size.bit_length() - 1):
        count_next()
    fw = {}
    for j in range(C):
        ag[j][0].wait()
        fw[j] = ag_forward(0, j, r.g1)
    project(mx)
    for j in range(C):
        fw[j].wait()
    project(md)

    pair_row = lax.broadcasted_iota(jnp.int32, (2 * HD, BQ), 0) // HD
    pair_lane = lax.broadcasted_iota(jnp.int32, (BQ, 2 * HD), 1) // HD
    scale2 = log2_e / math.sqrt(HD)
    K_AT, V_AT, Q_AT, DIST = 0, HW, 2 * HW, 3 * HW

    def make_dist(i):
        def one(b, carry):
            key = lax.broadcasted_iota(jnp.int32, (BQ, BQ), 0) + b * BQ
            query = lax.broadcasted_iota(jnp.int32, (BQ, BQ), 1) + i * BQ
            apart = query - key
            key_seg = r.segr[:, pl.ds(pl.multiple_of(b * BQ, BQ), BQ)]
            key_seg = jnp.broadcast_to(key_seg, (BQ, BQ)).T
            same = key_seg == r.segr[:, i * BQ : (i + 1) * BQ]
            r.big[b, :, DIST : DIST + BQ] = jnp.where((apart >= 0) & same, apart.astype(F32), jnp.inf)
            return carry

        lax.fori_loop(0, i + 1, one, 0)

    def head_slope(h):
        head = jnp.zeros((1, BQ), jnp.int32) + (m * LOCAL_HEADS + h + 1)
        return jnp.exp2(head.astype(F32) * (-8.0 / HEADS)) * log2_e

    def pair_lanes(h, start):
        return pl.ds(pl.multiple_of(start + (h // 2) * PAIR, PAIR), PAIR)

    def kind_lanes(h, kind):
        return pl.ds(pl.multiple_of((h // 2) * 3 * PAIR + kind * PAIR, PAIR), PAIR)

    def head_scores(i, ke, h):
        mask = (pair_row == lax.rem(h, 2)).astype(F32).astype(BF16)
        q_cols = r.qT[pair_lanes(h, 0), i * BQ : (i + 1) * BQ] * mask
        raw = mm(r.qkv[0:ke, kind_lanes(h, 1)], q_cols, NN)
        return raw * scale2 - head_slope(h) * r.big[0 : i + 1, :, DIST : DIST + BQ].reshape(ke, BQ)

    n_blocks = T // BQ
    for i in range(n_blocks):
        ke = (i + 1) * BQ
        block = slice(i * BQ, (i + 1) * BQ)
        make_dist(i)

        def head_body(h, carry):
            s = head_scores(i, ke, h)
            top = jnp.max(s, 0, keepdims=True)
            e = jnp.exp2(s - top)
            total = jnp.sum(e, 0, keepdims=True)
            p = (e * (1.0 / total)).astype(BF16)
            r.lse[h, :, block] = top + jnp.log2(total)
            at = pl.ds(pl.multiple_of(h * HD, HD), HD)
            r.mixT[at, :] = mm(r.vT[at, 0:ke], p, NN).astype(BF16)
            return carry

        lax.fori_loop(0, LOCAL_HEADS, head_body, 0, unroll=True)
        r.mix[block, :] = r.mixT[...].T
        if i < mp_size.bit_length() - 1:
            count_next()

    def rows4(ref, j):
        v = ref[:, pl.ds(j * rc, rc), :]
        return v.reshape(v.shape[0] * rc, v.shape[2])

    def pair_rows(ref, j):
        def of(first):
            v = ref[pl.ds(first, 2), pl.ds(j * rc, rc), :]
            return v.reshape(2 * rc, v.shape[2])

        return of

    def pair_flat(ref, j):
        def of(first):
            a = ref[pl.ds(pl.multiple_of(first * R + j * rc, rc), rc), :]
            b = ref[pl.ds(pl.multiple_of(first * R + R + j * rc, rc), rc), :]
            return jnp.concatenate([a, b], 0)

        return of

    def ag_finish(site, j, ref):
        ag[j][0].wait()
        cf = ag_forward(site, j, ref)
        ag[j][1].wait()
        cf.wait()

    weights[0].wait()
    rs = {}
    for j in range(C):
        rs[j] = rs_start(0, j, pair_flat(r.mix, j), lambda lanes: (r.wout[:, lanes], NN))
    for j in range(C):
        rows = slice(j * rc, (j + 1) * rc)
        hid = r.x[rows, :].astype(F32) + rs_finish(j, rs[j]) + r.vec[2:3, :]
        r.hidden[rows, :] = hid
        normed, inverse = norm_rows(hid)
        r.n2[rows, :] = normed
        r.inv2[rows, :] = inverse
        ag[j] = ag_start(1, j, r.g2, (normed * r.vec[3:4, :] + r.vec[4:5, :]).astype(BF16))

    weights[1].wait()
    weights[2].wait()
    for j in range(C):
        ag_finish(1, j, r.g2)
        rows = rows4(r.g2, j)

        def up_body(n, carry):
            lanes = pl.ds(pl.multiple_of(n * TILE, TILE), TILE)
            u = mm(rows, r.wup[:, lanes], NN) + r.vec[pl.ds(8 + m, 1), lanes]
            a, b = gelu_both(u)
            r.act[:, pl.ds(j * rc, rc), lanes] = a.astype(BF16).reshape(mp_size, rc, TILE)
            r.big[:, pl.ds(j * rc, rc), lanes] = b.reshape(mp_size, rc, TILE)
            return carry

        lax.fori_loop(0, FU // TILE, up_body, 0)
        rs[j] = rs_start(1, j, pair_rows(r.act, j), lambda lanes: (r.wdown[:, lanes], NN))

    loss_scale = token_total / r.cnt[len(bits), 0:1, 0:1]
    for j in range(C):
        rows = slice(j * rc, (j + 1) * rc)
        out = r.hidden[rows, :] + rs_finish(j, rs[j]) + r.vec[5:6, :]
        r.bo[rows, :] = out.astype(BF16)
        valid = jnp.broadcast_to(r.valid[:, rows].astype(F32), (SHARE, rc)).T[:, 0:1]
        grad = valid * (out - r.t[rows, :].astype(F32)) * loss_scale
        r.ig[rows, :] = grad
        ag[j] = ag_start(2, j, r.g3, grad.astype(BF16))
        r.vg[5:6, :] += jnp.sum(grad, 0, keepdims=True)

    for j in range(C):
        ag_finish(2, j, r.g3)
        if j == C - 1:
            turn("third rows")
        rows = rows4(r.g3, j)

        def act_body(n, carry):
            lanes = pl.ds(pl.multiple_of(n * TILE, TILE), TILE)
            ga = mm(rows, r.wdown[lanes, :], NT)
            gu = ga * r.big[:, pl.ds(j * rc, rc), lanes].reshape(mp_size * rc, TILE)
            r.gup[:, pl.ds(j * rc, rc), lanes] = gu.astype(BF16).reshape(mp_size, rc, TILE)
            return carry

        lax.fori_loop(0, FU // TILE, act_body, 0)
        rs[j] = rs_start(2, j, pair_rows(r.gup, j), lambda lanes: (r.wup[lanes, :], NT))

    def whole_grad(left, right, width, dst):
        def body(n, carry):
            lanes = pl.ds(pl.multiple_of(n * TILE, TILE), TILE)
            r.stage[:, 0:width] = mm(right_tile(left, lanes), right[...].reshape(T, width), TN)
            put_out(r.stage.at[:, 0:width], dst.at[lanes, :])
            return carry

        lax.fori_loop(0, dst.shape[0] // TILE, body, 0)

    if not fast:
        whole_grad(r.act, r.g3, D, r.d_grad)

    for j in range(C):
        rows = slice(j * rc, (j + 1) * rc)
        gs = rs_finish(j, rs[j])
        gh = r.ig[rows, :] + norm_backward(gs, r.n2[rows, :], r.inv2[rows, :], r.vec[3:4, :])
        r.hidden[rows, :] = gh
        ag[j] = ag_start(3, j, r.g4, gh.astype(BF16))
        r.vg[2:3, :] += jnp.sum(gh, 0, keepdims=True)
        r.vg[3:4, :] += jnp.sum(gs * r.n2[rows, :], 0, keepdims=True)
        r.vg[4:5, :] += jnp.sum(gs, 0, keepdims=True)

    turn("second norm")
    if not fast:
        whole_grad(r.g2, r.gup, FU, r.u_grad)
    r.vg[pl.ds(8 + m, 1), :] = jnp.sum(r.gup[...].reshape(T, FU).astype(F32), 0, keepdims=True)

    for j in range(C):
        ag_finish(3, j, r.g4)

    def gm_body(o, carry):
        at = pl.ds(pl.multiple_of(o * R, R), R)
        gmx = mm(r.g4[o], r.wout[...], NT).astype(BF16)
        r.gm[at, :] = gmx
        r.vT[:, at] = gmx.T
        return carry

    lax.fori_loop(0, mp_size, gm_body, 0)
    turn("fourth rows")

    r.big[:, :, K_AT : K_AT + HW] = jnp.zeros((mp_size, R, HW), F32)
    r.big[:, :, V_AT : V_AT + HW] = jnp.zeros((mp_size, R, HW), F32)
    for pair in range(PAIRS):
        for i in range(n_blocks):
            ke = (i + 1) * BQ
            block = slice(i * BQ, (i + 1) * BQ)
            make_dist(i)

            def back_body(half, carry):
                h = 2 * pair + half
                row_mask = (pair_row == half).astype(F32).astype(BF16)
                lane_mask = (pair_lane == half).astype(F32).astype(BF16)
                lanes = slice(pair * PAIR, (pair + 1) * PAIR)
                p = jnp.exp2(head_scores(i, ke, h) - r.lse[h, :, block])
                gp = mm(r.qkv[0:ke, qkv_lanes(pair, 2)], r.vT[lanes, block] * row_mask, NN)
                inner = jnp.sum(p * gp, 0, keepdims=True)
                raw = (p * (gp - inner)).astype(BF16)
                low = p.astype(BF16)
                r.big[0 : i + 1, :, V_AT + lanes.start : V_AT + lanes.stop] += mm(
                    low, r.gm[block, lanes] * lane_mask, NN
                ).reshape(i + 1, BQ, PAIR)
                r.big[0 : i + 1, :, K_AT + lanes.start : K_AT + lanes.stop] += mm(
                    raw, r.qkv[block, qkv_lanes(pair, 0)] * lane_mask, NN
                ).reshape(i + 1, BQ, PAIR)
                at = pl.ds(pl.multiple_of(h * HD, HD), HD)
                r.big[i, at, Q_AT : Q_AT + BQ] = mm(r.kT[at, 0:ke], raw, NN) * (1.0 / math.sqrt(HD))
                return carry

            lax.fori_loop(0, 2, back_body, 0)
            rows = slice(pair * PAIR, (pair + 1) * PAIR)
            r.st[block, qkv_lanes(pair, 0)] = r.big[i, rows, Q_AT : Q_AT + BQ].T.astype(BF16)
            turn("block %d %d" % (pair, i))
        lanes = slice(pair * PAIR, (pair + 1) * PAIR)
        r.st[:, qkv_lanes(pair, 1)] = (
            r.big[:, :, K_AT + lanes.start : K_AT + lanes.stop].reshape(T, PAIR) * (1.0 / math.sqrt(HD))
        ).astype(BF16)
        r.st[:, qkv_lanes(pair, 2)] = (
            r.big[:, :, V_AT + lanes.start : V_AT + lanes.stop].reshape(T, PAIR).astype(BF16)
        )
        turn("pair %d" % pair)
    for pair in range(PAIRS):
        lanes = pl.ds(pl.multiple_of(m * HW + pair * PAIR, PAIR), PAIR)
        for row, kind in ((6, 0), (7, 2)):
            r.vg[row : row + 1, lanes] = jnp.sum(
                r.st[:, qkv_lanes(pair, kind)].astype(F32), 0, keepdims=True
            )

    if fast:
        fetch_state("u")
        fetch_state("q")

    for j in range(C):
        rs[j] = rs_start(3, j, pair_flat(r.st, j), lambda lanes: (r.wqkv[lanes, :], NT))

    turn("projections back")
    if not fast:
        whole_grad(r.mix, r.g4, D, r.o_grad)
        whole_grad(r.g1, r.st, 3 * HW, r.q_grad)

    for j in range(C):
        rows = slice(j * rc, (j + 1) * rc)
        gf = rs_finish(j, rs[j])
        normed, inverse = norm_rows(r.x[rows, :].astype(F32))
        r.ig[rows, :] = r.hidden[rows, :] + norm_backward(gf, normed, inverse, r.vec[0:1, :])
        r.vg[0:1, :] += jnp.sum(gf * normed, 0, keepdims=True)
        r.vg[1:2, :] += jnp.sum(gf, 0, keepdims=True)

    vector_send, vector_next = doubling(mp_bits + dp_bits, r.vs, r.vs_r, r.vs_ss, r.vs_rs)
    r.vs[0] = r.vg[...]
    vector_send(0)
    late["vector_next"] = vector_next
    turn("end")
    if fast:
        for name in parts:
            gather_end(name)
        for cp in local_out:
            cp.wait()
    else:
        for _ in bits:
            vector_next()
    rows = r.vec.shape[0]
    total = r.vs[len(bits), 0:rows]
    r.v_grad[...] = total
    new = adam_step(total, r.vec_state[0], r.vec_state[1], r.vec_state[2], 0.0, token_total)
    for k in range(3):
        r.v_new[k] = new[k]
    r.v_low[...] = new[0].astype(BF16)


Z_FIRST = ("d0",)
Y_FIRST = ("u1",)
ORDER = {
    "third rows": "yd1 c0d0",
    "second norm": "yu0 c0d1 c1d0 yu1 c1d1 c2d0",
    "block 0 0": "yo0 c0u0",
    "block 0 2": "c2d1",
    "block 0 3": "c0u1",
    "pair 0": "ed0 c1u0",
    "block 1 1": "yq0 c1u1 fd1",
    "block 1 2": "fd0",
    "block 1 3": "c2u1",
    "pair 1": "c2u0",
    "projections back": "yq1 g1d0 c0q0 g1d1 c1q0 c0o0 g2d0 fu0 c1o0 g3d0 c2q0 c0q1 fu1 g1u0",
    "end": """
c1q1 c2o0 g2d1 g3d1 g2u0 c2q1 fq0 g3u0 v hu1
fq1 fo0 v g1u1 g1q0 g1q1 g1o0 v g2q1 g2q0
g2o0 v g3q1 g2u1 g3o0 v g3q0 g3u1
""",
}


def pieces(head_width, units):
    return [
        ("d0", units // 2),
        ("d1", units // 2),
        ("u0", units // 2),
        ("u1", units // 2),
        ("o0", head_width),
    ] + [("q%d" % pair, 6 * HD) for pair in range(head_width // (2 * HD))]


SHARE = 128


def block_call(sizes, x, teacher, segments, valid, vectors, copies, states):
    dp_size, mp_size = sizes
    R, D = x.shape
    T = mp_size * R
    wqkv, wout, wup, wdown = copies
    HW = wout.shape[0]
    FU = wup.shape[1]
    C = CHUNKS
    rc = R // C
    n_bits = (dp_size * mp_size).bit_length() - 1
    NZ = dp_size // 2
    PAIRS = HW // (2 * HD)
    fast = D == dp_size * SHARE
    dma = pltpu.SemaphoreType.DMA
    V = pltpu.VMEM
    S = jax.ShapeDtypeStruct
    vmem = pl.BlockSpec(memory_space=pltpu.VMEM)
    anywhere = pl.BlockSpec(memory_space=pl.ANY)

    ins = {
        "x": (x, vmem),
        "t": (teacher, vmem),
        "segr": (segments, vmem),
        "valid": (valid.reshape(1, R), vmem),
        "vec_low": (vectors, vmem),
        "vec_state": (states[4], vmem),
        "wqkv_hbm": (wqkv, anywhere),
        "wout_hbm": (wout, anywhere),
        "wup_hbm": (wup, anywhere),
        "wdown_hbm": (wdown, anywhere),
    }
    outs = {
        "bo": (S((R, D), BF16), vmem),
        "ig": (S((R, D), F32), vmem),
        "v_grad": (S(vectors.shape, F32), vmem),
        "v_new": (S(states[4].shape, F32), vmem),
        "v_low": (S(vectors.shape, BF16), vmem),
    }
    if fast:
        shard = {"q": (3, SHARE, HW), "o": (HW, SHARE), "u": (SHARE, FU), "d": (FU, SHARE)}
        whole = {"q": (3, D, HW), "o": (HW, D), "u": (D, FU), "d": (FU, D)}
        for name, state in zip("qoud", states):
            ins["s%s_hbm" % name] = (state, anywhere)
        for name in "qoud":
            outs[name + "_grad"] = (S(shard[name], F32), anywhere)
        for name in "qoud":
            outs[name + "_new"] = (S((3,) + shard[name], F32), anywhere)
        for name in "qoud":
            outs[name + "_full"] = (S(whole[name], BF16), anywhere)
    else:
        outs["q_grad"] = (S((D, 3 * HW), F32), anywhere)
        outs["o_grad"] = (S((HW, D), F32), anywhere)
        outs["u_grad"] = (S((D, FU), F32), anywhere)
        outs["d_grad"] = (S((FU, D), F32), anywhere)
    scratch = {
        "wqkv": V((D, 3 * HW), BF16),
        "wout": V((HW, D), BF16),
        "wup": V((D, FU), BF16),
        "wdown": V((FU, D), BF16),
        "w_sem": dma((3,)),
        "wq_sem": dma((PAIRS, 3)),
        "vec": V(vectors.shape, F32),
        "g1": V((mp_size, R, D), BF16),
        "g2": V((mp_size, R, D), BF16),
        "g3": V((mp_size, R, D), BF16),
        "g4": V((mp_size, R, D), BF16),
        "qkv": V((T, 3 * HW), BF16),
        "qT": V((HW, T), BF16),
        "kT": V((HW, T), BF16),
        "vT": V((HW, T), BF16),
        "mixT": V((HW, BQ), BF16),
        "mix": V((T, HW), BF16),
        "lse": V((HW // HD, 1, T), F32),
        "hidden": V((R, D), F32),
        "n2": V((R, D), F32),
        "inv2": V((R, 1), F32),
        "act": V((mp_size, R, FU), BF16),
        "big": V((mp_size, R, FU), F32),
        "gup": V((mp_size, R, FU), BF16),
        "gm": V((T, HW), BF16),
        "st": V((T, 3 * HW), BF16),
        "pass_on": V((C, rc, D), F32),
        "keep": V((C, rc, D), F32),
        "rs_cs": V((C, 2, rc, D), BF16),
        "rs_cr": V((C, 2, rc, D), BF16),
        "rs_xs": V((C, rc, D), BF16),
        "rs_xr": V((C, rc, D), BF16),
        "cnt": V((n_bits + 1, 8, 128), F32),
        "cnt_r": V((n_bits, 8, 128), F32),
        "vg": V((16, D), F32),
        "vs": V((n_bits + 1, 16, D), F32),
        "vs_r": V((n_bits, 16, D), F32),
        "ag_ss": dma((4, C, 3)),
        "ag_rs": dma((4, C, 3)),
        "rs_ss": dma((4, C, 3)),
        "rs_rs": dma((4, C, 3)),
        "cnt_ss": dma((n_bits,)),
        "cnt_rs": dma((n_bits,)),
        "vs_ss": dma((n_bits,)),
        "vs_rs": dma((n_bits,)),
    }
    if fast:
        for name, w in pieces(HW, FU):
            shares = 1 if name in Z_FIRST else NZ
            rows = 2 * SHARE if name in Z_FIRST else SHARE
            scratch["ys" + name] = V((shares, SHARE, w), BF16)
            scratch["yr" + name] = V((shares, SHARE, w), BF16)
            scratch["zs" + name] = V((2, rows, w), BF16)
            scratch["zr" + name] = V((2, NZ - 1, rows, w), BF16)
        for name in "qoud":
            scratch["gr" + name] = V(shard[name], F32)
            scratch["nc" + name] = V(shard[name], BF16)
        scratch["sd"] = V((3,) + shard["d"], F32)
        scratch["so"] = V((3,) + shard["o"], F32)
        scratch["acc"] = V((SHARE, FU // 2), F32)
        scratch["wide"] = V((2 * SHARE, FU // 2), F32)
        n = len(pieces(HW, FU))
        scratch["s_sem"] = dma((n, 3))
        scratch["o_sem"] = dma((n, 5))
        scratch["y_ss"] = dma((n, NZ))
        scratch["y_rs"] = dma((n, NZ))
        scratch["z_ss"] = dma((n, 2, NZ - 1))
        scratch["z_rs"] = dma((n, 2, NZ - 1))
        scratch["az_ss"] = dma((n, 2, 2, NZ - 1))
        scratch["az_rs"] = dma((n, 2, 2, NZ - 1))
        scratch["ay_ss"] = dma((n, NZ))
        scratch["ay_rs"] = dma((n, NZ))
    else:
        scratch["stage"] = V((TILE, D), F32)
        scratch["stage_sem"] = dma
    names = list(ins) + list(outs) + list(scratch)
    results = pl.pallas_call(
        functools.partial(block_kernel, sizes, fast, names),
        out_shape=[v[0] for v in outs.values()],
        in_specs=[v[1] for v in ins.values()],
        out_specs=[v[1] for v in outs.values()],
        scratch_shapes=list(scratch.values()),
        compiler_params=pltpu.CompilerParams(
            collective_id=0, has_side_effects=True, vmem_limit_bytes=62 << 20
        ),
        name="block",
    )(*[v[0] for v in ins.values()])
    outs = dict(zip(outs, results))
    if fast:
        names, results = list(outs), list(outs.values())
        outs = dict(zip(names, settle(results)))
    return outs, fast


def settle_kernel(count, *refs):
    sources, results, held = refs[:count], refs[count : 2 * count], refs[2 * count : 3 * count]
    in_sem, out_sem = refs[3 * count :]
    loads = [pltpu.make_async_copy(sources[i], held[i], in_sem.at[i]) for i in range(count)]
    stores = [pltpu.make_async_copy(held[i], results[i], out_sem.at[i]) for i in range(count)]
    for cp in loads:
        cp.start()
    for load, store in zip(loads, stores):
        load.wait()
        store.start()
    for cp in stores:
        cp.wait()


def settle(arrays):
    anywhere = pl.BlockSpec(memory_space=pltpu.HBM)
    dma = pltpu.SemaphoreType.DMA((len(arrays),))
    return pl.pallas_call(
        functools.partial(settle_kernel, len(arrays)),
        out_shape=[jax.ShapeDtypeStruct(a.shape, a.dtype) for a in arrays],
        in_specs=[anywhere] * len(arrays),
        out_specs=[anywhere] * len(arrays),
        scratch_shapes=[pltpu.VMEM(a.shape, a.dtype) for a in arrays] + [dma, dma],
        compiler_params=pltpu.CompilerParams(vmem_limit_bytes=62 << 20),
        name="settle",
    )(*arrays)


def adam_update(gradient, stored, decay_factor, token_total):
    new = adam_step(gradient, stored[0], stored[1], stored[2], decay_factor, token_total)
    return (jnp.stack(new), new[0].astype(jnp.bfloat16))


def shards(
    inputs,
    teacher,
    segments,
    valid_mask,
    qkv_copy,
    out_copy,
    up_copy,
    down_copy,
    vector_copy,
    qkv_state,
    out_state,
    up_state,
    down_state,
    vector_state,
):
    sizes = (lax.axis_size("dp"), lax.axis_size("mp"))
    token_total = inputs.shape[0] * sizes[0] * sizes[1]
    width = inputs.shape[1]
    head_width = qkv_copy.shape[2]
    pairs = head_width // (2 * HD)
    outs, fast = block_call(
        sizes,
        inputs,
        teacher,
        segments,
        valid_mask,
        vector_copy,
        (qkv_copy.transpose(1, 0, 2), out_copy, up_copy, down_copy),
        (qkv_state.transpose(0, 2, 1, 3), out_state, up_state, down_state, vector_state),
    )
    vector_grad, vector_new, vector_low = outs["v_grad"], outs["v_new"], outs["v_low"]
    if fast:
        qkv_grad = outs["q_grad"].transpose(1, 0, 2)
        out_grad, up_grad, down_grad = (outs[n + "_grad"] for n in "oud")
        qkv_new = outs["q_new"].transpose(0, 2, 1, 3)
        out_new, up_new, down_new = (outs[n + "_new"] for n in "oud")
        qkv_full = outs["q_full"].transpose(1, 0, 2)
        out_full, up_full, down_full = (outs[n + "_full"] for n in "oud")
    else:
        qkv_local = outs["q_grad"].reshape(width, pairs, 3, 2 * HD)
        qkv_local = qkv_local.transpose(0, 2, 1, 3).reshape(width, 3, head_width)
        qkv_grad, out_grad, up_grad, down_grad = (
            lax.psum_scatter(qkv_local, "dp", scatter_dimension=0, tiled=True),
            lax.psum_scatter(outs["o_grad"], "dp", scatter_dimension=1, tiled=True),
            lax.psum_scatter(outs["u_grad"], "dp", scatter_dimension=0, tiled=True),
            lax.psum_scatter(outs["d_grad"], "dp", scatter_dimension=1, tiled=True),
        )
        qkv_new, qkv_low = adam_update(qkv_grad, qkv_state, decay_rate, token_total)
        out_new, out_low = adam_update(out_grad, out_state, decay_rate, token_total)
        up_new, up_low = adam_update(up_grad, up_state, decay_rate, token_total)
        down_new, down_low = adam_update(down_grad, down_state, decay_rate, token_total)
        qkv_full, out_full, up_full, down_full = (
            lax.all_gather(qkv_low, "dp", axis=0, tiled=True),
            lax.all_gather(out_low, "dp", axis=1, tiled=True),
            lax.all_gather(up_low, "dp", axis=0, tiled=True),
            lax.all_gather(down_low, "dp", axis=1, tiled=True),
        )
    return (
        outs["bo"],
        outs["ig"],
        qkv_grad,
        out_grad,
        up_grad,
        down_grad,
        vector_grad,
        qkv_new,
        out_new,
        up_new,
        down_new,
        vector_new,
        qkv_full,
        out_full,
        up_full,
        down_full,
        vector_low,
    )


def solution(mesh):
    in_specs = (
        P(("dp", "mp"), None),
        P(("dp", "mp"), None),
        P("dp", None),
        P(("dp", "mp")),
        P(None, None, "mp"),
        P("mp", None),
        P(None, "mp"),
        P("mp", None),
        P(),
        P(None, "dp", None, "mp"),
        P(None, "mp", "dp"),
        P(None, "dp", "mp"),
        P(None, "mp", "dp"),
        P(),
    )
    out_specs = (
        P(("dp", "mp"), None),
        P(("dp", "mp"), None),
        P("dp", None, "mp"),
        P("mp", "dp"),
        P("dp", "mp"),
        P("mp", "dp"),
        P(),
        P(None, "dp", None, "mp"),
        P(None, "mp", "dp"),
        P(None, "dp", "mp"),
        P(None, "mp", "dp"),
        P(),
        P(None, None, "mp"),
        P("mp", None),
        P(None, "mp"),
        P("mp", None),
        P(),
    )
    return jax.shard_map(shards, mesh=mesh, in_specs=in_specs, out_specs=out_specs, check_vma=False)
```

```python
import functools
import math
import types

import jax
import jax.numpy as jnp
from jax import lax
from jax.experimental import pallas as pl
from jax.experimental.pallas import tpu as pltpu
from jax.sharding import PartitionSpec as P

HEADS = 16
HD = 64

norm_eps = 1e-05
beta_one = 0.9
beta_two = 0.95
adam_eps = 1e-08
learn_rate = 0.001
decay_rate = 0.1
correction_one = 1.0 - (0.9**10) ** 10
correction_two = 1.0 - (0.95**10) ** 10
log2_e = 1.4426950408889634

CHUNKS = 2
BQ = 256
TILE = 256
MESH = pl.DeviceIdType.MESH
F32 = jnp.float32
BF16 = jnp.bfloat16
NN = ((1,), (0,))
NT = ((1,), (1,))
TN = ((0,), (0,))


def mm(a, b, dims):
    return lax.dot_general(a, b, (dims, ((), ())), preferred_element_type=F32)


def gelu_both(v):
    c = 0.7978845608
    v2 = v * v
    th = jnp.tanh(c * (v + 0.044715 * v2 * v))
    half = 0.5 * (1.0 + th)
    back = half + 0.5 * v * (1.0 - th * th) * (c * (1.0 + 3.0 * 0.044715 * v2))
    return v * half, back


def norm_rows(v):
    centred = v - jnp.mean(v, -1, keepdims=True)
    inverse = lax.rsqrt(jnp.mean(centred * centred, -1, keepdims=True) + norm_eps)
    return centred * inverse, inverse


def norm_backward(grad_out, normed, inverse, gain_row):
    scaled = grad_out * gain_row
    return inverse * (
        scaled
        - jnp.mean(scaled, -1, keepdims=True)
        - normed * jnp.mean(scaled * normed, -1, keepdims=True)
    )


def adam_step(gradient, weight, first, second, decay_factor, token_total):
    mean_grad = gradient / token_total
    moment_one = beta_one * first + (1.0 - beta_one) * mean_grad
    moment_two = beta_two * second + (1.0 - beta_two) * mean_grad * mean_grad
    update = (
        moment_one / correction_one / (jnp.sqrt(moment_two / correction_two) + adam_eps)
        + decay_factor * weight
    )
    return weight - learn_rate * update, moment_one, moment_two


def block_kernel(sizes, fast, names, *refs):
    r = types.SimpleNamespace(**dict(zip(names, refs)))
    dp_size, mp_size = sizes
    dp = lax.axis_index("dp")
    m = lax.axis_index("mp")
    core = lax.rem(m, 2)
    chip = m // 2
    mc = m + 1 - 2 * core
    mx = lax.rem(m + 2, 4)
    md = mc + mx - m
    C = CHUNKS
    R, D = r.x.shape
    rc = R // C
    T = mp_size * R
    HW = r.wout.shape[0]
    FU = r.wup.shape[1]
    LOCAL_HEADS = HW // HD
    PAIR = 2 * HD
    PAIRS = HW // PAIR
    token_total = float(dp_size * T)

    dp_bits = [("dp", b) for b in range(dp_size.bit_length() - 1)]
    mp_bits = [("mp", b) for b in range(mp_size.bit_length() - 1)]
    bits = dp_bits + mp_bits

    def flip(v, b):
        w = 1 << b
        return v + w - 2 * w * lax.rem(v // w, 2)

    def bit_partner(item):
        axis, b = item
        if axis == "mp":
            return (dp, flip(m, b))
        return (flip(dp, b), m)

    to_core = (dp, mc)
    to_x = (dp, mx)

    NZ = dp_size // 2
    z = dp // 2
    y = lax.rem(dp, 2)
    to_y = (dp + 1 - 2 * y, m)

    def line(direction):
        place = z + direction * (NZ - 1 - 2 * z)
        return place, (dp + 2 - 4 * direction, m)

    def local_copy(src, dst, sem):
        cp = pltpu.make_async_copy(src, dst, sem)
        cp.start()
        return cp

    def qkv_lanes(pair, kind):
        return slice((3 * pair + kind) * PAIR, (3 * pair + kind + 1) * PAIR)

    x_in = local_copy(r.x_hbm, r.x, r.in_sem.at[0])
    t_in = local_copy(r.t_hbm, r.t, r.in_sem.at[1])
    qkv_weights = [
        local_copy(
            r.wqkv_hbm.at[kind, :, pair * PAIR : (pair + 1) * PAIR],
            r.wqkv.at[:, qkv_lanes(pair, kind)],
            r.wq_sem.at[pair, kind],
        )
        for pair in range(PAIRS)
        for kind in range(3)
    ]
    weights = [
        local_copy(src, dst, r.w_sem.at[i])
        for i, (src, dst) in enumerate(
            [(r.wout_hbm, r.wout), (r.wup_hbm, r.wup), (r.wdown_hbm, r.wdown)]
        )
    ]
    if fast:
        parts = {}
        for name, width in pieces(HW, FU):
            left, right = {
                "d": (r.g3, r.act),
                "u": (r.g2, r.gup),
                "o": (r.g4, r.mix),
                "q": (r.g1, r.st),
            }[name[0]]
            parts[name] = (len(parts), left, right, width)
        state_in = {}

        def span(name):
            width = PAIR if name[0] == "q" else parts[name][3]
            return slice(int(name[1]) * width, (int(name[1]) + 1) * width)

        def piece(ref, name):
            at = span(name)
            if name[0] == "q":
                return ref.at[:, :, at]
            return ref.at[:, at] if name[0] == "u" else ref.at[at, :]

        def state_copies(name, out):
            far = getattr(r, name[0] + "_new") if out else getattr(r, "s%s_hbm" % name[0])
            at = span(name)
            if name[0] == "q":
                return [
                    (
                        far.at[:, kind, :, at],
                        r.big.at[0:3, SHARE : 2 * SHARE, kind * HW + at.start : kind * HW + at.stop],
                    )
                    for kind in range(3)
                ]
            if name[0] == "u":
                return [(far.at[:, :, at], r.big.at[0:3, 0:SHARE, at])]
            return [(far.at[:, at, :], getattr(r, "s" + name[0]).at[:, at, :])]

        def fetch_state(matrix):
            for name in parts:
                if name[0] == matrix:
                    p = parts[name][0]
                    state_in[name] = [
                        local_copy(far, near, r.s_sem.at[p, k])
                        for k, (far, near) in enumerate(state_copies(name, False))
                    ]

        fetch_state("d")
        fetch_state("o")

    vec_in = local_copy(r.vec_state_hbm, r.vec_state, r.in_sem.at[2])
    barrier = pltpu.get_barrier_semaphore()
    for item in bits:
        pl.semaphore_signal(barrier, inc=1, device_id=bit_partner(item), device_id_type=MESH)
    greetings = len(bits)
    if fast:
        for direction in range(2):
            place, following = line(direction)

            @pl.when(place < NZ - 1)
            def _():
                pl.semaphore_signal(barrier, inc=1, device_id=following, device_id_type=MESH)

        greetings = greetings + (z > 0).astype(jnp.int32) + (z < NZ - 1).astype(jnp.int32)
    r.vec[...] = r.vec_low[...].astype(F32)
    x_in.wait()
    for j in range(C):
        rows = slice(j * rc, (j + 1) * rc)
        normed, inverse = norm_rows(r.x[rows, :].astype(F32))
        r.g1[m, rows, :] = (normed * r.vec[0:1, :] + r.vec[1:2, :]).astype(BF16)
    r.vg[...] = jnp.zeros(r.vg.shape, F32)
    r.cnt[0] = jnp.zeros((8, 128), F32) + jnp.sum(r.valid[...].astype(F32))
    pl.semaphore_wait(barrier, greetings)

    def doubling(order, values, received, send_sems, recv_sems):
        copies = []

        def send(step):
            cp = pltpu.make_async_remote_copy(
                src_ref=values.at[step], dst_ref=received.at[step],
                send_sem=send_sems.at[step], recv_sem=recv_sems.at[step],
                device_id=bit_partner(order[step]), device_id_type=MESH,
            )
            cp.start()
            copies.append(cp)

        def following():
            step = len(copies) - 1
            copies[step].wait()
            values[step + 1] = values[step] + received[step]
            if step + 1 < len(order):
                send(step + 1)

        return send, following

    count_send, count_next = doubling(bits, r.cnt, r.cnt_r, r.cnt_ss, r.cnt_rs)

    def ag_copy(site, j, kind, ref, block, device):
        part = ref.at[block, pl.ds(j * rc, rc)]
        return pltpu.make_async_remote_copy(
            src_ref=part, dst_ref=part, send_sem=r.ag_ss.at[site, j, kind],
            recv_sem=r.ag_rs.at[site, j, kind], device_id=device, device_id_type=MESH,
        )

    def ag_send(site, j, ref):
        cx = ag_copy(site, j, 0, ref, m, to_x)
        cx.start()
        cc = ag_copy(site, j, 1, ref, m, to_core)
        cc.start()
        return cx, cc

    def ag_start(site, j, ref, value):
        ref[m, pl.ds(j * rc, rc), :] = value
        return ag_send(site, j, ref)

    def ag_forward(site, j, ref):
        cf = ag_copy(site, j, 2, ref, mx, to_core)
        cf.start()
        return cf

    def rs_copy(site, j, kind, src, dst, device):
        return pltpu.make_async_remote_copy(
            src_ref=src, dst_ref=dst, send_sem=r.rs_ss.at[site, j, kind],
            recv_sem=r.rs_rs.at[site, j, kind], device_id=device, device_id_type=MESH,
        )

    def rs_product(j, lhs, rhs_of, slot, kept_ref):
        def tile_body(n, carry):
            lanes = pl.ds(pl.multiple_of(n * TILE, TILE), TILE)
            rhs, dims = rhs_of(lanes)
            both = mm(lhs, rhs, dims)
            low, high = both[:rc], both[rc:]
            r.rs_cs[j, slot, :, lanes] = jnp.where(core == 0, high, low).astype(BF16)
            kept_ref[j, :, lanes] = jnp.where(core == 0, low, high)
            return carry

        lax.fori_loop(0, D // TILE, tile_body, 0)

    def rs_core(site, j, slot):
        cp = rs_copy(site, j, slot, r.rs_cs.at[j, slot], r.rs_cr.at[j, slot], to_core)
        cp.start()
        return cp

    def rs_own(site, j, lhs_of, rhs_of):
        rs_product(j, lhs_of(2 * chip), rhs_of, 1, r.keep)
        return rs_core(site, j, 1)

    def rs_other(site, j, lhs_of, rhs_of, between=None):
        rs_product(j, lhs_of(2 * (1 - chip)), rhs_of, 0, r.pass_on)
        c0 = rs_core(site, j, 0)
        c1 = between() if between else None
        c0.wait()
        r.rs_xs[j] = (r.pass_on[j] + r.rs_cr[j, 0].astype(F32)).astype(BF16)
        cx = rs_copy(site, j, 2, r.rs_xs.at[j], r.rs_xr.at[j], to_x)
        cx.start()
        return cx, c1

    def rs_start(site, j, lhs_of, rhs_of):
        return rs_other(site, j, lhs_of, rhs_of, lambda: rs_own(site, j, lhs_of, rhs_of))

    def rs_finish(j, copies):
        for cp in copies:
            cp.wait()
        return r.keep[j] + r.rs_cr[j, 1].astype(F32) + r.rs_xr[j].astype(F32)

    def share_rows(ref, share):
        lanes = pl.ds(pl.multiple_of(share * SHARE, SHARE), SHARE)
        return ref[:, :, lanes].reshape(T, SHARE).T

    def right_tile(ref, lanes):
        if len(ref.shape) == 3:
            return ref[:, :, lanes].reshape(T, lanes.size)
        return ref[:, lanes]

    def tiles(width):
        return width if width < 2 * TILE else TILE

    def part_tile(name, n, step):
        _, _, right, width = parts[name]
        lanes = pl.ds(pl.multiple_of(n * step, 128), step)
        from_lanes = pl.ds(pl.multiple_of(int(name[1]) * width + n * step, 128), step)
        return lanes, right_tile(right, from_lanes)

    def part_product(name, lhs, put):
        width = parts[name][3]
        step = tiles(width)

        def tile_body(n, carry):
            lanes, rhs = part_tile(name, n, step)
            put(lanes, mm(lhs, rhs, NN))
            return carry

        lax.fori_loop(0, width // step, tile_body, 0)

    def y_copy(name, i):
        p = parts[name][0]
        return pltpu.make_async_remote_copy(
            src_ref=getattr(r, "ys" + name).at[i], dst_ref=getattr(r, "yr" + name).at[i],
            send_sem=r.y_ss.at[p, i], recv_sem=r.y_rs.at[p, i], device_id=to_y, device_id_type=MESH,
        )

    def y_start(name):
        left = parts[name][1]
        out = getattr(r, "ys" + name)

        def pair_body(i, carry):
            lhs = jnp.concatenate(
                [share_rows(left, 4 * i + 1 - y), share_rows(left, 4 * i + 3 - y)], 0
            )

            def put(lanes, both):
                out[2 * i, :, lanes] = both[:SHARE].astype(BF16)
                out[2 * i + 1, :, lanes] = both[SHARE:].astype(BF16)

            part_product(name, lhs, put)
            y_copy(name, 2 * i).start()
            y_copy(name, 2 * i + 1).start()
            return carry

        lax.fori_loop(0, NZ // 2, pair_body, 0)

    def share_sum(name, target):
        got = getattr(r, "yr" + name)
        y_copy(name, target).wait_recv()

        def put(lanes, value):
            r.acc[0:SHARE, lanes] = value + got[target, :, lanes].astype(F32)

        part_product(name, share_rows(parts[name][1], 2 * target + y), put)

    def both_shares(name, target):
        def put(lanes, value):
            r.wide[:, lanes] = value

        left = parts[name][1]
        lanes = pl.ds(pl.multiple_of(2 * target * SHARE, 2 * SHARE), 2 * SHARE)
        part_product(name, left[:, :, lanes].reshape(T, 2 * SHARE).T, put)

    def z_copy(name, direction, step, device):
        p = parts[name][0]
        return pltpu.make_async_remote_copy(
            src_ref=getattr(r, "zs" + name).at[direction],
            dst_ref=getattr(r, "zr" + name).at[direction, step],
            send_sem=r.z_ss.at[p, direction, step], recv_sem=r.z_rs.at[p, direction, step],
            device_id=device, device_id_type=MESH,
        )

    def chain_step(name, step):
        out = getattr(r, "zs" + name)
        got = getattr(r, "zr" + name)
        width = parts[name][3]
        total = (r.wide if name in Z_FIRST else r.acc).at[:, 0:width]

        def one(direction, carry):
            place, following = line(direction)

            @pl.when(place <= step)
            def _():
                mirrored = NZ - 1 - step + place
                target = mirrored + direction * (NZ - 1 - 2 * mirrored)
                (both_shares if name in Z_FIRST else share_sum)(name, target)
                if step > 0:

                    @pl.when(place < step)
                    def _():
                        z_copy(name, direction, step - 1, following).wait_send()

                    @pl.when(place > 0)
                    def _():
                        z_copy(name, direction, step - 1, following).wait_recv()
                        total[...] += got[direction, step - 1].astype(F32)

                out[direction] = total[...].astype(BF16)
                z_copy(name, direction, step, following).start()

            return carry

        lax.fori_loop(0, 2, one, 0)

    def chain_end(name):
        got = getattr(r, "zr" + name)
        width = parts[name][3]
        total = (r.wide if name in Z_FIRST else r.acc).at[:, 0:width]
        (both_shares if name in Z_FIRST else share_sum)(name, z)

        def one(direction, carry):
            place, _ = line(direction)

            @pl.when(place > 0)
            def _():
                z_copy(name, direction, NZ - 2, (dp, m)).wait_recv()
                total[...] += got[direction, NZ - 2].astype(F32)

            return carry

        lax.fori_loop(0, 2, one, 0)

    def y_exchange(name):
        chain_end(name)
        width = parts[name][3]
        theirs = pl.ds(pl.multiple_of((1 - y) * SHARE, SHARE), SHARE)
        getattr(r, "ys" + name)[0] = r.wide[theirs, 0:width].astype(BF16)
        y_copy(name, 0).start()

    def a_src(name, share):
        ref = getattr(r, name[0] + "_full")
        at = pl.ds(pl.multiple_of(share * SHARE, SHARE), SHARE)
        if name[0] == "q":
            return ref.at[:, at, span(name)]
        return ref.at[at, span(name)] if name[0] == "u" else ref.at[span(name), at]

    def az_copy(name, side, direction, step, share, src, device):
        p = parts[name][0]
        return pltpu.make_async_remote_copy(
            src_ref=src, dst_ref=a_src(name, share), send_sem=r.az_ss.at[p, side, direction, step],
            recv_sem=r.az_rs.at[p, side, direction, step], device_id=device, device_id_type=MESH,
        )

    def ay_copy(name, place, src):
        p = parts[name][0]
        return pltpu.make_async_remote_copy(
            src_ref=src, dst_ref=a_src(name, 2 * place + y), send_sem=r.ay_ss.at[p, place],
            recv_sem=r.ay_rs.at[p, place], device_id=to_y, device_id_type=MESH,
        )

    local_out = []

    def finish_share(name):
        p, _, _, width = parts[name]
        matrix = name[0]
        at0 = span(name)
        if name in Z_FIRST:
            y_copy(name, 0).wait_recv()
            ours = pl.ds(pl.multiple_of(y * SHARE, SHARE), SHARE)
            r.acc[:, 0:width] = r.wide[ours, 0:width] + getattr(r, "yr" + name)[0].astype(F32)
        else:
            chain_end(name)
        for cp in state_in[name]:
            cp.wait()
        grad_out = getattr(r, "gr" + matrix)
        fresh = getattr(r, "nc" + matrix)

        def adam_block(cols, at, state, state_at):
            grad = r.acc[:, cols]
            if matrix in "do":
                grad = grad.T
            grad_out[at] = grad
            w, a, b = adam_step(
                grad,
                state[(0,) + state_at],
                state[(1,) + state_at],
                state[(2,) + state_at],
                decay_rate,
                token_total,
            )
            state[(0,) + state_at] = w
            state[(1,) + state_at] = a
            state[(2,) + state_at] = b
            fresh[at] = w.astype(BF16)

        if matrix == "q":
            for kind in range(3):
                adam_block(
                    slice(kind * PAIR, (kind + 1) * PAIR),
                    (kind, slice(None), at0),
                    r.big,
                    (slice(SHARE, 2 * SHARE), slice(kind * HW + at0.start, kind * HW + at0.stop)),
                )
        else:

            def adam_body(n, carry):
                cols = pl.ds(pl.multiple_of(n * SHARE, SHARE), SHARE)
                there = pl.ds(pl.multiple_of(at0.start + n * SHARE, SHARE), SHARE)
                if matrix == "u":
                    adam_block(cols, (slice(None), there), r.big, (slice(0, SHARE), there))
                else:
                    at = (there, slice(None))
                    adam_block(cols, at, getattr(r, "s" + matrix), at)
                return carry

            lax.fori_loop(0, width // SHARE, adam_body, 0)
        fresh = piece(fresh, name)
        if name in Y_FIRST:
            ay_copy(name, z, fresh).start()
        for direction in range(2):
            place, following = line(direction)

            @pl.when(place < NZ - 1)
            def _():
                az_copy(name, 0, direction, 0, 2 * z + y, fresh, following).start()

        if name not in Y_FIRST:
            ay_copy(name, z, fresh).start()
        local_out.append(local_copy(fresh, a_src(name, 2 * z + y), r.o_sem.at[p, 0]))
        local_out.append(
            local_copy(piece(grad_out, name), piece(getattr(r, matrix + "_grad"), name), r.o_sem.at[p, 1])
        )
        for k, (far, near) in enumerate(state_copies(name, True)):
            local_out.append(local_copy(near, far, r.o_sem.at[p, 2 + k]))

    def neighbour_share(name):
        part = a_src(name, 2 * z + 1 - y)
        ay_copy(name, z, part).wait_recv()
        for direction in range(2):
            place, following = line(direction)

            @pl.when(place < NZ - 1)
            def _():
                az_copy(name, 1, direction, 0, 2 * z + 1 - y, part, following).start()

    def gather_step(name, step):
        for side in range(2 if name in Y_FIRST else 1):
            for direction in range(2):
                place, following = line(direction)

                @pl.when(place >= step)
                def _():
                    source = z - step + 2 * step * direction
                    share = 2 * source + (1 - y if side else y)
                    part = a_src(name, share)
                    az_copy(name, side, direction, step - 1, share, part, following).wait_recv()
                    if step < NZ - 1:

                        @pl.when(place < NZ - 1)
                        def _():
                            az_copy(name, side, direction, step, share, part, following).start()

                    if name not in Y_FIRST:
                        ay_copy(name, source, part).start()

    def gather_end(name):
        part = a_src(name, 2 * z + y)

        def one(direction, carry):
            place, following = line(direction)

            @pl.when(place <= NZ - 2)
            def _():
                z_copy(name, direction, NZ - 2, following).wait_send()

            for step in range(NZ - 1):

                @pl.when((place >= step) & (place < NZ - 1))
                def _():
                    for side in range(2 if name in Y_FIRST else 1):
                        az_copy(name, side, direction, step, 2 * z + y, part, following).wait_send()

            return carry

        lax.fori_loop(0, 2, one, 0)
        if name in Z_FIRST:
            y_copy(name, 0).wait_send()
        if name in Y_FIRST:
            ay_copy(name, z, part).wait_send()

        def y_body(i, carry):
            if name not in Z_FIRST:
                y_copy(name, i).wait_send()
            if name not in Y_FIRST:
                there = a_src(name, 2 * i + y)
                ay_copy(name, i, there).wait_send()
                ay_copy(name, i, there).wait_recv()
            return carry

        lax.fori_loop(0, NZ, y_body, 0)

    def put_out(src, dst):
        cp = pltpu.make_async_copy(src, dst, r.stage_sem)
        cp.start()
        cp.wait()

    late = {}

    def turn(point):
        if not fast:
            return
        for item in ORDER.get(point, ()):
            kind, rest = item[0], item[1:]
            if kind == "v":
                late["vector_next"]()
            elif kind == "y":
                y_start(rest)
            elif kind == "f":
                finish_share(rest)
            elif kind == "e":
                y_exchange(rest)
            elif kind == "h":
                neighbour_share(rest)
            elif kind == "c":
                chain_step(rest[1:], int(rest[0]))
            elif kind == "g":
                gather_step(rest[1:], int(rest[0]))

    ag = {}
    for j in range(C):
        ag[j] = ag_send(0, j, r.g1)
    count_send(0)

    def w_copy(kind, src, block, device):
        return pltpu.make_async_remote_copy(
            src_ref=src, dst_ref=r.act.at[block], send_sem=r.ow_ss.at[kind],
            recv_sem=r.ow_rs.at[kind], device_id=device, device_id_type=MESH,
        )

    weights[0].wait()
    w_x = w_copy(0, r.wout, m, to_x)
    w_x.start()
    w_c = w_copy(1, r.wout, m, to_core)
    w_c.start()
    r.act[m] = r.wout[...]
    for w in qkv_weights:
        w.wait()

    def project(o):
        p = mm(r.g1[o], r.wqkv[...], NN)
        at = pl.ds(pl.multiple_of(o * R, R), R)
        for pair in range(PAIRS):
            rows = slice(pair * PAIR, (pair + 1) * PAIR)
            lanes = pl.ds(pl.multiple_of(m * HW + pair * PAIR, PAIR), PAIR)
            q, k, v = (p[:, qkv_lanes(pair, kind)] for kind in range(3))
            q = (q + r.vec[6:7, lanes]).astype(BF16)
            k = k.astype(BF16)
            v = (v + r.vec[7:8, lanes]).astype(BF16)
            for kind, value in enumerate((q, k, v)):
                r.qkv[at, qkv_lanes(pair, kind)] = value
            r.qT[rows, at] = q.T
            r.kT[rows, at] = k.T
            r.vT[rows, at] = v.T

    project(m)
    count_next()
    for j in range(C):
        ag[j][1].wait()
    project(mc)
    for _ in range(1, dp_size.bit_length() - 1):
        count_next()
    fw = {}
    for j in range(C):
        ag[j][0].wait()
        fw[j] = ag_forward(0, j, r.g1)
    project(mx)
    for j in range(C):
        fw[j].wait()
    project(md)

    pair_row = lax.broadcasted_iota(jnp.int32, (2 * HD, BQ), 0) // HD
    pair_lane = lax.broadcasted_iota(jnp.int32, (BQ, 2 * HD), 1) // HD
    scale2 = log2_e / math.sqrt(HD)
    K_AT, V_AT, Q_AT, DIST = 0, HW, 2 * HW, 3 * HW

    def make_dist(i):
        def one(b, carry):
            key = lax.broadcasted_iota(jnp.int32, (BQ, BQ), 0) + b * BQ
            query = lax.broadcasted_iota(jnp.int32, (BQ, BQ), 1) + i * BQ
            apart = query - key
            key_seg = r.segr[:, pl.ds(pl.multiple_of(b * BQ, BQ), BQ)]
            key_seg = jnp.broadcast_to(key_seg, (BQ, BQ)).T
            same = key_seg == r.segr[:, i * BQ : (i + 1) * BQ]
            r.big[b, :, DIST : DIST + BQ] = jnp.where((apart >= 0) & same, apart.astype(F32), jnp.inf)
            return carry

        lax.fori_loop(0, i + 1, one, 0)

    def head_slope(h):
        head = jnp.zeros((1, BQ), jnp.int32) + (m * LOCAL_HEADS + h + 1)
        return jnp.exp2(head.astype(F32) * (-8.0 / HEADS)) * log2_e

    def pair_lanes(h, start):
        return pl.ds(pl.multiple_of(start + (h // 2) * PAIR, PAIR), PAIR)

    def kind_lanes(h, kind):
        return pl.ds(pl.multiple_of((h // 2) * 3 * PAIR + kind * PAIR, PAIR), PAIR)

    def head_scores(i, ke, h):
        mask = (pair_row == lax.rem(h, 2)).astype(F32).astype(BF16)
        q_cols = r.qT[pair_lanes(h, 0), i * BQ : (i + 1) * BQ] * mask
        raw = mm(r.qkv[0:ke, kind_lanes(h, 1)], q_cols, NN)
        return raw * scale2 - head_slope(h) * r.big[0 : i + 1, :, DIST : DIST + BQ].reshape(ke, BQ)

    OWN, PASSING = slice(0, HW), slice(HW, 2 * HW)

    def mix_copy(kind, src, dst, device):
        return pltpu.make_async_remote_copy(
            src_ref=src, dst_ref=dst, send_sem=r.mix_ss.at[kind], recv_sem=r.mix_rs.at[kind],
            device_id=device, device_id_type=MESH,
        )

    def send_mixture(i):
        src = r.mix.at[i * BQ : (i + 1) * BQ, :]

        @pl.when(i // 2 != chip)
        def _():
            kind = (core + i) % 2
            lanes = pl.ds(pl.multiple_of(kind * HW, HW), HW)
            mix_copy(kind, src, r.gup.at[m, :, lanes], to_x).start()

        @pl.when(mc == i)
        def _():
            mix_copy(2, src, r.gup.at[m, :, OWN], to_core).start()

        @pl.when(m == i)
        def _():
            r.gup[m, :, OWN] = src[...]

    n_blocks = T // BQ
    for i in reversed(range(n_blocks)):
        ke = (i + 1) * BQ
        block = slice(i * BQ, (i + 1) * BQ)
        make_dist(i)

        def head_body(h, carry):
            s = head_scores(i, ke, h)
            top = jnp.max(s, 0, keepdims=True)
            e = jnp.exp2(s - top)
            total = jnp.sum(e, 0, keepdims=True)
            p = (e * (1.0 / total)).astype(BF16)
            r.lse[h, :, block] = top + jnp.log2(total)
            at = pl.ds(pl.multiple_of(h * HD, HD), HD)
            r.mixT[at, :] = mm(r.vT[at, 0:ke], p, NN).astype(BF16)
            return carry

        lax.fori_loop(0, LOCAL_HEADS, head_body, 0, unroll=True)
        r.mix[block, :] = r.mixT[...].T
        send_mixture(i)
        if i < mp_size.bit_length() - 1:
            count_next()

    def pair_rows(ref, j):
        def of(first):
            v = ref[pl.ds(first, 2), pl.ds(j * rc, rc), :]
            return v.reshape(2 * rc, v.shape[2])

        return of

    def pair_flat(ref, j):
        def of(first):
            a = ref[pl.ds(pl.multiple_of(first * R + j * rc, rc), rc), :]
            b = ref[pl.ds(pl.multiple_of(first * R + R + j * rc, rc), rc), :]
            return jnp.concatenate([a, b], 0)

        return of

    def ag_finish(site, j, ref):
        ag[j][0].wait()
        cf = ag_forward(site, j, ref)
        ag[j][1].wait()
        cf.wait()

    here = r.gup.at[m, :, OWN]
    mix_copy(1, here, here, to_x).wait_recv()
    m_f = mix_copy(3, r.gup.at[mx, :, PASSING], r.gup.at[mx, :, OWN], to_core)
    m_f.start()
    w_x.wait()
    w_f = w_copy(2, r.act.at[mx], mx, to_core)
    w_f.start()
    w_c.wait()
    mix_copy(0, here, here, to_x).wait_recv()
    mix_copy(2, here, here, to_core).wait_recv()
    m_f.wait()
    w_f.wait()
    for kind, device in ((0, to_x), (1, to_x), (2, to_core)):
        mix_copy(kind, here, here, device).wait_send()
    rs = {}
    for j in range(C):
        rows = slice(j * rc, (j + 1) * rc)

        def out_body(n, carry):
            lanes = pl.ds(pl.multiple_of(n * TILE, TILE), TILE)
            total = mm(r.gup[0, rows, OWN], r.act[0, :, lanes], NN)
            for q in range(1, mp_size):
                total += mm(r.gup[q, rows, OWN], r.act[q, :, lanes], NN)
            r.keep[j, :, lanes] = total
            return carry

        lax.fori_loop(0, D // TILE, out_body, 0)
        hid = r.x[rows, :].astype(F32) + r.keep[j] + r.vec[2:3, :]
        r.hidden[rows, :] = hid
        normed, inverse = norm_rows(hid)
        r.n2[rows, :] = normed
        r.inv2[rows, :] = inverse
        ag[j] = ag_start(1, j, r.g2, (normed * r.vec[3:4, :] + r.vec[4:5, :]).astype(BF16))

    weights[1].wait()
    weights[2].wait()
    def up_half(j, first):
        pair = pl.ds(first, 2)
        rows = pair_rows(r.g2, j)(first)

        def up_body(n, carry):
            lanes = pl.ds(pl.multiple_of(n * TILE, TILE), TILE)
            u = mm(rows, r.wup[:, lanes], NN) + r.vec[pl.ds(8 + m, 1), lanes]
            a, b = gelu_both(u)
            r.act[pair, pl.ds(j * rc, rc), lanes] = a.astype(BF16).reshape(2, rc, TILE)
            r.big[pair, pl.ds(j * rc, rc), lanes] = b.reshape(2, rc, TILE)
            return carry

        lax.fori_loop(0, FU // TILE, up_body, 0)

    def by_halves(site, gather, ref, half, left, rhs_of):
        own = {}
        for j in range(C):
            ag[j][1].wait()
            half(j, 2 * chip)
            own[j] = rs_own(site, j, pair_rows(left, j), rhs_of)
        for j in range(C):
            ag[j][0].wait()
            ag_forward(gather, j, ref).wait()
            if site == 2 and j == C - 1:
                turn("third rows")
            half(j, 2 * (1 - chip))
            cx, _ = rs_other(site, j, pair_rows(left, j), rhs_of)
            rs[j] = (cx, own[j])

    by_halves(1, 1, r.g2, up_half, r.act, lambda lanes: (r.wdown[:, lanes], NN))

    t_in.wait()
    loss_scale = token_total / r.cnt[len(bits), 0:1, 0:1]
    for j in range(C):
        rows = slice(j * rc, (j + 1) * rc)
        out = r.hidden[rows, :] + rs_finish(j, rs[j]) + r.vec[5:6, :]
        r.bo[rows, :] = out.astype(BF16)
        valid = jnp.broadcast_to(r.valid[:, rows].astype(F32), (SHARE, rc)).T[:, 0:1]
        grad = valid * (out - r.t[rows, :].astype(F32)) * loss_scale
        r.ig[rows, :] = grad
        ag[j] = ag_start(2, j, r.g3, grad.astype(BF16))
        r.vg[5:6, :] += jnp.sum(grad, 0, keepdims=True)
    bo_out = local_copy(r.bo, r.bo_hbm, r.in_sem.at[3])

    def act_half(j, first):
        pair = pl.ds(first, 2)
        rows = pair_rows(r.g3, j)(first)

        def act_body(n, carry):
            lanes = pl.ds(pl.multiple_of(n * TILE, TILE), TILE)
            ga = mm(rows, r.wdown[lanes, :], NT)
            gu = ga * r.big[pair, pl.ds(j * rc, rc), lanes].reshape(2 * rc, TILE)
            r.gup[pair, pl.ds(j * rc, rc), lanes] = gu.astype(BF16).reshape(2, rc, TILE)
            return carry

        lax.fori_loop(0, FU // TILE, act_body, 0)

    by_halves(2, 2, r.g3, act_half, r.gup, lambda lanes: (r.wup[lanes, :], NT))

    def whole_grad(left, right, width, dst):
        def body(n, carry):
            lanes = pl.ds(pl.multiple_of(n * TILE, TILE), TILE)
            r.stage[:, 0:width] = mm(right_tile(left, lanes), right[...].reshape(T, width), TN)
            put_out(r.stage.at[:, 0:width], dst.at[lanes, :])
            return carry

        lax.fori_loop(0, dst.shape[0] // TILE, body, 0)

    if not fast:
        whole_grad(r.act, r.g3, D, r.d_grad)

    for j in range(C):
        rows = slice(j * rc, (j + 1) * rc)
        gs = rs_finish(j, rs[j])
        gh = r.ig[rows, :] + norm_backward(gs, r.n2[rows, :], r.inv2[rows, :], r.vec[3:4, :])
        r.hidden[rows, :] = gh
        ag[j] = ag_start(3, j, r.g4, gh.astype(BF16))
        r.vg[2:3, :] += jnp.sum(gh, 0, keepdims=True)
        r.vg[3:4, :] += jnp.sum(gs * r.n2[rows, :], 0, keepdims=True)
        r.vg[4:5, :] += jnp.sum(gs, 0, keepdims=True)

    turn("second norm")
    if not fast:
        whole_grad(r.g2, r.gup, FU, r.u_grad)
    r.vg[pl.ds(8 + m, 1), :] = jnp.sum(r.gup[...].reshape(T, FU).astype(F32), 0, keepdims=True)

    for j in range(C):
        ag_finish(3, j, r.g4)

    def gm_body(o, carry):
        at = pl.ds(pl.multiple_of(o * R, R), R)
        gmx = mm(r.g4[o], r.wout[...], NT).astype(BF16)
        r.gm[at, :] = gmx
        r.vT[:, at] = gmx.T
        return carry

    lax.fori_loop(0, mp_size, gm_body, 0)
    turn("fourth rows")

    r.big[:, :, K_AT : K_AT + HW] = jnp.zeros((mp_size, R, HW), F32)
    r.big[:, :, V_AT : V_AT + HW] = jnp.zeros((mp_size, R, HW), F32)
    for pair in range(PAIRS):
        for i in range(n_blocks):
            ke = (i + 1) * BQ
            block = slice(i * BQ, (i + 1) * BQ)
            make_dist(i)

            def back_body(half, carry):
                h = 2 * pair + half
                row_mask = (pair_row == half).astype(F32).astype(BF16)
                lane_mask = (pair_lane == half).astype(F32).astype(BF16)
                lanes = slice(pair * PAIR, (pair + 1) * PAIR)
                p = jnp.exp2(head_scores(i, ke, h) - r.lse[h, :, block])
                gp = mm(r.qkv[0:ke, qkv_lanes(pair, 2)], r.vT[lanes, block] * row_mask, NN)
                inner = jnp.sum(p * gp, 0, keepdims=True)
                raw = (p * (gp - inner)).astype(BF16)
                low = p.astype(BF16)
                r.big[0 : i + 1, :, V_AT + lanes.start : V_AT + lanes.stop] += mm(
                    low, r.gm[block, lanes] * lane_mask, NN
                ).reshape(i + 1, BQ, PAIR)
                r.big[0 : i + 1, :, K_AT + lanes.start : K_AT + lanes.stop] += mm(
                    raw, r.qkv[block, qkv_lanes(pair, 0)] * lane_mask, NN
                ).reshape(i + 1, BQ, PAIR)
                at = pl.ds(pl.multiple_of(h * HD, HD), HD)
                r.big[i, at, Q_AT : Q_AT + BQ] = mm(r.kT[at, 0:ke], raw, NN) * (1.0 / math.sqrt(HD))
                return carry

            lax.fori_loop(0, 2, back_body, 0)
            rows = slice(pair * PAIR, (pair + 1) * PAIR)
            r.st[block, qkv_lanes(pair, 0)] = r.big[i, rows, Q_AT : Q_AT + BQ].T.astype(BF16)
            turn("block %d %d" % (pair, i))
        lanes = slice(pair * PAIR, (pair + 1) * PAIR)
        r.st[:, qkv_lanes(pair, 1)] = (
            r.big[:, :, K_AT + lanes.start : K_AT + lanes.stop].reshape(T, PAIR) * (1.0 / math.sqrt(HD))
        ).astype(BF16)
        r.st[:, qkv_lanes(pair, 2)] = (
            r.big[:, :, V_AT + lanes.start : V_AT + lanes.stop].reshape(T, PAIR).astype(BF16)
        )
        turn("pair %d" % pair)
    for pair in range(PAIRS):
        lanes = pl.ds(pl.multiple_of(m * HW + pair * PAIR, PAIR), PAIR)
        for row, kind in ((6, 0), (7, 2)):
            r.vg[row : row + 1, lanes] = jnp.sum(
                r.st[:, qkv_lanes(pair, kind)].astype(F32), 0, keepdims=True
            )

    if fast:
        fetch_state("u")
        fetch_state("q")

    for j in range(C):
        rs[j] = rs_start(3, j, pair_flat(r.st, j), lambda lanes: (r.wqkv[lanes, :], NT))

    turn("projections back")
    if not fast:
        whole_grad(r.mix, r.g4, D, r.o_grad)
        whole_grad(r.g1, r.st, 3 * HW, r.q_grad)

    for j in range(C):
        rows = slice(j * rc, (j + 1) * rc)
        gf = rs_finish(j, rs[j])
        normed, inverse = norm_rows(r.x[rows, :].astype(F32))
        r.ig[rows, :] = r.hidden[rows, :] + norm_backward(gf, normed, inverse, r.vec[0:1, :])
        r.vg[0:1, :] += jnp.sum(gf * normed, 0, keepdims=True)
        r.vg[1:2, :] += jnp.sum(gf, 0, keepdims=True)
    ig_out = local_copy(r.ig, r.ig_hbm, r.in_sem.at[4])

    vector_send, vector_step = doubling(mp_bits + dp_bits, r.vs, r.vs_r, r.vs_ss, r.vs_rs)
    r.vs[0] = r.vg[...]
    vector_send(0)
    vector_out = []

    def vector_next():
        vector_step()
        late["steps"] = late.get("steps", 0) + 1
        if late["steps"] < len(bits):
            return
        vec_in.wait()
        total = r.vs[len(bits), 0 : r.vec.shape[0]]
        new = adam_step(total, r.vec_state[0], r.vec_state[1], r.vec_state[2], 0.0, token_total)
        r.v_sum[...] = total
        for k in range(3):
            r.vec_state[k] = new[k]
        r.v_copy[...] = new[0].astype(BF16)
        for k, (near, far) in enumerate(
            [(r.v_sum, r.v_grad), (r.vec_state, r.v_new), (r.v_copy, r.v_low)]
        ):
            vector_out.append(local_copy(near, far, r.in_sem.at[5 + k]))

    late["vector_next"] = vector_next
    if fast:
        turn("end")
        for name in parts:
            gather_end(name)
        for cp in local_out:
            cp.wait()
    else:
        for _ in bits:
            vector_next()
    for cp in [bo_out, ig_out] + vector_out:
        cp.wait()


Z_FIRST = ("d0",)
Y_FIRST = ("u1",)
ORDER = {
    "third rows": ("yd1", "c0d0",),
    "second norm": ("c0d1", "yu0", "c1d0", "yu1", "c1d1", "c2d0",),
    "fourth rows": ("c0u0",),
    "block 0 1": ("c2d1",),
    "block 0 2": ("ed0",),
    "pair 0": ("yq0",),
    "block 1 0": ("c0u1",),
    "block 1 1": ("c1u0",),
    "block 1 2": ("c1u1", "fd1", "yo0",),
    "block 1 3": ("fd0", "c0q0", "c2u1",),
    "projections back": (
        "g1d0", "yq1", "c1q0", "g1d1", "c2u0", "c0o0", "fu1", "c2q0", "g2d1",
    ),
    "end": (
        "fu0", "c1o0", "c0q1", "g3d1", "g2d0", "fq0", "c2o0", "v", "c1q1", "g1u0",
        "hu1", "v", "g1q0", "fo0", "c2q1", "g2u0", "g1o0", "fq1", "g2o0", "g2q0",
        "g3q0", "v", "g1q1", "g2q1", "g1u1", "g3u0", "v", "g3q1", "g2u1", "g3d0",
        "v", "g3o0", "g3u1",
    ),
}


def pieces(head_width, units):
    return [
        ("d0", units // 2),
        ("d1", units // 2),
        ("u0", units // 2),
        ("u1", units // 2),
        ("o0", head_width),
    ] + [("q%d" % pair, 6 * HD) for pair in range(head_width // (2 * HD))]


SHARE = 128


def block_call(sizes, x, teacher, segments, valid, vectors, copies, states):
    dp_size, mp_size = sizes
    R, D = x.shape
    T = mp_size * R
    wqkv, wout, wup, wdown = copies
    HW = wout.shape[0]
    FU = wup.shape[1]
    C = CHUNKS
    rc = R // C
    n_bits = (dp_size * mp_size).bit_length() - 1
    NZ = dp_size // 2
    PAIRS = HW // (2 * HD)
    fast = D == dp_size * SHARE
    dma = pltpu.SemaphoreType.DMA
    V = pltpu.VMEM
    S = jax.ShapeDtypeStruct
    vmem = pl.BlockSpec(memory_space=pltpu.VMEM)
    anywhere = pl.BlockSpec(memory_space=pl.ANY)

    ins = {
        "x_hbm": (x, anywhere),
        "t_hbm": (teacher, anywhere),
        "segr": (segments, vmem),
        "valid": (valid.reshape(1, R), vmem),
        "vec_low": (vectors, vmem),
        "vec_state_hbm": (states[4], anywhere),
        "wqkv_hbm": (wqkv, anywhere),
        "wout_hbm": (wout, anywhere),
        "wup_hbm": (wup, anywhere),
        "wdown_hbm": (wdown, anywhere),
    }
    outs = {
        "bo_hbm": (S((R, D), BF16), anywhere),
        "ig_hbm": (S((R, D), F32), anywhere),
        "v_grad": (S(vectors.shape, F32), anywhere),
        "v_new": (S(states[4].shape, F32), anywhere),
        "v_low": (S(vectors.shape, BF16), anywhere),
    }
    if fast:
        shard = {"q": (3, SHARE, HW), "o": (HW, SHARE), "u": (SHARE, FU), "d": (FU, SHARE)}
        whole = {"q": (3, D, HW), "o": (HW, D), "u": (D, FU), "d": (FU, D)}
        for name, state in zip("qoud", states):
            ins["s%s_hbm" % name] = (state, anywhere)
        for name in "qoud":
            outs[name + "_grad"] = (S(shard[name], F32), anywhere)
        for name in "qoud":
            outs[name + "_new"] = (S((3,) + shard[name], F32), anywhere)
        for name in "qoud":
            outs[name + "_full"] = (S(whole[name], BF16), anywhere)
    else:
        outs["q_grad"] = (S((D, 3 * HW), F32), anywhere)
        outs["o_grad"] = (S((HW, D), F32), anywhere)
        outs["u_grad"] = (S((D, FU), F32), anywhere)
        outs["d_grad"] = (S((FU, D), F32), anywhere)
    scratch = {
        "wqkv": V((D, 3 * HW), BF16),
        "wout": V((HW, D), BF16),
        "wup": V((D, FU), BF16),
        "wdown": V((FU, D), BF16),
        "w_sem": dma((3,)),
        "ow_ss": dma((3,)),
        "ow_rs": dma((3,)),
        "mix_ss": dma((4,)),
        "mix_rs": dma((4,)),
        "in_sem": dma((8,)),
        "x": V((R, D), BF16),
        "t": V((R, D), BF16),
        "bo": V((R, D), BF16),
        "ig": V((R, D), F32),
        "vec_state": V(states[4].shape, F32),
        "v_sum": V(vectors.shape, F32),
        "v_copy": V(vectors.shape, BF16),
        "wq_sem": dma((PAIRS, 3)),
        "vec": V(vectors.shape, F32),
        "g1": V((mp_size, R, D), BF16),
        "g2": V((mp_size, R, D), BF16),
        "g3": V((mp_size, R, D), BF16),
        "g4": V((mp_size, R, D), BF16),
        "qkv": V((T, 3 * HW), BF16),
        "qT": V((HW, T), BF16),
        "kT": V((HW, T), BF16),
        "vT": V((HW, T), BF16),
        "mixT": V((HW, BQ), BF16),
        "mix": V((T, HW), BF16),
        "lse": V((HW // HD, 1, T), F32),
        "hidden": V((R, D), F32),
        "n2": V((R, D), F32),
        "inv2": V((R, 1), F32),
        "act": V((mp_size, R, FU), BF16),
        "big": V((mp_size, R, FU), F32),
        "gup": V((mp_size, R, FU), BF16),
        "gm": V((T, HW), BF16),
        "st": V((T, 3 * HW), BF16),
        "pass_on": V((C, rc, D), F32),
        "keep": V((C, rc, D), F32),
        "rs_cs": V((C, 2, rc, D), BF16),
        "rs_cr": V((C, 2, rc, D), BF16),
        "rs_xs": V((C, rc, D), BF16),
        "rs_xr": V((C, rc, D), BF16),
        "cnt": V((n_bits + 1, 8, 128), F32),
        "cnt_r": V((n_bits, 8, 128), F32),
        "vg": V((16, D), F32),
        "vs": V((n_bits + 1, 16, D), F32),
        "vs_r": V((n_bits, 16, D), F32),
        "ag_ss": dma((4, C, 3)),
        "ag_rs": dma((4, C, 3)),
        "rs_ss": dma((4, C, 3)),
        "rs_rs": dma((4, C, 3)),
        "cnt_ss": dma((n_bits,)),
        "cnt_rs": dma((n_bits,)),
        "vs_ss": dma((n_bits,)),
        "vs_rs": dma((n_bits,)),
    }
    if fast:
        for name, w in pieces(HW, FU):
            shares = 1 if name in Z_FIRST else NZ
            rows = 2 * SHARE if name in Z_FIRST else SHARE
            scratch["ys" + name] = V((shares, SHARE, w), BF16)
            scratch["yr" + name] = V((shares, SHARE, w), BF16)
            scratch["zs" + name] = V((2, rows, w), BF16)
            scratch["zr" + name] = V((2, NZ - 1, rows, w), BF16)
        for name in "qoud":
            scratch["gr" + name] = V(shard[name], F32)
            scratch["nc" + name] = V(shard[name], BF16)
        scratch["sd"] = V((3,) + shard["d"], F32)
        scratch["so"] = V((3,) + shard["o"], F32)
        scratch["acc"] = V((SHARE, FU // 2), F32)
        scratch["wide"] = V((2 * SHARE, FU // 2), F32)
        n = len(pieces(HW, FU))
        scratch["s_sem"] = dma((n, 3))
        scratch["o_sem"] = dma((n, 5))
        scratch["y_ss"] = dma((n, NZ))
        scratch["y_rs"] = dma((n, NZ))
        scratch["z_ss"] = dma((n, 2, NZ - 1))
        scratch["z_rs"] = dma((n, 2, NZ - 1))
        scratch["az_ss"] = dma((n, 2, 2, NZ - 1))
        scratch["az_rs"] = dma((n, 2, 2, NZ - 1))
        scratch["ay_ss"] = dma((n, NZ))
        scratch["ay_rs"] = dma((n, NZ))
    else:
        scratch["stage"] = V((TILE, D), F32)
        scratch["stage_sem"] = dma
    names = list(ins) + list(outs) + list(scratch)
    results = pl.pallas_call(
        functools.partial(block_kernel, sizes, fast, names),
        out_shape=[v[0] for v in outs.values()],
        in_specs=[v[1] for v in ins.values()],
        out_specs=[v[1] for v in outs.values()],
        scratch_shapes=list(scratch.values()),
        compiler_params=pltpu.CompilerParams(
            collective_id=0, has_side_effects=True, vmem_limit_bytes=62 << 20
        ),
        name="block",
    )(*[v[0] for v in ins.values()])
    outs = dict(zip(outs, results))
    if fast:
        names, results = list(outs), list(outs.values())
        outs = dict(zip(names, settle(results)))
    return outs, fast


def settle_kernel(count, *refs):
    sources, results, held = refs[:count], refs[count : 2 * count], refs[2 * count : 3 * count]
    in_sem, out_sem = refs[3 * count :]
    loads = [pltpu.make_async_copy(sources[i], held[i], in_sem.at[i]) for i in range(count)]
    stores = [pltpu.make_async_copy(held[i], results[i], out_sem.at[i]) for i in range(count)]
    for cp in loads:
        cp.start()
    for load, store in zip(loads, stores):
        load.wait()
        store.start()
    for cp in stores:
        cp.wait()


def settle(arrays):
    anywhere = pl.BlockSpec(memory_space=pltpu.HBM)
    dma = pltpu.SemaphoreType.DMA((len(arrays),))
    return pl.pallas_call(
        functools.partial(settle_kernel, len(arrays)),
        out_shape=[jax.ShapeDtypeStruct(a.shape, a.dtype) for a in arrays],
        in_specs=[anywhere] * len(arrays),
        out_specs=[anywhere] * len(arrays),
        scratch_shapes=[pltpu.VMEM(a.shape, a.dtype) for a in arrays] + [dma, dma],
        compiler_params=pltpu.CompilerParams(vmem_limit_bytes=62 << 20),
        name="settle",
    )(*arrays)


def adam_update(gradient, stored, decay_factor, token_total):
    new = adam_step(gradient, stored[0], stored[1], stored[2], decay_factor, token_total)
    return (jnp.stack(new), new[0].astype(jnp.bfloat16))


def shards(
    inputs,
    teacher,
    segments,
    valid_mask,
    qkv_copy,
    out_copy,
    up_copy,
    down_copy,
    vector_copy,
    qkv_state,
    out_state,
    up_state,
    down_state,
    vector_state,
):
    sizes = (lax.axis_size("dp"), lax.axis_size("mp"))
    token_total = inputs.shape[0] * sizes[0] * sizes[1]
    width = inputs.shape[1]
    head_width = qkv_copy.shape[2]
    pairs = head_width // (2 * HD)
    outs, fast = block_call(
        sizes,
        inputs,
        teacher,
        segments,
        valid_mask,
        vector_copy,
        (qkv_copy.transpose(1, 0, 2), out_copy, up_copy, down_copy),
        (qkv_state.transpose(0, 2, 1, 3), out_state, up_state, down_state, vector_state),
    )
    vector_grad, vector_new, vector_low = outs["v_grad"], outs["v_new"], outs["v_low"]
    if fast:
        qkv_grad = outs["q_grad"].transpose(1, 0, 2)
        out_grad, up_grad, down_grad = (outs[n + "_grad"] for n in "oud")
        qkv_new = outs["q_new"].transpose(0, 2, 1, 3)
        out_new, up_new, down_new = (outs[n + "_new"] for n in "oud")
        qkv_full = outs["q_full"].transpose(1, 0, 2)
        out_full, up_full, down_full = (outs[n + "_full"] for n in "oud")
    else:
        qkv_local = outs["q_grad"].reshape(width, pairs, 3, 2 * HD)
        qkv_local = qkv_local.transpose(0, 2, 1, 3).reshape(width, 3, head_width)
        qkv_grad, out_grad, up_grad, down_grad = (
            lax.psum_scatter(qkv_local, "dp", scatter_dimension=0, tiled=True),
            lax.psum_scatter(outs["o_grad"], "dp", scatter_dimension=1, tiled=True),
            lax.psum_scatter(outs["u_grad"], "dp", scatter_dimension=0, tiled=True),
            lax.psum_scatter(outs["d_grad"], "dp", scatter_dimension=1, tiled=True),
        )
        qkv_new, qkv_low = adam_update(qkv_grad, qkv_state, decay_rate, token_total)
        out_new, out_low = adam_update(out_grad, out_state, decay_rate, token_total)
        up_new, up_low = adam_update(up_grad, up_state, decay_rate, token_total)
        down_new, down_low = adam_update(down_grad, down_state, decay_rate, token_total)
        qkv_full, out_full, up_full, down_full = (
            lax.all_gather(qkv_low, "dp", axis=0, tiled=True),
            lax.all_gather(out_low, "dp", axis=1, tiled=True),
            lax.all_gather(up_low, "dp", axis=0, tiled=True),
            lax.all_gather(down_low, "dp", axis=1, tiled=True),
        )
    return (
        outs["bo_hbm"],
        outs["ig_hbm"],
        qkv_grad,
        out_grad,
        up_grad,
        down_grad,
        vector_grad,
        qkv_new,
        out_new,
        up_new,
        down_new,
        vector_new,
        qkv_full,
        out_full,
        up_full,
        down_full,
        vector_low,
    )


def solution(mesh):
    in_specs = (
        P(("dp", "mp"), None),
        P(("dp", "mp"), None),
        P("dp", None),
        P(("dp", "mp")),
        P(None, None, "mp"),
        P("mp", None),
        P(None, "mp"),
        P("mp", None),
        P(),
        P(None, "dp", None, "mp"),
        P(None, "mp", "dp"),
        P(None, "dp", "mp"),
        P(None, "mp", "dp"),
        P(),
    )
    out_specs = (
        P(("dp", "mp"), None),
        P(("dp", "mp"), None),
        P("dp", None, "mp"),
        P("mp", "dp"),
        P("dp", "mp"),
        P("mp", "dp"),
        P(),
        P(None, "dp", None, "mp"),
        P(None, "mp", "dp"),
        P(None, "dp", "mp"),
        P(None, "mp", "dp"),
        P(),
        P(None, None, "mp"),
        P("mp", None),
        P(None, "mp"),
        P("mp", None),
        P(),
    )
    return jax.shard_map(shards, mesh=mesh, in_specs=in_specs, out_specs=out_specs, check_vma=False)
```

```python
import functools
import math
import types

import jax
import jax.numpy as jnp
from jax import lax
from jax.experimental import pallas as pl
from jax.experimental.pallas import tpu as pltpu
from jax.sharding import PartitionSpec as P

HEADS = 16
HD = 64

norm_eps = 1e-05
beta_one = 0.9
beta_two = 0.95
adam_eps = 1e-08
learn_rate = 0.001
decay_rate = 0.1
correction_one = 1.0 - (0.9**10) ** 10
correction_two = 1.0 - (0.95**10) ** 10
log2_e = 1.4426950408889634

CHUNKS = 2
BQ = 256
TILE = 256
MESH = pl.DeviceIdType.MESH
F32 = jnp.float32
BF16 = jnp.bfloat16
NN = ((1,), (0,))
NT = ((1,), (1,))
TN = ((0,), (0,))


def mm(a, b, dims):
    return lax.dot_general(a, b, (dims, ((), ())), preferred_element_type=F32)


def gelu_both(v):
    c = 0.7978845608
    v2 = v * v
    th = jnp.tanh(c * (v + 0.044715 * v2 * v))
    half = 0.5 * (1.0 + th)
    back = half + 0.5 * v * (1.0 - th * th) * (c * (1.0 + 3.0 * 0.044715 * v2))
    return v * half, back


def norm_rows(v):
    centred = v - jnp.mean(v, -1, keepdims=True)
    inverse = lax.rsqrt(jnp.mean(centred * centred, -1, keepdims=True) + norm_eps)
    return centred * inverse, inverse


def norm_backward(grad_out, normed, inverse, gain_row):
    scaled = grad_out * gain_row
    return inverse * (
        scaled
        - jnp.mean(scaled, -1, keepdims=True)
        - normed * jnp.mean(scaled * normed, -1, keepdims=True)
    )


def adam_step(gradient, weight, first, second, decay_factor, token_total):
    mean_grad = gradient / token_total
    moment_one = beta_one * first + (1.0 - beta_one) * mean_grad
    moment_two = beta_two * second + (1.0 - beta_two) * mean_grad * mean_grad
    update = (
        moment_one / correction_one / (jnp.sqrt(moment_two / correction_two) + adam_eps)
        + decay_factor * weight
    )
    return weight - learn_rate * update, moment_one, moment_two


def block_kernel(sizes, fast, names, *refs):
    r = types.SimpleNamespace(**dict(zip(names, refs)))
    dp_size, mp_size = sizes
    dp = lax.axis_index("dp")
    m = lax.axis_index("mp")
    core = lax.rem(m, 2)
    chip = m // 2
    mc = m + 1 - 2 * core
    mx = lax.rem(m + 2, 4)
    md = mc + mx - m
    C = CHUNKS
    R, D = r.x.shape
    rc = R // C
    T = mp_size * R
    HW = r.wout.shape[0]
    FU = r.wup.shape[1]
    LOCAL_HEADS = HW // HD
    PAIR = 2 * HD
    PAIRS = HW // PAIR
    token_total = float(dp_size * T)

    dp_bits = [("dp", b) for b in range(dp_size.bit_length() - 1)]
    mp_bits = [("mp", b) for b in range(mp_size.bit_length() - 1)]
    bits = dp_bits + mp_bits

    def flip(v, b):
        w = 1 << b
        return v + w - 2 * w * lax.rem(v // w, 2)

    def bit_partner(item):
        axis, b = item
        if axis == "mp":
            return (dp, flip(m, b))
        return (flip(dp, b), m)

    to_core = (dp, mc)
    to_x = (dp, mx)

    NZ = dp_size // 2
    z = dp // 2
    y = lax.rem(dp, 2)
    to_y = (dp + 1 - 2 * y, m)

    def line(direction):
        place = z + direction * (NZ - 1 - 2 * z)
        return place, (dp + 2 - 4 * direction, m)

    def local_copy(src, dst, sem):
        cp = pltpu.make_async_copy(src, dst, sem)
        cp.start()
        return cp

    def qkv_lanes(pair, kind):
        return slice((3 * pair + kind) * PAIR, (3 * pair + kind + 1) * PAIR)

    x_in = local_copy(r.x_hbm, r.x, r.in_sem.at[0])
    t_in = local_copy(r.t_hbm, r.t, r.in_sem.at[1])
    qkv_weights = [
        local_copy(
            r.wqkv_hbm.at[kind, :, pair * PAIR : (pair + 1) * PAIR],
            r.wqkv.at[:, qkv_lanes(pair, kind)],
            r.wq_sem.at[pair, kind],
        )
        for pair in range(PAIRS)
        for kind in range(3)
    ]
    weights = [
        local_copy(src, dst, r.w_sem.at[i])
        for i, (src, dst) in enumerate(
            [(r.wout_hbm, r.wout), (r.wup_hbm, r.wup), (r.wdown_hbm, r.wdown)]
        )
    ]
    if fast:
        parts = {}
        for name, width in pieces(HW, FU):
            left, right = {
                "d": (r.g3, r.act),
                "u": (r.g2, r.gup),
                "o": (r.g4, r.mix),
                "q": (r.g1, r.st),
            }[name[0]]
            parts[name] = (len(parts), left, right, width)
        names_of = list(parts)
        state_in = {}

        def span(name):
            width = PAIR if name[0] == "q" else parts[name][3]
            return slice(int(name[1]) * width, (int(name[1]) + 1) * width)

        def piece(ref, name):
            at = span(name)
            if name[0] == "q":
                return ref.at[:, :, at]
            return ref.at[:, at] if name[0] == "u" else ref.at[at, :]

        def state_copies(name, out):
            far = getattr(r, name[0] + "_new") if out else getattr(r, "s%s_hbm" % name[0])
            at = span(name)
            if name[0] == "q":
                return [
                    (
                        far.at[:, kind, :, at],
                        r.big.at[0:3, SHARE : 2 * SHARE, kind * HW + at.start : kind * HW + at.stop],
                    )
                    for kind in range(3)
                ]
            if name[0] == "u":
                return [(far.at[:, :, at], r.big.at[0:3, 0:SHARE, at])]
            return [(far.at[:, at, :], getattr(r, "s" + name[0]).at[:, at, :])]

        def fetch_state(matrix):
            for name in parts:
                if name[0] == matrix:
                    p = parts[name][0]
                    state_in[name] = [
                        local_copy(far, near, r.s_sem.at[p, k])
                        for k, (far, near) in enumerate(state_copies(name, False))
                    ]

        fetch_state("d")
        fetch_state("o")

    vec_in = local_copy(r.vec_state_hbm, r.vec_state, r.in_sem.at[2])
    barrier = pltpu.get_barrier_semaphore()
    for item in bits:
        pl.semaphore_signal(barrier, inc=1, device_id=bit_partner(item), device_id_type=MESH)
    greetings = len(bits)
    if fast:
        for direction in range(2):
            place, following = line(direction)

            @pl.when(place < NZ - 1)
            def _():
                pl.semaphore_signal(barrier, inc=1, device_id=following, device_id_type=MESH)

        greetings = greetings + (z > 0).astype(jnp.int32) + (z < NZ - 1).astype(jnp.int32)
    r.vec[...] = r.vec_low[...].astype(F32)
    x_in.wait()
    for j in range(C):
        rows = slice(j * rc, (j + 1) * rc)
        normed, inverse = norm_rows(r.x[rows, :].astype(F32))
        r.g1[m, rows, :] = (normed * r.vec[0:1, :] + r.vec[1:2, :]).astype(BF16)
    r.vg[...] = jnp.zeros(r.vg.shape, F32)
    r.cnt[0] = jnp.zeros((8, 128), F32) + jnp.sum(r.valid[...].astype(F32))
    pl.semaphore_wait(barrier, greetings)

    def doubling(order, values, received, send_sems, recv_sems):
        copies = []

        def send(step):
            cp = pltpu.make_async_remote_copy(
                src_ref=values.at[step], dst_ref=received.at[step],
                send_sem=send_sems.at[step], recv_sem=recv_sems.at[step],
                device_id=bit_partner(order[step]), device_id_type=MESH,
            )
            cp.start()
            copies.append(cp)

        def following():
            step = len(copies) - 1
            copies[step].wait()
            values[step + 1] = values[step] + received[step]
            if step + 1 < len(order):
                send(step + 1)

        return send, following

    count_send, count_next = doubling(bits, r.cnt, r.cnt_r, r.cnt_ss, r.cnt_rs)

    def ag_copy(site, j, kind, ref, block, device):
        part = ref.at[block, pl.ds(j * rc, rc)]
        return pltpu.make_async_remote_copy(
            src_ref=part, dst_ref=part, send_sem=r.ag_ss.at[site, j, kind],
            recv_sem=r.ag_rs.at[site, j, kind], device_id=device, device_id_type=MESH,
        )

    def ag_send(site, j, ref):
        cx = ag_copy(site, j, 0, ref, m, to_x)
        cx.start()
        cc = ag_copy(site, j, 1, ref, m, to_core)
        cc.start()
        return cx, cc

    def ag_start(site, j, ref, value):
        ref[m, pl.ds(j * rc, rc), :] = value
        return ag_send(site, j, ref)

    def ag_forward(site, j, ref):
        cf = ag_copy(site, j, 2, ref, mx, to_core)
        cf.start()
        return cf

    def rs_copy(site, j, kind, src, dst, device):
        return pltpu.make_async_remote_copy(
            src_ref=src, dst_ref=dst, send_sem=r.rs_ss.at[site, j, kind],
            recv_sem=r.rs_rs.at[site, j, kind], device_id=device, device_id_type=MESH,
        )

    def rs_product(j, lhs, rhs_of, slot, kept_ref):
        def tile_body(n, carry):
            lanes = pl.ds(pl.multiple_of(n * TILE, TILE), TILE)
            rhs, dims = rhs_of(lanes)
            both = mm(lhs, rhs, dims)
            low, high = both[:rc], both[rc:]
            r.rs_cs[j, slot, :, lanes] = jnp.where(core == 0, high, low).astype(BF16)
            kept_ref[j, :, lanes] = jnp.where(core == 0, low, high)
            return carry

        lax.fori_loop(0, D // TILE, tile_body, 0)

    def rs_core(site, j, slot):
        cp = rs_copy(site, j, slot, r.rs_cs.at[j, slot], r.rs_cr.at[j, slot], to_core)
        cp.start()
        return cp

    def rs_own(site, j, lhs_of, rhs_of):
        rs_product(j, lhs_of(2 * chip), rhs_of, 1, r.keep)
        return rs_core(site, j, 1)

    def rs_other(site, j, lhs_of, rhs_of, between=None):
        rs_product(j, lhs_of(2 * (1 - chip)), rhs_of, 0, r.pass_on)
        c0 = rs_core(site, j, 0)
        c1 = between() if between else None
        c0.wait()
        r.rs_xs[j] = (r.pass_on[j] + r.rs_cr[j, 0].astype(F32)).astype(BF16)
        cx = rs_copy(site, j, 2, r.rs_xs.at[j], r.rs_xr.at[j], to_x)
        cx.start()
        return cx, c1

    def rs_start(site, j, lhs_of, rhs_of):
        return rs_other(site, j, lhs_of, rhs_of, lambda: rs_own(site, j, lhs_of, rhs_of))

    def rs_finish(j, copies):
        for cp in copies:
            cp.wait()
        return r.keep[j] + r.rs_cr[j, 1].astype(F32) + r.rs_xr[j].astype(F32)

    def share_rows(ref, share):
        lanes = pl.ds(pl.multiple_of(share * SHARE, SHARE), SHARE)
        return ref[:, :, lanes].reshape(T, SHARE).T

    def right_tile(ref, lanes):
        if len(ref.shape) == 3:
            return ref[:, :, lanes].reshape(T, lanes.size)
        return ref[:, lanes]

    def tiles(width):
        return width if width < 2 * TILE else TILE

    def part_tile(name, n, step):
        _, _, right, width = parts[name]
        lanes = pl.ds(pl.multiple_of(n * step, 128), step)
        from_lanes = pl.ds(pl.multiple_of(int(name[1]) * width + n * step, 128), step)
        return lanes, right_tile(right, from_lanes)

    def part_product(name, lhs, put):
        width = parts[name][3]
        step = tiles(width)

        def tile_body(n, carry):
            lanes, rhs = part_tile(name, n, step)
            put(lanes, mm(lhs, rhs, NN))
            return carry

        lax.fori_loop(0, width // step, tile_body, 0)

    def y_copy(name, i):
        p = parts[name][0]
        return pltpu.make_async_remote_copy(
            src_ref=getattr(r, "ys" + name).at[i], dst_ref=getattr(r, "yr" + name).at[i],
            send_sem=r.y_ss.at[p, i], recv_sem=r.y_rs.at[p, i], device_id=to_y, device_id_type=MESH,
        )

    def y_start(name):
        left = parts[name][1]
        out = getattr(r, "ys" + name)

        def pair_body(i, carry):
            lhs = jnp.concatenate(
                [share_rows(left, 4 * i + 1 - y), share_rows(left, 4 * i + 3 - y)], 0
            )

            def put(lanes, both):
                out[2 * i, :, lanes] = both[:SHARE].astype(BF16)
                out[2 * i + 1, :, lanes] = both[SHARE:].astype(BF16)

            part_product(name, lhs, put)
            y_copy(name, 2 * i).start()
            y_copy(name, 2 * i + 1).start()
            return carry

        lax.fori_loop(0, NZ // 2, pair_body, 0)

    def share_sum(name, target):
        got = getattr(r, "yr" + name)
        y_copy(name, target).wait_recv()

        def put(lanes, value):
            r.acc[0:SHARE, lanes] = value + got[target, :, lanes].astype(F32)

        part_product(name, share_rows(parts[name][1], 2 * target + y), put)

    def both_shares(name, target):
        def put(lanes, value):
            r.wide[:, lanes] = value

        left = parts[name][1]
        lanes = pl.ds(pl.multiple_of(2 * target * SHARE, 2 * SHARE), 2 * SHARE)
        part_product(name, left[:, :, lanes].reshape(T, 2 * SHARE).T, put)

    def z_copy(name, direction, step, device):
        p = parts[name][0]
        return pltpu.make_async_remote_copy(
            src_ref=getattr(r, "zs" + name).at[direction],
            dst_ref=getattr(r, "zr" + name).at[direction, step],
            send_sem=r.z_ss.at[p, direction, step], recv_sem=r.z_rs.at[p, direction, step],
            device_id=device, device_id_type=MESH,
        )

    def chain_step(name, step):
        out = getattr(r, "zs" + name)
        got = getattr(r, "zr" + name)
        width = parts[name][3]
        total = (r.wide if name in Z_FIRST else r.acc).at[:, 0:width]

        def one(direction, carry):
            place, following = line(direction)

            @pl.when(place <= step)
            def _():
                mirrored = NZ - 1 - step + place
                target = mirrored + direction * (NZ - 1 - 2 * mirrored)
                (both_shares if name in Z_FIRST else share_sum)(name, target)
                if step > 0:

                    @pl.when(place < step)
                    def _():
                        z_copy(name, direction, step - 1, following).wait_send()

                    @pl.when(place > 0)
                    def _():
                        z_copy(name, direction, step - 1, following).wait_recv()
                        total[...] += got[direction, step - 1].astype(F32)

                out[direction] = total[...].astype(BF16)
                z_copy(name, direction, step, following).start()

            return carry

        lax.fori_loop(0, 2, one, 0)

    def chain_end(name):
        got = getattr(r, "zr" + name)
        width = parts[name][3]
        total = (r.wide if name in Z_FIRST else r.acc).at[:, 0:width]
        (both_shares if name in Z_FIRST else share_sum)(name, z)

        def one(direction, carry):
            place, _ = line(direction)

            @pl.when(place > 0)
            def _():
                z_copy(name, direction, NZ - 2, (dp, m)).wait_recv()
                total[...] += got[direction, NZ - 2].astype(F32)

            return carry

        lax.fori_loop(0, 2, one, 0)

    def y_exchange(name):
        chain_end(name)
        width = parts[name][3]
        theirs = pl.ds(pl.multiple_of((1 - y) * SHARE, SHARE), SHARE)
        getattr(r, "ys" + name)[0] = r.wide[theirs, 0:width].astype(BF16)
        y_copy(name, 0).start()

    def a_src(name, share):
        ref = getattr(r, name[0] + "_full")
        at = pl.ds(pl.multiple_of(share * SHARE, SHARE), SHARE)
        if name[0] == "q":
            return ref.at[:, at, span(name)]
        return ref.at[at, span(name)] if name[0] == "u" else ref.at[span(name), at]

    def az_copy(name, side, direction, step, share, src, device):
        p = parts[name][0]
        return pltpu.make_async_remote_copy(
            src_ref=src, dst_ref=a_src(name, share), send_sem=r.az_ss.at[p, side, direction, step],
            recv_sem=r.az_rs.at[p, side, direction, step], device_id=device, device_id_type=MESH,
        )

    def ay_copy(name, place, src):
        p = parts[name][0]
        return pltpu.make_async_remote_copy(
            src_ref=src, dst_ref=a_src(name, 2 * place + y), send_sem=r.ay_ss.at[p, place],
            recv_sem=r.ay_rs.at[p, place], device_id=to_y, device_id_type=MESH,
        )

    local_out = []

    def finish_share(name):
        p, _, _, width = parts[name]
        matrix = name[0]
        at0 = span(name)
        if name in Z_FIRST:
            y_copy(name, 0).wait_recv()
            ours = pl.ds(pl.multiple_of(y * SHARE, SHARE), SHARE)
            r.acc[:, 0:width] = r.wide[ours, 0:width] + getattr(r, "yr" + name)[0].astype(F32)
        else:
            chain_end(name)
        for cp in state_in[name]:
            cp.wait()
        grad_out = getattr(r, "gr" + matrix)
        fresh = getattr(r, "nc" + matrix)

        def adam_block(cols, at, state, state_at):
            grad = r.acc[:, cols]
            if matrix in "do":
                grad = grad.T
            grad_out[at] = grad
            w, a, b = adam_step(
                grad,
                state[(0,) + state_at],
                state[(1,) + state_at],
                state[(2,) + state_at],
                decay_rate,
                token_total,
            )
            state[(0,) + state_at] = w
            state[(1,) + state_at] = a
            state[(2,) + state_at] = b
            fresh[at] = w.astype(BF16)

        if matrix == "q":
            for kind in range(3):
                adam_block(
                    slice(kind * PAIR, (kind + 1) * PAIR),
                    (kind, slice(None), at0),
                    r.big,
                    (slice(SHARE, 2 * SHARE), slice(kind * HW + at0.start, kind * HW + at0.stop)),
                )
        else:

            def adam_body(n, carry):
                cols = pl.ds(pl.multiple_of(n * SHARE, SHARE), SHARE)
                there = pl.ds(pl.multiple_of(at0.start + n * SHARE, SHARE), SHARE)
                if matrix == "u":
                    adam_block(cols, (slice(None), there), r.big, (slice(0, SHARE), there))
                else:
                    at = (there, slice(None))
                    adam_block(cols, at, getattr(r, "s" + matrix), at)
                return carry

            lax.fori_loop(0, width // SHARE, adam_body, 0)
        fresh = piece(fresh, name)
        if name in Y_FIRST:
            ay_copy(name, z, fresh).start()
        for direction in range(2):
            place, following = line(direction)

            @pl.when(place < NZ - 1)
            def _():
                az_copy(name, 0, direction, 0, 2 * z + y, fresh, following).start()

        if name not in Y_FIRST:
            ay_copy(name, z, fresh).start()
        local_out.append(local_copy(fresh, a_src(name, 2 * z + y), r.o_sem.at[p, 0]))
        local_out.append(
            local_copy(piece(grad_out, name), piece(getattr(r, matrix + "_grad"), name), r.o_sem.at[p, 1])
        )
        for k, (far, near) in enumerate(state_copies(name, True)):
            local_out.append(local_copy(near, far, r.o_sem.at[p, 2 + k]))

    def neighbour_share(name):
        part = a_src(name, 2 * z + 1 - y)
        ay_copy(name, z, part).wait_recv()
        for direction in range(2):
            place, following = line(direction)

            @pl.when(place < NZ - 1)
            def _():
                az_copy(name, 1, direction, 0, 2 * z + 1 - y, part, following).start()

    def gather_step(name, step):
        for side in range(2 if name in Y_FIRST else 1):
            for direction in range(2):
                place, following = line(direction)

                @pl.when(place >= step)
                def _():
                    source = z - step + 2 * step * direction
                    share = 2 * source + (1 - y if side else y)
                    part = a_src(name, share)
                    az_copy(name, side, direction, step - 1, share, part, following).wait_recv()
                    if step < NZ - 1:

                        @pl.when(place < NZ - 1)
                        def _():
                            az_copy(name, side, direction, step, share, part, following).start()

                    if name not in Y_FIRST:
                        ay_copy(name, source, part).start()

    def gather_end(name):
        part = a_src(name, 2 * z + y)

        def one(direction, carry):
            place, following = line(direction)

            @pl.when(place <= NZ - 2)
            def _():
                z_copy(name, direction, NZ - 2, following).wait_send()

            for step in range(NZ - 1):

                @pl.when((place >= step) & (place < NZ - 1))
                def _():
                    for side in range(2 if name in Y_FIRST else 1):
                        az_copy(name, side, direction, step, 2 * z + y, part, following).wait_send()

            return carry

        lax.fori_loop(0, 2, one, 0)
        if name in Z_FIRST:
            y_copy(name, 0).wait_send()
        if name in Y_FIRST:
            ay_copy(name, z, part).wait_send()

        def y_body(i, carry):
            if name not in Z_FIRST:
                y_copy(name, i).wait_send()
            if name not in Y_FIRST:
                there = a_src(name, 2 * i + y)
                ay_copy(name, i, there).wait_send()
                ay_copy(name, i, there).wait_recv()
            return carry

        lax.fori_loop(0, NZ, y_body, 0)

    def put_out(src, dst):
        cp = pltpu.make_async_copy(src, dst, r.stage_sem)
        cp.start()
        cp.wait()

    late = {}

    def turn(point):
        if not fast:
            return
        for kind, number in ORDER.get(point, ()):
            name = names_of[number] if number is not None else None
            if kind == V:
                late["vector_next"]()
            elif kind == Y:
                y_start(name)
            elif kind == F:
                finish_share(name)
            elif kind == E:
                y_exchange(name)
            elif kind == H:
                neighbour_share(name)
            elif kind in (C0, C1, C2):
                chain_step(name, kind - C0)
            else:
                gather_step(name, kind - G1 + 1)

    ag = {}
    for j in range(C):
        ag[j] = ag_send(0, j, r.g1)
    count_send(0)

    def w_copy(kind, src, block, device):
        return pltpu.make_async_remote_copy(
            src_ref=src, dst_ref=r.act.at[block], send_sem=r.ow_ss.at[kind],
            recv_sem=r.ow_rs.at[kind], device_id=device, device_id_type=MESH,
        )

    weights[0].wait()
    w_x = w_copy(0, r.wout, m, to_x)
    w_x.start()
    w_c = w_copy(1, r.wout, m, to_core)
    w_c.start()
    r.act[m] = r.wout[...]
    for w in qkv_weights:
        w.wait()

    def project(o):
        p = mm(r.g1[o], r.wqkv[...], NN)
        at = pl.ds(pl.multiple_of(o * R, R), R)
        for pair in range(PAIRS):
            rows = slice(pair * PAIR, (pair + 1) * PAIR)
            lanes = pl.ds(pl.multiple_of(m * HW + pair * PAIR, PAIR), PAIR)
            q, k, v = (p[:, qkv_lanes(pair, kind)] for kind in range(3))
            q = (q + r.vec[6:7, lanes]).astype(BF16)
            k = k.astype(BF16)
            v = (v + r.vec[7:8, lanes]).astype(BF16)
            for kind, value in enumerate((q, k, v)):
                r.qkv[at, qkv_lanes(pair, kind)] = value
            r.qT[rows, at] = q.T
            r.kT[rows, at] = k.T
            r.vT[rows, at] = v.T

    def make_dist(i, start):
        def one(b, carry):
            key = lax.broadcasted_iota(jnp.int32, (BQ, BQ), 0) + b * BQ
            query = lax.broadcasted_iota(jnp.int32, (BQ, BQ), 1) + i * BQ
            apart = query - key
            key_seg = r.segr[:, pl.ds(pl.multiple_of(b * BQ, BQ), BQ)]
            key_seg = jnp.broadcast_to(key_seg, (BQ, BQ)).T
            same = key_seg == r.segr[:, i * BQ : (i + 1) * BQ]
            r.big[b, :, start : start + BQ] = jnp.where((apart >= 0) & same, apart.astype(F32), jnp.inf)
            return carry

        lax.fori_loop(0, i + 1, one, 0)

    n_blocks = T // BQ
    project(m)
    for i in range(n_blocks):
        make_dist(i, i * BQ)
    count_next()
    for j in range(C):
        ag[j][1].wait()
    project(mc)
    for _ in range(1, dp_size.bit_length() - 1):
        count_next()
    fw = {}
    for j in range(C):
        ag[j][0].wait()
        fw[j] = ag_forward(0, j, r.g1)
    project(mx)
    for j in range(C):
        fw[j].wait()
    project(md)

    pair_row = lax.broadcasted_iota(jnp.int32, (2 * HD, BQ), 0) // HD
    pair_lane = lax.broadcasted_iota(jnp.int32, (BQ, 2 * HD), 1) // HD
    scale2 = log2_e / math.sqrt(HD)
    K_AT, V_AT, Q_AT, DIST = 0, HW, 2 * HW, 3 * HW

    def head_slope(h):
        head = jnp.zeros((1, BQ), jnp.int32) + (m * LOCAL_HEADS + h + 1)
        return jnp.exp2(head.astype(F32) * (-8.0 / HEADS)) * log2_e

    def pair_lanes(h, start):
        return pl.ds(pl.multiple_of(start + (h // 2) * PAIR, PAIR), PAIR)

    def kind_lanes(h, kind):
        return pl.ds(pl.multiple_of((h // 2) * 3 * PAIR + kind * PAIR, PAIR), PAIR)

    def head_scores(i, ke, h, start):
        mask = (pair_row == lax.rem(h, 2)).astype(F32).astype(BF16)
        q_cols = r.qT[pair_lanes(h, 0), i * BQ : (i + 1) * BQ] * mask
        raw = mm(r.qkv[0:ke, kind_lanes(h, 1)], q_cols, NN)
        return raw * scale2 - head_slope(h) * r.big[0 : i + 1, :, start : start + BQ].reshape(ke, BQ)

    OWN, PASSING = slice(0, HW), slice(HW, 2 * HW)

    def mix_copy(kind, j, src, dst, device):
        return pltpu.make_async_remote_copy(
            src_ref=src, dst_ref=dst, send_sem=r.mix_ss.at[kind, j], recv_sem=r.mix_rs.at[kind, j],
            device_id=device, device_id_type=MESH,
        )

    def send_mixture(i):
        for j in range(C):
            rows = slice(j * rc, (j + 1) * rc)
            src = r.mix.at[i * BQ + rows.start : i * BQ + rows.stop, :]

            @pl.when(i // 2 != chip)
            def _():
                kind = (core + i) % 2
                lanes = pl.ds(pl.multiple_of(kind * HW, HW), HW)
                mix_copy(kind, j, src, r.gup.at[m, rows, lanes], to_x).start()

            @pl.when(mc == i)
            def _():
                mix_copy(2, j, src, r.gup.at[m, rows, OWN], to_core).start()

            @pl.when(m == i)
            def _():
                r.gup[m, rows, OWN] = src[...]

    for turn_of, i in enumerate([*range(n_blocks - 2), n_blocks - 1, n_blocks - 2]):
        ke = (i + 1) * BQ
        block = slice(i * BQ, (i + 1) * BQ)

        def head_body(h, carry):
            s = head_scores(i, ke, h, i * BQ)
            top = jnp.max(s, 0, keepdims=True)
            e = jnp.exp2(s - top)
            total = jnp.sum(e, 0, keepdims=True)
            p = (e * (1.0 / total)).astype(BF16)
            r.lse[h, :, block] = top + jnp.log2(total)
            at = pl.ds(pl.multiple_of(h * HD, HD), HD)
            r.mixT[at, :] = mm(r.vT[at, 0:ke], p, NN).astype(BF16)
            return carry

        lax.fori_loop(0, LOCAL_HEADS, head_body, 0, unroll=True)
        r.mix[block, :] = r.mixT[...].T
        send_mixture(i)
        if turn_of >= n_blocks - (mp_size.bit_length() - 1):
            count_next()

    def pair_rows(ref, j):
        def of(first):
            v = ref[pl.ds(first, 2), pl.ds(j * rc, rc), :]
            return v.reshape(2 * rc, v.shape[2])

        return of

    def pair_flat(ref, j):
        def of(first):
            a = ref[pl.ds(pl.multiple_of(first * R + j * rc, rc), rc), :]
            b = ref[pl.ds(pl.multiple_of(first * R + R + j * rc, rc), rc), :]
            return jnp.concatenate([a, b], 0)

        return of

    def ag_finish(site, j, ref):
        ag[j][0].wait()
        cf = ag_forward(site, j, ref)
        ag[j][1].wait()
        cf.wait()

    w_x.wait()
    w_f = w_copy(2, r.act.at[mx], mx, to_core)
    w_f.start()
    m_f = {}
    for j in range(C):
        rows = slice(j * rc, (j + 1) * rc)
        here = r.gup.at[m, rows, OWN]
        mix_copy(1, j, here, here, to_x).wait_recv()
        m_f[j] = mix_copy(3, j, r.gup.at[mx, rows, PASSING], r.gup.at[mx, rows, OWN], to_core)
        m_f[j].start()
    w_c.wait()
    w_f.wait()
    rs = {}
    for j in range(C):
        rows = slice(j * rc, (j + 1) * rc)
        here = r.gup.at[m, rows, OWN]
        mix_copy(0, j, here, here, to_x).wait()
        mix_copy(1, j, here, here, to_x).wait_send()
        mix_copy(2, j, here, here, to_core).wait()
        m_f[j].wait()

        def out_body(n, carry):
            lanes = pl.ds(pl.multiple_of(n * TILE, TILE), TILE)
            total = mm(r.gup[0, rows, OWN], r.act[0, :, lanes], NN)
            for q in range(1, mp_size):
                total += mm(r.gup[q, rows, OWN], r.act[q, :, lanes], NN)
            r.keep[j, :, lanes] = total
            return carry

        lax.fori_loop(0, D // TILE, out_body, 0)
        hid = r.x[rows, :].astype(F32) + r.keep[j] + r.vec[2:3, :]
        r.hidden[rows, :] = hid
        normed, inverse = norm_rows(hid)
        r.n2[rows, :] = normed
        r.inv2[rows, :] = inverse
        ag[j] = ag_start(1, j, r.g2, (normed * r.vec[3:4, :] + r.vec[4:5, :]).astype(BF16))

    weights[1].wait()
    weights[2].wait()
    def up_half(j, first):
        pair = pl.ds(first, 2)
        rows = pair_rows(r.g2, j)(first)

        def up_body(n, carry):
            lanes = pl.ds(pl.multiple_of(n * TILE, TILE), TILE)
            u = mm(rows, r.wup[:, lanes], NN) + r.vec[pl.ds(8 + m, 1), lanes]
            a, b = gelu_both(u)
            r.act[pair, pl.ds(j * rc, rc), lanes] = a.astype(BF16).reshape(2, rc, TILE)
            r.big[pair, pl.ds(j * rc, rc), lanes] = b.reshape(2, rc, TILE)
            return carry

        lax.fori_loop(0, FU // TILE, up_body, 0)

    def by_halves(site, gather, ref, half, left, rhs_of):
        own = {}
        for j in range(C):
            ag[j][1].wait()
            half(j, 2 * chip)
            own[j] = rs_own(site, j, pair_rows(left, j), rhs_of)
        for j in range(C):
            ag[j][0].wait()
            ag_forward(gather, j, ref).wait()
            if site == 2 and j == C - 1:
                turn(THIRD)
            half(j, 2 * (1 - chip))
            cx, _ = rs_other(site, j, pair_rows(left, j), rhs_of)
            rs[j] = (cx, own[j])

    by_halves(1, 1, r.g2, up_half, r.act, lambda lanes: (r.wdown[:, lanes], NN))

    t_in.wait()
    loss_scale = token_total / r.cnt[len(bits), 0:1, 0:1]
    for j in range(C):
        rows = slice(j * rc, (j + 1) * rc)
        out = r.hidden[rows, :] + rs_finish(j, rs[j]) + r.vec[5:6, :]
        r.bo[rows, :] = out.astype(BF16)
        valid = jnp.broadcast_to(r.valid[:, rows].astype(F32), (SHARE, rc)).T[:, 0:1]
        grad = valid * (out - r.t[rows, :].astype(F32)) * loss_scale
        r.ig[rows, :] = grad
        ag[j] = ag_start(2, j, r.g3, grad.astype(BF16))
        r.vg[5:6, :] += jnp.sum(grad, 0, keepdims=True)
    bo_out = local_copy(r.bo, r.bo_hbm, r.in_sem.at[3])

    def act_half(j, first):
        pair = pl.ds(first, 2)
        rows = pair_rows(r.g3, j)(first)

        def act_body(n, carry):
            lanes = pl.ds(pl.multiple_of(n * TILE, TILE), TILE)
            ga = mm(rows, r.wdown[lanes, :], NT)
            gu = ga * r.big[pair, pl.ds(j * rc, rc), lanes].reshape(2 * rc, TILE)
            r.gup[pair, pl.ds(j * rc, rc), lanes] = gu.astype(BF16).reshape(2, rc, TILE)
            return carry

        lax.fori_loop(0, FU // TILE, act_body, 0)

    by_halves(2, 2, r.g3, act_half, r.gup, lambda lanes: (r.wup[lanes, :], NT))

    def whole_grad(left, right, width, dst):
        def body(n, carry):
            lanes = pl.ds(pl.multiple_of(n * TILE, TILE), TILE)
            r.stage[:, 0:width] = mm(right_tile(left, lanes), right[...].reshape(T, width), TN)
            put_out(r.stage.at[:, 0:width], dst.at[lanes, :])
            return carry

        lax.fori_loop(0, dst.shape[0] // TILE, body, 0)

    if not fast:
        whole_grad(r.act, r.g3, D, r.d_grad)

    for j in range(C):
        rows = slice(j * rc, (j + 1) * rc)
        gs = rs_finish(j, rs[j])
        gh = r.ig[rows, :] + norm_backward(gs, r.n2[rows, :], r.inv2[rows, :], r.vec[3:4, :])
        r.hidden[rows, :] = gh
        ag[j] = ag_start(3, j, r.g4, gh.astype(BF16))
        r.vg[2:3, :] += jnp.sum(gh, 0, keepdims=True)
        r.vg[3:4, :] += jnp.sum(gs * r.n2[rows, :], 0, keepdims=True)
        r.vg[4:5, :] += jnp.sum(gs, 0, keepdims=True)

    turn(NORM)
    if not fast:
        whole_grad(r.g2, r.gup, FU, r.u_grad)
    r.vg[pl.ds(8 + m, 1), :] = jnp.sum(r.gup[...].reshape(T, FU).astype(F32), 0, keepdims=True)

    for j in range(C):
        ag_finish(3, j, r.g4)

    def gm_body(o, carry):
        at = pl.ds(pl.multiple_of(o * R, R), R)
        gmx = mm(r.g4[o], r.wout[...], NT).astype(BF16)
        r.gm[at, :] = gmx
        r.vT[:, at] = gmx.T
        return carry

    lax.fori_loop(0, mp_size, gm_body, 0)
    turn(FOURTH)

    r.big[:, :, K_AT : K_AT + HW] = jnp.zeros((mp_size, R, HW), F32)
    r.big[:, :, V_AT : V_AT + HW] = jnp.zeros((mp_size, R, HW), F32)
    for pair in range(PAIRS):
        for i in range(n_blocks):
            ke = (i + 1) * BQ
            block = slice(i * BQ, (i + 1) * BQ)
            make_dist(i, DIST)

            def back_body(half, carry):
                h = 2 * pair + half
                row_mask = (pair_row == half).astype(F32).astype(BF16)
                lane_mask = (pair_lane == half).astype(F32).astype(BF16)
                lanes = slice(pair * PAIR, (pair + 1) * PAIR)
                p = jnp.exp2(head_scores(i, ke, h, DIST) - r.lse[h, :, block])
                gp = mm(r.qkv[0:ke, qkv_lanes(pair, 2)], r.vT[lanes, block] * row_mask, NN)
                inner = jnp.sum(p * gp, 0, keepdims=True)
                raw = (p * (gp - inner)).astype(BF16)
                low = p.astype(BF16)
                r.big[0 : i + 1, :, V_AT + lanes.start : V_AT + lanes.stop] += mm(
                    low, r.gm[block, lanes] * lane_mask, NN
                ).reshape(i + 1, BQ, PAIR)
                r.big[0 : i + 1, :, K_AT + lanes.start : K_AT + lanes.stop] += mm(
                    raw, r.qkv[block, qkv_lanes(pair, 0)] * lane_mask, NN
                ).reshape(i + 1, BQ, PAIR)
                at = pl.ds(pl.multiple_of(h * HD, HD), HD)
                r.big[i, at, Q_AT : Q_AT + BQ] = mm(r.kT[at, 0:ke], raw, NN) * (1.0 / math.sqrt(HD))
                return carry

            lax.fori_loop(0, 2, back_body, 0)
            rows = slice(pair * PAIR, (pair + 1) * PAIR)
            r.st[block, qkv_lanes(pair, 0)] = r.big[i, rows, Q_AT : Q_AT + BQ].T.astype(BF16)
            turn((pair, i))
        lanes = slice(pair * PAIR, (pair + 1) * PAIR)
        r.st[:, qkv_lanes(pair, 1)] = (
            r.big[:, :, K_AT + lanes.start : K_AT + lanes.stop].reshape(T, PAIR) * (1.0 / math.sqrt(HD))
        ).astype(BF16)
        r.st[:, qkv_lanes(pair, 2)] = (
            r.big[:, :, V_AT + lanes.start : V_AT + lanes.stop].reshape(T, PAIR).astype(BF16)
        )
        turn((pair,))
    for pair in range(PAIRS):
        lanes = pl.ds(pl.multiple_of(m * HW + pair * PAIR, PAIR), PAIR)
        for row, kind in ((6, 0), (7, 2)):
            r.vg[row : row + 1, lanes] = jnp.sum(
                r.st[:, qkv_lanes(pair, kind)].astype(F32), 0, keepdims=True
            )

    if fast:
        fetch_state("u")
        fetch_state("q")

    for j in range(C):
        rs[j] = rs_start(3, j, pair_flat(r.st, j), lambda lanes: (r.wqkv[lanes, :], NT))

    turn(BACK)
    if not fast:
        whole_grad(r.mix, r.g4, D, r.o_grad)
        whole_grad(r.g1, r.st, 3 * HW, r.q_grad)

    for j in range(C):
        rows = slice(j * rc, (j + 1) * rc)
        gf = rs_finish(j, rs[j])
        normed, inverse = norm_rows(r.x[rows, :].astype(F32))
        r.ig[rows, :] = r.hidden[rows, :] + norm_backward(gf, normed, inverse, r.vec[0:1, :])
        r.vg[0:1, :] += jnp.sum(gf * normed, 0, keepdims=True)
        r.vg[1:2, :] += jnp.sum(gf, 0, keepdims=True)
    ig_out = local_copy(r.ig, r.ig_hbm, r.in_sem.at[4])

    vector_send, vector_step = doubling(mp_bits + dp_bits, r.vs, r.vs_r, r.vs_ss, r.vs_rs)
    r.vs[0] = r.vg[...]
    vector_send(0)
    vector_out = []

    def vector_next():
        vector_step()
        late["steps"] = late.get("steps", 0) + 1
        if late["steps"] < len(bits):
            return
        vec_in.wait()
        total = r.vs[len(bits), 0 : r.vec.shape[0]]
        new = adam_step(total, r.vec_state[0], r.vec_state[1], r.vec_state[2], 0.0, token_total)
        r.v_sum[...] = total
        for k in range(3):
            r.vec_state[k] = new[k]
        r.v_copy[...] = new[0].astype(BF16)
        for k, (near, far) in enumerate(
            [(r.v_sum, r.v_grad), (r.vec_state, r.v_new), (r.v_copy, r.v_low)]
        ):
            vector_out.append(local_copy(near, far, r.in_sem.at[5 + k]))

    late["vector_next"] = vector_next
    if fast:
        turn(END)
        for name in parts:
            gather_end(name)
        for cp in local_out:
            cp.wait()
    else:
        for _ in bits:
            vector_next()
    for cp in [bo_out, ig_out] + vector_out:
        cp.wait()


Z_FIRST = ("d0",)
Y_FIRST = ("u1",)
Y, C0, C1, C2, E, F, H, G1, G2, G3, V = range(11)
D0, D1, U0, U1, O0, Q0, Q1 = range(7)
THIRD, NORM, FOURTH, BACK, END = range(5)
ORDER = {
    THIRD: ((Y, D1), (C0, D0),),
    NORM: ((C0, D1), (Y, U0), (C1, D0), (Y, U1), (C1, D1), (C2, D0),),
    FOURTH: ((C0, U0),),
    (0, 1): ((C2, D1),),
    (0, 2): ((E, D0),),
    (0,): ((Y, Q0),),
    (1, 0): ((C0, U1),),
    (1, 1): ((C1, U0),),
    (1, 2): ((C1, U1), (F, D1), (Y, O0),),
    (1, 3): ((F, D0), (C0, Q0), (C2, U1),),
    BACK: (
        (G1, D0), (Y, Q1), (C1, Q0), (G1, D1), (C2, U0), (C0, O0), (F, U1), (C2, Q0), (G2, D1),
    ),
    END: (
        (F, U0), (C1, O0), (C0, Q1), (G3, D1), (G2, D0), (F, Q0), (C2, O0), (V, None), (C1, Q1), (G1, U0),
        (H, U1), (V, None), (G1, Q0), (F, O0), (C2, Q1), (G2, U0), (G1, O0), (F, Q1), (G2, O0), (G2, Q0),
        (G3, Q0), (V, None), (G1, Q1), (G2, Q1), (G1, U1), (G3, U0), (V, None), (G3, Q1), (G2, U1), (G3, D0),
        (V, None), (G3, O0), (G3, U1),
    ),
}


def pieces(head_width, units):
    return [
        ("d0", units // 2),
        ("d1", units // 2),
        ("u0", units // 2),
        ("u1", units // 2),
        ("o0", head_width),
    ] + [("q%d" % pair, 6 * HD) for pair in range(head_width // (2 * HD))]


SHARE = 128


def block_call(sizes, x, teacher, segments, valid, vectors, copies, states):
    dp_size, mp_size = sizes
    R, D = x.shape
    T = mp_size * R
    wqkv, wout, wup, wdown = copies
    HW = wout.shape[0]
    FU = wup.shape[1]
    C = CHUNKS
    rc = R // C
    n_bits = (dp_size * mp_size).bit_length() - 1
    NZ = dp_size // 2
    PAIRS = HW // (2 * HD)
    fast = D == dp_size * SHARE
    dma = pltpu.SemaphoreType.DMA
    M = pltpu.VMEM
    S = jax.ShapeDtypeStruct
    vmem = pl.BlockSpec(memory_space=pltpu.VMEM)
    anywhere = pl.BlockSpec(memory_space=pl.ANY)

    ins = {
        "x_hbm": (x, anywhere),
        "t_hbm": (teacher, anywhere),
        "segr": (segments, vmem),
        "valid": (valid.reshape(1, R), vmem),
        "vec_low": (vectors, vmem),
        "vec_state_hbm": (states[4], anywhere),
        "wqkv_hbm": (wqkv, anywhere),
        "wout_hbm": (wout, anywhere),
        "wup_hbm": (wup, anywhere),
        "wdown_hbm": (wdown, anywhere),
    }
    outs = {
        "bo_hbm": (S((R, D), BF16), anywhere),
        "ig_hbm": (S((R, D), F32), anywhere),
        "v_grad": (S(vectors.shape, F32), anywhere),
        "v_new": (S(states[4].shape, F32), anywhere),
        "v_low": (S(vectors.shape, BF16), anywhere),
    }
    if fast:
        shard = {"q": (3, SHARE, HW), "o": (HW, SHARE), "u": (SHARE, FU), "d": (FU, SHARE)}
        whole = {"q": (3, D, HW), "o": (HW, D), "u": (D, FU), "d": (FU, D)}
        for name, state in zip("qoud", states):
            ins["s%s_hbm" % name] = (state, anywhere)
        for name in "qoud":
            outs[name + "_grad"] = (S(shard[name], F32), anywhere)
        for name in "qoud":
            outs[name + "_new"] = (S((3,) + shard[name], F32), anywhere)
        for name in "qoud":
            outs[name + "_full"] = (S(whole[name], BF16), anywhere)
    else:
        outs["q_grad"] = (S((D, 3 * HW), F32), anywhere)
        outs["o_grad"] = (S((HW, D), F32), anywhere)
        outs["u_grad"] = (S((D, FU), F32), anywhere)
        outs["d_grad"] = (S((FU, D), F32), anywhere)
    scratch = {
        "wqkv": M((D, 3 * HW), BF16),
        "wout": M((HW, D), BF16),
        "wup": M((D, FU), BF16),
        "wdown": M((FU, D), BF16),
        "w_sem": dma((3,)),
        "ow_ss": dma((3,)),
        "ow_rs": dma((3,)),
        "mix_ss": dma((4, C)),
        "mix_rs": dma((4, C)),
        "in_sem": dma((8,)),
        "x": M((R, D), BF16),
        "t": M((R, D), BF16),
        "bo": M((R, D), BF16),
        "ig": M((R, D), F32),
        "vec_state": M(states[4].shape, F32),
        "v_sum": M(vectors.shape, F32),
        "v_copy": M(vectors.shape, BF16),
        "wq_sem": dma((PAIRS, 3)),
        "vec": M(vectors.shape, F32),
        "g1": M((mp_size, R, D), BF16),
        "g2": M((mp_size, R, D), BF16),
        "g3": M((mp_size, R, D), BF16),
        "g4": M((mp_size, R, D), BF16),
        "qkv": M((T, 3 * HW), BF16),
        "qT": M((HW, T), BF16),
        "kT": M((HW, T), BF16),
        "vT": M((HW, T), BF16),
        "mixT": M((HW, BQ), BF16),
        "mix": M((T, HW), BF16),
        "lse": M((HW // HD, 1, T), F32),
        "hidden": M((R, D), F32),
        "n2": M((R, D), F32),
        "inv2": M((R, 1), F32),
        "act": M((mp_size, R, FU), BF16),
        "big": M((mp_size, R, FU), F32),
        "gup": M((mp_size, R, FU), BF16),
        "gm": M((T, HW), BF16),
        "st": M((T, 3 * HW), BF16),
        "pass_on": M((C, rc, D), F32),
        "keep": M((C, rc, D), F32),
        "rs_cs": M((C, 2, rc, D), BF16),
        "rs_cr": M((C, 2, rc, D), BF16),
        "rs_xs": M((C, rc, D), BF16),
        "rs_xr": M((C, rc, D), BF16),
        "cnt": M((n_bits + 1, 8, 128), F32),
        "cnt_r": M((n_bits, 8, 128), F32),
        "vg": M((16, D), F32),
        "vs": M((n_bits + 1, 16, D), F32),
        "vs_r": M((n_bits, 16, D), F32),
        "ag_ss": dma((4, C, 3)),
        "ag_rs": dma((4, C, 3)),
        "rs_ss": dma((4, C, 3)),
        "rs_rs": dma((4, C, 3)),
        "cnt_ss": dma((n_bits,)),
        "cnt_rs": dma((n_bits,)),
        "vs_ss": dma((n_bits,)),
        "vs_rs": dma((n_bits,)),
    }
    if fast:
        for name, w in pieces(HW, FU):
            shares = 1 if name in Z_FIRST else NZ
            rows = 2 * SHARE if name in Z_FIRST else SHARE
            scratch["ys" + name] = M((shares, SHARE, w), BF16)
            scratch["yr" + name] = M((shares, SHARE, w), BF16)
            scratch["zs" + name] = M((2, rows, w), BF16)
            scratch["zr" + name] = M((2, NZ - 1, rows, w), BF16)
        for name in "qoud":
            scratch["gr" + name] = M(shard[name], F32)
            scratch["nc" + name] = M(shard[name], BF16)
        scratch["sd"] = M((3,) + shard["d"], F32)
        scratch["so"] = M((3,) + shard["o"], F32)
        scratch["acc"] = M((SHARE, FU // 2), F32)
        scratch["wide"] = M((2 * SHARE, FU // 2), F32)
        n = len(pieces(HW, FU))
        scratch["s_sem"] = dma((n, 3))
        scratch["o_sem"] = dma((n, 5))
        scratch["y_ss"] = dma((n, NZ))
        scratch["y_rs"] = dma((n, NZ))
        scratch["z_ss"] = dma((n, 2, NZ - 1))
        scratch["z_rs"] = dma((n, 2, NZ - 1))
        scratch["az_ss"] = dma((n, 2, 2, NZ - 1))
        scratch["az_rs"] = dma((n, 2, 2, NZ - 1))
        scratch["ay_ss"] = dma((n, NZ))
        scratch["ay_rs"] = dma((n, NZ))
    else:
        scratch["stage"] = M((TILE, D), F32)
        scratch["stage_sem"] = dma
    names = list(ins) + list(outs) + list(scratch)
    results = pl.pallas_call(
        functools.partial(block_kernel, sizes, fast, names),
        out_shape=[v[0] for v in outs.values()],
        in_specs=[v[1] for v in ins.values()],
        out_specs=[v[1] for v in outs.values()],
        scratch_shapes=list(scratch.values()),
        compiler_params=pltpu.CompilerParams(
            collective_id=0, has_side_effects=True, vmem_limit_bytes=62 << 20
        ),
        name="block",
    )(*[v[0] for v in ins.values()])
    outs = dict(zip(outs, results))
    if fast:
        names, results = list(outs), list(outs.values())
        outs = dict(zip(names, settle(results)))
    return outs, fast


def settle_kernel(count, *refs):
    sources, results, held = refs[:count], refs[count : 2 * count], refs[2 * count : 3 * count]
    in_sem, out_sem = refs[3 * count :]
    loads = [pltpu.make_async_copy(sources[i], held[i], in_sem.at[i]) for i in range(count)]
    stores = [pltpu.make_async_copy(held[i], results[i], out_sem.at[i]) for i in range(count)]
    for cp in loads:
        cp.start()
    for load, store in zip(loads, stores):
        load.wait()
        store.start()
    for cp in stores:
        cp.wait()


def settle(arrays):
    anywhere = pl.BlockSpec(memory_space=pltpu.HBM)
    dma = pltpu.SemaphoreType.DMA((len(arrays),))
    return pl.pallas_call(
        functools.partial(settle_kernel, len(arrays)),
        out_shape=[jax.ShapeDtypeStruct(a.shape, a.dtype) for a in arrays],
        in_specs=[anywhere] * len(arrays),
        out_specs=[anywhere] * len(arrays),
        scratch_shapes=[pltpu.VMEM(a.shape, a.dtype) for a in arrays] + [dma, dma],
        compiler_params=pltpu.CompilerParams(vmem_limit_bytes=62 << 20),
        name="settle",
    )(*arrays)


def adam_update(gradient, stored, decay_factor, token_total):
    new = adam_step(gradient, stored[0], stored[1], stored[2], decay_factor, token_total)
    return (jnp.stack(new), new[0].astype(jnp.bfloat16))


def shards(
    inputs,
    teacher,
    segments,
    valid_mask,
    qkv_copy,
    out_copy,
    up_copy,
    down_copy,
    vector_copy,
    qkv_state,
    out_state,
    up_state,
    down_state,
    vector_state,
):
    sizes = (lax.axis_size("dp"), lax.axis_size("mp"))
    token_total = inputs.shape[0] * sizes[0] * sizes[1]
    width = inputs.shape[1]
    head_width = qkv_copy.shape[2]
    pairs = head_width // (2 * HD)
    outs, fast = block_call(
        sizes,
        inputs,
        teacher,
        segments,
        valid_mask,
        vector_copy,
        (qkv_copy.transpose(1, 0, 2), out_copy, up_copy, down_copy),
        (qkv_state.transpose(0, 2, 1, 3), out_state, up_state, down_state, vector_state),
    )
    vector_grad, vector_new, vector_low = outs["v_grad"], outs["v_new"], outs["v_low"]
    if fast:
        qkv_grad = outs["q_grad"].transpose(1, 0, 2)
        out_grad, up_grad, down_grad = (outs[n + "_grad"] for n in "oud")
        qkv_new = outs["q_new"].transpose(0, 2, 1, 3)
        out_new, up_new, down_new = (outs[n + "_new"] for n in "oud")
        qkv_full = outs["q_full"].transpose(1, 0, 2)
        out_full, up_full, down_full = (outs[n + "_full"] for n in "oud")
    else:
        qkv_local = outs["q_grad"].reshape(width, pairs, 3, 2 * HD)
        qkv_local = qkv_local.transpose(0, 2, 1, 3).reshape(width, 3, head_width)
        qkv_grad, out_grad, up_grad, down_grad = (
            lax.psum_scatter(qkv_local, "dp", scatter_dimension=0, tiled=True),
            lax.psum_scatter(outs["o_grad"], "dp", scatter_dimension=1, tiled=True),
            lax.psum_scatter(outs["u_grad"], "dp", scatter_dimension=0, tiled=True),
            lax.psum_scatter(outs["d_grad"], "dp", scatter_dimension=1, tiled=True),
        )
        qkv_new, qkv_low = adam_update(qkv_grad, qkv_state, decay_rate, token_total)
        out_new, out_low = adam_update(out_grad, out_state, decay_rate, token_total)
        up_new, up_low = adam_update(up_grad, up_state, decay_rate, token_total)
        down_new, down_low = adam_update(down_grad, down_state, decay_rate, token_total)
        qkv_full, out_full, up_full, down_full = (
            lax.all_gather(qkv_low, "dp", axis=0, tiled=True),
            lax.all_gather(out_low, "dp", axis=1, tiled=True),
            lax.all_gather(up_low, "dp", axis=0, tiled=True),
            lax.all_gather(down_low, "dp", axis=1, tiled=True),
        )
    return (
        outs["bo_hbm"],
        outs["ig_hbm"],
        qkv_grad,
        out_grad,
        up_grad,
        down_grad,
        vector_grad,
        qkv_new,
        out_new,
        up_new,
        down_new,
        vector_new,
        qkv_full,
        out_full,
        up_full,
        down_full,
        vector_low,
    )


def solution(mesh):
    in_specs = (
        P(("dp", "mp"), None),
        P(("dp", "mp"), None),
        P("dp", None),
        P(("dp", "mp")),
        P(None, None, "mp"),
        P("mp", None),
        P(None, "mp"),
        P("mp", None),
        P(),
        P(None, "dp", None, "mp"),
        P(None, "mp", "dp"),
        P(None, "dp", "mp"),
        P(None, "mp", "dp"),
        P(),
    )
    out_specs = (
        P(("dp", "mp"), None),
        P(("dp", "mp"), None),
        P("dp", None, "mp"),
        P("mp", "dp"),
        P("dp", "mp"),
        P("mp", "dp"),
        P(),
        P(None, "dp", None, "mp"),
        P(None, "mp", "dp"),
        P(None, "dp", "mp"),
        P(None, "mp", "dp"),
        P(),
        P(None, None, "mp"),
        P("mp", None),
        P(None, "mp"),
        P("mp", None),
        P(),
    )
    return jax.shard_map(shards, mesh=mesh, in_specs=in_specs, out_specs=out_specs, check_vma=False)
```

```python
import functools
import math
import types

import jax
import jax.numpy as jnp
from jax import lax
from jax.experimental import pallas as pl
from jax.experimental.pallas import tpu as pltpu
from jax.sharding import PartitionSpec as P

HEADS = 16
HD = 64

norm_eps = 1e-05
beta_one = 0.9
beta_two = 0.95
adam_eps = 1e-08
learn_rate = 0.001
decay_rate = 0.1
correction_one = 1.0 - (0.9**10) ** 10
correction_two = 1.0 - (0.95**10) ** 10
log2_e = 1.4426950408889634

CHUNKS = 2
BQ = 256
TILE = 256
MESH = pl.DeviceIdType.MESH
F32 = jnp.float32
BF16 = jnp.bfloat16
NN = ((1,), (0,))
NT = ((1,), (1,))
TN = ((0,), (0,))


def mm(a, b, dims):
    return lax.dot_general(a, b, (dims, ((), ())), preferred_element_type=F32)


def gelu_both(v):
    c = 0.7978845608
    v2 = v * v
    th = jnp.tanh(c * (v + 0.044715 * v2 * v))
    half = 0.5 * (1.0 + th)
    back = half + 0.5 * v * (1.0 - th * th) * (c * (1.0 + 3.0 * 0.044715 * v2))
    return v * half, back


def norm_rows(v):
    centred = v - jnp.mean(v, -1, keepdims=True)
    inverse = lax.rsqrt(jnp.mean(centred * centred, -1, keepdims=True) + norm_eps)
    return centred * inverse, inverse


def norm_backward(grad_out, normed, inverse, gain_row):
    scaled = grad_out * gain_row
    return inverse * (
        scaled
        - jnp.mean(scaled, -1, keepdims=True)
        - normed * jnp.mean(scaled * normed, -1, keepdims=True)
    )


def adam_step(gradient, weight, first, second, decay_factor, token_total):
    mean_grad = gradient / token_total
    moment_one = beta_one * first + (1.0 - beta_one) * mean_grad
    moment_two = beta_two * second + (1.0 - beta_two) * mean_grad * mean_grad
    update = (
        moment_one / correction_one / (jnp.sqrt(moment_two / correction_two) + adam_eps)
        + decay_factor * weight
    )
    return weight - learn_rate * update, moment_one, moment_two


def block_kernel(sizes, fast, names, *refs):
    r = types.SimpleNamespace(**dict(zip(names, refs)))
    dp_size, mp_size = sizes
    dp = lax.axis_index("dp")
    m = lax.axis_index("mp")
    core = lax.rem(m, 2)
    chip = m // 2
    mc = m + 1 - 2 * core
    mx = lax.rem(m + 2, 4)
    md = mc + mx - m
    C = CHUNKS
    R, D = r.x.shape
    rc = R // C
    T = mp_size * R
    HW = r.wout.shape[0]
    FU = r.wup.shape[1]
    LOCAL_HEADS = HW // HD
    PAIR = 2 * HD
    PAIRS = HW // PAIR
    token_total = float(dp_size * T)

    dp_bits = [("dp", b) for b in range(dp_size.bit_length() - 1)]
    mp_bits = [("mp", b) for b in range(mp_size.bit_length() - 1)]
    bits = dp_bits + mp_bits

    def flip(v, b):
        w = 1 << b
        return v + w - 2 * w * lax.rem(v // w, 2)

    def bit_partner(item):
        axis, b = item
        if axis == "mp":
            return (dp, flip(m, b))
        return (flip(dp, b), m)

    to_core = (dp, mc)
    to_x = (dp, mx)

    NZ = dp_size // 2
    z = dp // 2
    y = lax.rem(dp, 2)
    to_y = (dp + 1 - 2 * y, m)

    def line(direction):
        place = z + direction * (NZ - 1 - 2 * z)
        return place, (dp + 2 - 4 * direction, m)

    def local_copy(src, dst, sem):
        cp = pltpu.make_async_copy(src, dst, sem)
        cp.start()
        return cp

    def qkv_lanes(pair, kind):
        return slice((3 * pair + kind) * PAIR, (3 * pair + kind + 1) * PAIR)

    x_in = local_copy(r.x_hbm, r.x, r.in_sem.at[0])
    t_in = local_copy(r.t_hbm, r.t, r.in_sem.at[1])
    qkv_weights = [
        local_copy(
            r.wqkv_hbm.at[kind, :, pair * PAIR : (pair + 1) * PAIR],
            r.wqkv.at[:, qkv_lanes(pair, kind)],
            r.wq_sem.at[pair, kind],
        )
        for pair in range(PAIRS)
        for kind in range(3)
    ]
    weights = [
        local_copy(src, dst, r.w_sem.at[i])
        for i, (src, dst) in enumerate(
            [(r.wout_hbm, r.wout), (r.wup_hbm, r.wup), (r.wdown_hbm, r.wdown)]
        )
    ]
    if fast:
        parts = {}
        for name, width in pieces(HW, FU):
            left, right = {
                "d": (r.g3, r.act),
                "u": (r.g2, r.gup),
                "o": (r.g4, r.mix),
                "q": (r.g1, r.st),
            }[name[0]]
            parts[name] = (len(parts), left, right, width)
        names_of = list(parts)
        state_in = {}

        def span(name):
            width = PAIR if name[0] == "q" else parts[name][3]
            return slice(int(name[1]) * width, (int(name[1]) + 1) * width)

        def piece(ref, name):
            at = span(name)
            if name[0] == "q":
                return ref.at[:, :, at]
            return ref.at[:, at] if name[0] == "u" else ref.at[at, :]

        def state_copies(name, out):
            far = getattr(r, name[0] + "_new") if out else getattr(r, "s%s_hbm" % name[0])
            at = span(name)
            if name[0] == "q":
                return [
                    (
                        far.at[:, kind, :, at],
                        r.big.at[0:3, SHARE : 2 * SHARE, kind * HW + at.start : kind * HW + at.stop],
                    )
                    for kind in range(3)
                ]
            if name[0] == "u":
                return [(far.at[:, :, at], r.big.at[0:3, 0:SHARE, at])]
            return [(far.at[:, at, :], getattr(r, "s" + name[0]).at[:, at, :])]

        def state_sem(name, k):
            p = parts[name][0]
            return r.s_sem.at[p + 2 * max(0, p - 5) + k]

        def fetch_state(matrix):
            for name in parts:
                if name[0] == matrix:
                    state_in[name] = [
                        local_copy(far, near, state_sem(name, k))
                        for k, (far, near) in enumerate(state_copies(name, False))
                    ]

        fetch_state("d")
        fetch_state("o")

    vec_in = local_copy(r.vec_state_hbm, r.vec_state, r.in_sem.at[2])
    barrier = pltpu.get_barrier_semaphore()
    for item in bits:
        pl.semaphore_signal(barrier, inc=1, device_id=bit_partner(item), device_id_type=MESH)
    greetings = len(bits)
    if fast:
        for direction in range(2):
            place, following = line(direction)

            @pl.when(place < NZ - 1)
            def _():
                pl.semaphore_signal(barrier, inc=1, device_id=following, device_id_type=MESH)

        greetings = greetings + (z > 0).astype(jnp.int32) + (z < NZ - 1).astype(jnp.int32)
    r.vec[...] = r.vec_low[...].astype(F32)
    x_in.wait()
    for j in range(C):
        rows = slice(j * rc, (j + 1) * rc)
        normed, inverse = norm_rows(r.x[rows, :].astype(F32))
        r.g1[m, rows, :] = (normed * r.vec[0:1, :] + r.vec[1:2, :]).astype(BF16)
    r.vg[...] = jnp.zeros(r.vg.shape, F32)
    r.cnt[0] = jnp.zeros((8, 128), F32) + jnp.sum(r.valid[...].astype(F32))
    pl.semaphore_wait(barrier, greetings)

    def doubling(order, values, received, send_sems, recv_sems):
        copies = []

        def send(step):
            cp = pltpu.make_async_remote_copy(
                src_ref=values.at[step], dst_ref=received.at[step],
                send_sem=send_sems.at[step], recv_sem=recv_sems.at[step],
                device_id=bit_partner(order[step]), device_id_type=MESH,
            )
            cp.start()
            copies.append(cp)

        def following():
            step = len(copies) - 1
            copies[step].wait()
            values[step + 1] = values[step] + received[step]
            if step + 1 < len(order):
                send(step + 1)

        return send, following

    count_send, count_next = doubling(bits, r.cnt, r.cnt_r, r.cnt_ss, r.cnt_rs)

    def ag_copy(site, j, kind, ref, block, device):
        part = ref.at[block, pl.ds(j * rc, rc)]
        return pltpu.make_async_remote_copy(
            src_ref=part, dst_ref=part, send_sem=r.ag_ss.at[site, j, kind],
            recv_sem=r.ag_rs.at[site, j, kind], device_id=device, device_id_type=MESH,
        )

    def ag_send(site, j, ref):
        cx = ag_copy(site, j, 0, ref, m, to_x)
        cx.start()
        cc = ag_copy(site, j, 1, ref, m, to_core)
        cc.start()
        return cx, cc

    def ag_start(site, j, ref, value):
        ref[m, pl.ds(j * rc, rc), :] = value
        return ag_send(site, j, ref)

    def ag_forward(site, j, ref):
        cf = ag_copy(site, j, 2, ref, mx, to_core)
        cf.start()
        return cf

    def rs_copy(site, j, kind, src, dst, device):
        return pltpu.make_async_remote_copy(
            src_ref=src, dst_ref=dst, send_sem=r.rs_ss.at[site - 1, j, kind],
            recv_sem=r.rs_rs.at[site - 1, j, kind], device_id=device, device_id_type=MESH,
        )

    def rs_product(j, lhs, rhs_of, slot, kept_ref):
        def tile_body(n, carry):
            lanes = pl.ds(pl.multiple_of(n * TILE, TILE), TILE)
            rhs, dims = rhs_of(lanes)
            both = mm(lhs, rhs, dims)
            low, high = both[:rc], both[rc:]
            r.rs_cs[j, slot, :, lanes] = jnp.where(core == 0, high, low).astype(BF16)
            kept_ref[j, :, lanes] = jnp.where(core == 0, low, high)
            return carry

        lax.fori_loop(0, D // TILE, tile_body, 0)

    def rs_core(site, j, slot):
        cp = rs_copy(site, j, slot, r.rs_cs.at[j, slot], r.rs_cr.at[j, slot], to_core)
        cp.start()
        return cp

    def rs_own(site, j, lhs_of, rhs_of):
        rs_product(j, lhs_of(2 * chip), rhs_of, 1, r.keep)
        return rs_core(site, j, 1)

    def rs_other(site, j, lhs_of, rhs_of, between=None):
        rs_product(j, lhs_of(2 * (1 - chip)), rhs_of, 0, r.pass_on)
        c0 = rs_core(site, j, 0)
        c1 = between() if between else None
        c0.wait()
        r.rs_xs[j] = (r.pass_on[j] + r.rs_cr[j, 0].astype(F32)).astype(BF16)
        cx = rs_copy(site, j, 2, r.rs_xs.at[j], r.rs_xr.at[j], to_x)
        cx.start()
        return cx, c1

    def rs_start(site, j, lhs_of, rhs_of):
        return rs_other(site, j, lhs_of, rhs_of, lambda: rs_own(site, j, lhs_of, rhs_of))

    def rs_finish(j, copies):
        for cp in copies:
            cp.wait()
        return r.keep[j] + r.rs_cr[j, 1].astype(F32) + r.rs_xr[j].astype(F32)

    def share_rows(ref, share):
        lanes = pl.ds(pl.multiple_of(share * SHARE, SHARE), SHARE)
        return ref[:, :, lanes].reshape(T, SHARE).T

    def right_tile(ref, lanes):
        if len(ref.shape) == 3:
            return ref[:, :, lanes].reshape(T, lanes.size)
        return ref[:, lanes]

    def tiles(width):
        return width if width < 2 * TILE else TILE

    def part_tile(name, n, step):
        _, _, right, width = parts[name]
        lanes = pl.ds(pl.multiple_of(n * step, 128), step)
        from_lanes = pl.ds(pl.multiple_of(int(name[1]) * width + n * step, 128), step)
        return lanes, right_tile(right, from_lanes)

    def part_product(name, lhs, put):
        width = parts[name][3]
        step = tiles(width)

        def tile_body(n, carry):
            lanes, rhs = part_tile(name, n, step)
            put(lanes, mm(lhs, rhs, NN))
            return carry

        lax.fori_loop(0, width // step, tile_body, 0)

    def y_copy(name, i):
        p = parts[name][0]
        return pltpu.make_async_remote_copy(
            src_ref=getattr(r, "ys" + name).at[i], dst_ref=getattr(r, "yr" + name).at[i],
            send_sem=r.y_ss.at[p, i], recv_sem=r.y_rs.at[p, i], device_id=to_y, device_id_type=MESH,
        )

    def y_start(name):
        left = parts[name][1]
        out = getattr(r, "ys" + name)

        def pair_body(i, carry):
            lhs = jnp.concatenate(
                [share_rows(left, 4 * i + 1 - y), share_rows(left, 4 * i + 3 - y)], 0
            )

            def put(lanes, both):
                out[2 * i, :, lanes] = both[:SHARE].astype(BF16)
                out[2 * i + 1, :, lanes] = both[SHARE:].astype(BF16)

            part_product(name, lhs, put)
            y_copy(name, 2 * i).start()
            y_copy(name, 2 * i + 1).start()
            return carry

        lax.fori_loop(0, NZ // 2, pair_body, 0)

    def share_sum(name, target):
        got = getattr(r, "yr" + name)
        y_copy(name, target).wait_recv()

        def put(lanes, value):
            r.acc[0:SHARE, lanes] = value + got[target, :, lanes].astype(F32)

        part_product(name, share_rows(parts[name][1], 2 * target + y), put)

    def both_shares(name, target):
        def put(lanes, value):
            r.wide[:, lanes] = value

        left = parts[name][1]
        lanes = pl.ds(pl.multiple_of(2 * target * SHARE, 2 * SHARE), 2 * SHARE)
        part_product(name, left[:, :, lanes].reshape(T, 2 * SHARE).T, put)

    def z_copy(name, direction, step, device):
        p = parts[name][0]
        return pltpu.make_async_remote_copy(
            src_ref=getattr(r, "zs" + name).at[direction],
            dst_ref=getattr(r, "zr" + name).at[direction, step],
            send_sem=r.z_ss.at[p, direction], recv_sem=r.z_rs.at[p, direction, step],
            device_id=device, device_id_type=MESH,
        )

    def chain_step(name, step):
        out = getattr(r, "zs" + name)
        got = getattr(r, "zr" + name)
        width = parts[name][3]
        total = (r.wide if name in Z_FIRST else r.acc).at[:, 0:width]

        def one(direction, carry):
            place, following = line(direction)

            @pl.when(place <= step)
            def _():
                mirrored = NZ - 1 - step + place
                target = mirrored + direction * (NZ - 1 - 2 * mirrored)
                (both_shares if name in Z_FIRST else share_sum)(name, target)
                if step > 0:

                    @pl.when(place < step)
                    def _():
                        z_copy(name, direction, step - 1, following).wait_send()

                    @pl.when(place > 0)
                    def _():
                        z_copy(name, direction, step - 1, following).wait_recv()
                        total[...] += got[direction, step - 1].astype(F32)

                out[direction] = total[...].astype(BF16)
                z_copy(name, direction, step, following).start()

            return carry

        lax.fori_loop(0, 2, one, 0)

    def chain_end(name):
        got = getattr(r, "zr" + name)
        width = parts[name][3]
        total = (r.wide if name in Z_FIRST else r.acc).at[:, 0:width]
        (both_shares if name in Z_FIRST else share_sum)(name, z)

        def one(direction, carry):
            place, _ = line(direction)

            @pl.when(place > 0)
            def _():
                z_copy(name, direction, NZ - 2, (dp, m)).wait_recv()
                total[...] += got[direction, NZ - 2].astype(F32)

            return carry

        lax.fori_loop(0, 2, one, 0)

    def y_exchange(name):
        chain_end(name)
        width = parts[name][3]
        theirs = pl.ds(pl.multiple_of((1 - y) * SHARE, SHARE), SHARE)
        getattr(r, "ys" + name)[0] = r.wide[theirs, 0:width].astype(BF16)
        y_copy(name, 0).start()

    def a_src(name, share):
        ref = getattr(r, name[0] + "_full")
        at = pl.ds(pl.multiple_of(share * SHARE, SHARE), SHARE)
        if name[0] == "q":
            return ref.at[:, at, span(name)]
        return ref.at[at, span(name)] if name[0] == "u" else ref.at[span(name), at]

    def az_copy(name, side, direction, step, share, src, device):
        p = len(parts) + Y_FIRST.index(name) if side else parts[name][0]
        return pltpu.make_async_remote_copy(
            src_ref=src, dst_ref=a_src(name, share), send_sem=r.az_ss.at[p, direction, step],
            recv_sem=r.az_rs.at[p, direction, step], device_id=device, device_id_type=MESH,
        )

    def ay_copy(name, place, src):
        p = parts[name][0]
        return pltpu.make_async_remote_copy(
            src_ref=src, dst_ref=a_src(name, 2 * place + y), send_sem=r.ay_ss.at[p, place],
            recv_sem=r.ay_rs.at[p, place], device_id=to_y, device_id_type=MESH,
        )

    local_out = []

    def finish_share(name):
        p, _, _, width = parts[name]
        matrix = name[0]
        at0 = span(name)
        if name in Z_FIRST:
            y_copy(name, 0).wait_recv()
            ours = pl.ds(pl.multiple_of(y * SHARE, SHARE), SHARE)
            r.acc[:, 0:width] = r.wide[ours, 0:width] + getattr(r, "yr" + name)[0].astype(F32)
        else:
            chain_end(name)
        for cp in state_in[name]:
            cp.wait()
        grad_out = getattr(r, "gr" + matrix)
        fresh = getattr(r, "nc" + matrix)

        def adam_block(cols, at, state, state_at):
            grad = r.acc[:, cols]
            if matrix in "do":
                grad = grad.T
            grad_out[at] = grad
            w, a, b = adam_step(
                grad,
                state[(0,) + state_at],
                state[(1,) + state_at],
                state[(2,) + state_at],
                decay_rate,
                token_total,
            )
            state[(0,) + state_at] = w
            state[(1,) + state_at] = a
            state[(2,) + state_at] = b
            fresh[at] = w.astype(BF16)

        if matrix == "q":
            for kind in range(3):
                adam_block(
                    slice(kind * PAIR, (kind + 1) * PAIR),
                    (kind, slice(None), at0),
                    r.big,
                    (slice(SHARE, 2 * SHARE), slice(kind * HW + at0.start, kind * HW + at0.stop)),
                )
        else:

            def adam_body(n, carry):
                cols = pl.ds(pl.multiple_of(n * SHARE, SHARE), SHARE)
                there = pl.ds(pl.multiple_of(at0.start + n * SHARE, SHARE), SHARE)
                if matrix == "u":
                    adam_block(cols, (slice(None), there), r.big, (slice(0, SHARE), there))
                else:
                    at = (there, slice(None))
                    adam_block(cols, at, getattr(r, "s" + matrix), at)
                return carry

            lax.fori_loop(0, width // SHARE, adam_body, 0)
        fresh = piece(fresh, name)
        if name in Y_FIRST:
            ay_copy(name, z, fresh).start()
        for direction in range(2):
            place, following = line(direction)

            @pl.when(place < NZ - 1)
            def _():
                az_copy(name, 0, direction, 0, 2 * z + y, fresh, following).start()

        if name not in Y_FIRST:
            ay_copy(name, z, fresh).start()
        local_out.append(local_copy(fresh, a_src(name, 2 * z + y), r.o_sem.at[p, 0]))
        local_out.append(
            local_copy(piece(grad_out, name), piece(getattr(r, matrix + "_grad"), name), r.o_sem.at[p, 1])
        )
        for k, (far, near) in enumerate(state_copies(name, True)):
            local_out.append(local_copy(near, far, state_sem(name, k)))

    def neighbour_share(name):
        part = a_src(name, 2 * z + 1 - y)
        ay_copy(name, z, part).wait_recv()
        for direction in range(2):
            place, following = line(direction)

            @pl.when(place < NZ - 1)
            def _():
                az_copy(name, 1, direction, 0, 2 * z + 1 - y, part, following).start()

    def gather_step(name, step):
        for side in range(2 if name in Y_FIRST else 1):
            for direction in range(2):
                place, following = line(direction)

                @pl.when(place >= step)
                def _():
                    source = z - step + 2 * step * direction
                    share = 2 * source + (1 - y if side else y)
                    part = a_src(name, share)
                    az_copy(name, side, direction, step - 1, share, part, following).wait_recv()
                    if step < NZ - 1:

                        @pl.when(place < NZ - 1)
                        def _():
                            az_copy(name, side, direction, step, share, part, following).start()

                    if name not in Y_FIRST:
                        ay_copy(name, source, part).start()

    def gather_end(name):
        part = a_src(name, 2 * z + y)

        def one(direction, carry):
            place, following = line(direction)

            @pl.when(place <= NZ - 2)
            def _():
                z_copy(name, direction, NZ - 2, following).wait_send()

            for step in range(NZ - 1):

                @pl.when((place >= step) & (place < NZ - 1))
                def _():
                    for side in range(2 if name in Y_FIRST else 1):
                        az_copy(name, side, direction, step, 2 * z + y, part, following).wait_send()

            return carry

        lax.fori_loop(0, 2, one, 0)
        if name in Z_FIRST:
            y_copy(name, 0).wait_send()
        if name in Y_FIRST:
            ay_copy(name, z, part).wait_send()

        def y_body(i, carry):
            if name not in Z_FIRST:
                y_copy(name, i).wait_send()
            if name not in Y_FIRST:
                there = a_src(name, 2 * i + y)
                ay_copy(name, i, there).wait_send()
                ay_copy(name, i, there).wait_recv()
            return carry

        lax.fori_loop(0, NZ, y_body, 0)

    def put_out(src, dst):
        cp = pltpu.make_async_copy(src, dst, r.stage_sem)
        cp.start()
        cp.wait()

    late = {}

    def turn(point):
        if not fast:
            return
        for kind, number in ORDER.get(point, ()):
            name = names_of[number] if number is not None else None
            if kind == V:
                late["vector_next"]()
            elif kind == Y:
                y_start(name)
            elif kind == F:
                finish_share(name)
            elif kind == E:
                y_exchange(name)
            elif kind == H:
                neighbour_share(name)
            elif kind in (C0, C1, C2):
                chain_step(name, kind - C0)
            else:
                gather_step(name, kind - G1 + 1)

    ag = {}
    for j in range(C):
        ag[j] = ag_send(0, j, r.g1)
    count_send(0)

    def w_copy(kind, src, block, device):
        return pltpu.make_async_remote_copy(
            src_ref=src, dst_ref=r.act.at[block], send_sem=r.ow_ss.at[kind],
            recv_sem=r.ow_rs.at[kind], device_id=device, device_id_type=MESH,
        )

    weights[0].wait()
    w_x = w_copy(0, r.wout, m, to_x)
    w_x.start()
    w_c = w_copy(1, r.wout, m, to_core)
    w_c.start()
    r.act[m] = r.wout[...]
    for w in qkv_weights:
        w.wait()

    def project(o):
        p = mm(r.g1[o], r.wqkv[...], NN)
        at = pl.ds(pl.multiple_of(o * R, R), R)
        for pair in range(PAIRS):
            rows = slice(pair * PAIR, (pair + 1) * PAIR)
            lanes = pl.ds(pl.multiple_of(m * HW + pair * PAIR, PAIR), PAIR)
            q, k, v = (p[:, qkv_lanes(pair, kind)] for kind in range(3))
            q = (q + r.vec[6:7, lanes]).astype(BF16)
            k = k.astype(BF16)
            v = (v + r.vec[7:8, lanes]).astype(BF16)
            for kind, value in enumerate((q, k, v)):
                r.qkv[at, qkv_lanes(pair, kind)] = value
            r.qT[rows, at] = q.T
            r.kT[rows, at] = k.T
            r.vT[rows, at] = v.T

    def make_dist(i, start):
        def one(b, carry):
            key = lax.broadcasted_iota(jnp.int32, (BQ, BQ), 0) + b * BQ
            query = lax.broadcasted_iota(jnp.int32, (BQ, BQ), 1) + i * BQ
            apart = query - key
            key_seg = r.segr[:, pl.ds(pl.multiple_of(b * BQ, BQ), BQ)]
            key_seg = jnp.broadcast_to(key_seg, (BQ, BQ)).T
            same = key_seg == r.segr[:, i * BQ : (i + 1) * BQ]
            r.big[b, :, start : start + BQ] = jnp.where((apart >= 0) & same, apart.astype(F32), jnp.inf)
            return carry

        lax.fori_loop(0, i + 1, one, 0)

    n_blocks = T // BQ
    project(m)
    for i in range(n_blocks):
        make_dist(i, i * BQ)
    count_next()
    for j in range(C):
        ag[j][1].wait()
    project(mc)
    for _ in range(1, dp_size.bit_length() - 1):
        count_next()
    fw = {}
    for j in range(C):
        ag[j][0].wait()
        fw[j] = ag_forward(0, j, r.g1)
    project(mx)
    for j in range(C):
        fw[j].wait()
    project(md)

    pair_row = lax.broadcasted_iota(jnp.int32, (2 * HD, BQ), 0) // HD
    pair_lane = lax.broadcasted_iota(jnp.int32, (BQ, 2 * HD), 1) // HD
    scale2 = log2_e / math.sqrt(HD)
    K_AT, V_AT, Q_AT, DIST = 0, HW, 2 * HW, 3 * HW

    def head_slope(h):
        head = jnp.zeros((1, BQ), jnp.int32) + (m * LOCAL_HEADS + h + 1)
        return jnp.exp2(head.astype(F32) * (-8.0 / HEADS)) * log2_e

    def pair_lanes(h, start):
        return pl.ds(pl.multiple_of(start + (h // 2) * PAIR, PAIR), PAIR)

    def kind_lanes(h, kind):
        return pl.ds(pl.multiple_of((h // 2) * 3 * PAIR + kind * PAIR, PAIR), PAIR)

    def head_scores(i, ke, h, start):
        mask = (pair_row == lax.rem(h, 2)).astype(F32).astype(BF16)
        q_cols = r.qT[pair_lanes(h, 0), i * BQ : (i + 1) * BQ] * mask
        raw = mm(r.qkv[0:ke, kind_lanes(h, 1)], q_cols, NN)
        return raw * scale2 - head_slope(h) * r.big[0 : i + 1, :, start : start + BQ].reshape(ke, BQ)

    OWN, PASSING = slice(0, HW), slice(HW, 2 * HW)

    def mix_copy(kind, j, src, dst, device):
        return pltpu.make_async_remote_copy(
            src_ref=src, dst_ref=dst, send_sem=r.mix_ss.at[kind, j], recv_sem=r.mix_rs.at[kind, j],
            device_id=device, device_id_type=MESH,
        )

    def send_mixture(i):
        for j in range(C):
            rows = slice(j * rc, (j + 1) * rc)
            src = r.mix.at[i * BQ + rows.start : i * BQ + rows.stop, :]

            @pl.when(i // 2 != chip)
            def _():
                kind = (core + i) % 2
                lanes = pl.ds(pl.multiple_of(kind * HW, HW), HW)
                mix_copy(kind, j, src, r.gup.at[m, rows, lanes], to_x).start()

            @pl.when(mc == i)
            def _():
                mix_copy(2, j, src, r.gup.at[m, rows, OWN], to_core).start()

            @pl.when(m == i)
            def _():
                r.gup[m, rows, OWN] = src[...]

    for turn_of, i in enumerate([*range(n_blocks - 2), n_blocks - 1, n_blocks - 2]):
        ke = (i + 1) * BQ
        block = slice(i * BQ, (i + 1) * BQ)

        def head_body(h, carry):
            s = head_scores(i, ke, h, i * BQ)
            top = jnp.max(s, 0, keepdims=True)
            e = jnp.exp2(s - top)
            total = jnp.sum(e, 0, keepdims=True)
            p = (e * (1.0 / total)).astype(BF16)
            r.lse[h, :, block] = top + jnp.log2(total)
            at = pl.ds(pl.multiple_of(h * HD, HD), HD)
            r.mixT[at, :] = mm(r.vT[at, 0:ke], p, NN).astype(BF16)
            return carry

        lax.fori_loop(0, LOCAL_HEADS, head_body, 0)
        r.mix[block, :] = r.mixT[...].T
        send_mixture(i)
        if turn_of >= n_blocks - (mp_size.bit_length() - 1):
            count_next()

    def pair_rows(ref, j):
        def of(first):
            v = ref[pl.ds(first, 2), pl.ds(j * rc, rc), :]
            return v.reshape(2 * rc, v.shape[2])

        return of

    def pair_flat(ref, j):
        def of(first):
            a = ref[pl.ds(pl.multiple_of(first * R + j * rc, rc), rc), :]
            b = ref[pl.ds(pl.multiple_of(first * R + R + j * rc, rc), rc), :]
            return jnp.concatenate([a, b], 0)

        return of

    def ag_finish(site, j, ref):
        ag[j][0].wait()
        cf = ag_forward(site, j, ref)
        ag[j][1].wait()
        cf.wait()

    w_x.wait()
    w_f = w_copy(2, r.act.at[mx], mx, to_core)
    w_f.start()
    m_f = {}
    for j in range(C):
        rows = slice(j * rc, (j + 1) * rc)
        here = r.gup.at[m, rows, OWN]
        mix_copy(1, j, here, here, to_x).wait_recv()
        m_f[j] = mix_copy(3, j, r.gup.at[mx, rows, PASSING], r.gup.at[mx, rows, OWN], to_core)
        m_f[j].start()
    w_c.wait()
    w_f.wait()
    rs = {}
    for j in range(C):
        rows = slice(j * rc, (j + 1) * rc)
        here = r.gup.at[m, rows, OWN]
        mix_copy(0, j, here, here, to_x).wait()
        mix_copy(1, j, here, here, to_x).wait_send()
        mix_copy(2, j, here, here, to_core).wait()
        m_f[j].wait()

        def out_body(n, carry):
            lanes = pl.ds(pl.multiple_of(n * TILE, TILE), TILE)
            total = mm(r.gup[0, rows, OWN], r.act[0, :, lanes], NN)
            for q in range(1, mp_size):
                total += mm(r.gup[q, rows, OWN], r.act[q, :, lanes], NN)
            r.keep[j, :, lanes] = total
            return carry

        lax.fori_loop(0, D // TILE, out_body, 0)
        hid = r.x[rows, :].astype(F32) + r.keep[j] + r.vec[2:3, :]
        r.hidden[rows, :] = hid
        normed, inverse = norm_rows(hid)
        r.n2[rows, :] = normed
        r.inv2[rows, :] = inverse
        ag[j] = ag_start(1, j, r.g2, (normed * r.vec[3:4, :] + r.vec[4:5, :]).astype(BF16))

    weights[1].wait()
    weights[2].wait()
    def up_half(j, first):
        pair = pl.ds(first, 2)
        rows = pair_rows(r.g2, j)(first)

        def up_body(n, carry):
            lanes = pl.ds(pl.multiple_of(n * TILE, TILE), TILE)
            u = mm(rows, r.wup[:, lanes], NN) + r.vec[pl.ds(8 + m, 1), lanes]
            a, b = gelu_both(u)
            r.act[pair, pl.ds(j * rc, rc), lanes] = a.astype(BF16).reshape(2, rc, TILE)
            r.big[pair, pl.ds(j * rc, rc), lanes] = b.reshape(2, rc, TILE)
            return carry

        lax.fori_loop(0, FU // TILE, up_body, 0)

    def by_halves(site, gather, ref, half, left, rhs_of):
        own = {}
        for j in range(C):
            ag[j][1].wait()
            half(j, 2 * chip)
            own[j] = rs_own(site, j, pair_rows(left, j), rhs_of)
        for j in range(C):
            ag[j][0].wait()
            ag_forward(gather, j, ref).wait()
            if site == 2 and j == C - 1:
                turn(THIRD)
            half(j, 2 * (1 - chip))
            cx, _ = rs_other(site, j, pair_rows(left, j), rhs_of)
            rs[j] = (cx, own[j])

    by_halves(1, 1, r.g2, up_half, r.act, lambda lanes: (r.wdown[:, lanes], NN))

    t_in.wait()
    loss_scale = token_total / r.cnt[len(bits), 0:1, 0:1]
    for j in range(C):
        rows = slice(j * rc, (j + 1) * rc)
        out = r.hidden[rows, :] + rs_finish(j, rs[j]) + r.vec[5:6, :]
        r.bo[rows, :] = out.astype(BF16)
        valid = jnp.broadcast_to(r.valid[:, rows].astype(F32), (SHARE, rc)).T[:, 0:1]
        grad = valid * (out - r.t[rows, :].astype(F32)) * loss_scale
        r.ig[rows, :] = grad
        ag[j] = ag_start(2, j, r.g3, grad.astype(BF16))
        r.vg[5:6, :] += jnp.sum(grad, 0, keepdims=True)
    bo_out = local_copy(r.bo, r.bo_hbm, r.in_sem.at[3])

    def act_half(j, first):
        pair = pl.ds(first, 2)
        rows = pair_rows(r.g3, j)(first)

        def act_body(n, carry):
            lanes = pl.ds(pl.multiple_of(n * TILE, TILE), TILE)
            ga = mm(rows, r.wdown[lanes, :], NT)
            gu = ga * r.big[pair, pl.ds(j * rc, rc), lanes].reshape(2 * rc, TILE)
            r.gup[pair, pl.ds(j * rc, rc), lanes] = gu.astype(BF16).reshape(2, rc, TILE)
            return carry

        lax.fori_loop(0, FU // TILE, act_body, 0)

    by_halves(2, 2, r.g3, act_half, r.gup, lambda lanes: (r.wup[lanes, :], NT))

    def whole_grad(left, right, width, dst):
        def body(n, carry):
            lanes = pl.ds(pl.multiple_of(n * TILE, TILE), TILE)
            r.stage[:, 0:width] = mm(right_tile(left, lanes), right[...].reshape(T, width), TN)
            put_out(r.stage.at[:, 0:width], dst.at[lanes, :])
            return carry

        lax.fori_loop(0, dst.shape[0] // TILE, body, 0)

    if not fast:
        whole_grad(r.act, r.g3, D, r.d_grad)

    for j in range(C):
        rows = slice(j * rc, (j + 1) * rc)
        gs = rs_finish(j, rs[j])
        gh = r.ig[rows, :] + norm_backward(gs, r.n2[rows, :], r.inv2[rows, :], r.vec[3:4, :])
        r.hidden[rows, :] = gh
        ag[j] = ag_start(3, j, r.g4, gh.astype(BF16))
        r.vg[2:3, :] += jnp.sum(gh, 0, keepdims=True)
        r.vg[3:4, :] += jnp.sum(gs * r.n2[rows, :], 0, keepdims=True)
        r.vg[4:5, :] += jnp.sum(gs, 0, keepdims=True)

    turn(NORM)
    if not fast:
        whole_grad(r.g2, r.gup, FU, r.u_grad)
    r.vg[pl.ds(8 + m, 1), :] = jnp.sum(r.gup[...].reshape(T, FU).astype(F32), 0, keepdims=True)

    for j in range(C):
        ag_finish(3, j, r.g4)

    def gm_body(o, carry):
        at = pl.ds(pl.multiple_of(o * R, R), R)
        gmx = mm(r.g4[o], r.wout[...], NT).astype(BF16)
        r.gm[at, :] = gmx
        r.vT[:, at] = gmx.T
        return carry

    lax.fori_loop(0, mp_size, gm_body, 0)
    turn(FOURTH)

    r.big[:, :, K_AT : K_AT + HW] = jnp.zeros((mp_size, R, HW), F32)
    r.big[:, :, V_AT : V_AT + HW] = jnp.zeros((mp_size, R, HW), F32)
    for pair in range(PAIRS):
        for i in range(n_blocks):
            ke = (i + 1) * BQ
            block = slice(i * BQ, (i + 1) * BQ)
            make_dist(i, DIST)

            def back_body(half, carry):
                h = 2 * pair + half
                row_mask = (pair_row == half).astype(F32).astype(BF16)
                lane_mask = (pair_lane == half).astype(F32).astype(BF16)
                lanes = slice(pair * PAIR, (pair + 1) * PAIR)
                p = jnp.exp2(head_scores(i, ke, h, DIST) - r.lse[h, :, block])
                gp = mm(r.qkv[0:ke, qkv_lanes(pair, 2)], r.vT[lanes, block] * row_mask, NN)
                inner = jnp.sum(p * gp, 0, keepdims=True)
                raw = (p * (gp - inner)).astype(BF16)
                low = p.astype(BF16)
                r.big[0 : i + 1, :, V_AT + lanes.start : V_AT + lanes.stop] += mm(
                    low, r.gm[block, lanes] * lane_mask, NN
                ).reshape(i + 1, BQ, PAIR)
                r.big[0 : i + 1, :, K_AT + lanes.start : K_AT + lanes.stop] += mm(
                    raw, r.qkv[block, qkv_lanes(pair, 0)] * lane_mask, NN
                ).reshape(i + 1, BQ, PAIR)
                at = pl.ds(pl.multiple_of(h * HD, HD), HD)
                r.big[i, at, Q_AT : Q_AT + BQ] = mm(r.kT[at, 0:ke], raw, NN) * (1.0 / math.sqrt(HD))
                return carry

            lax.fori_loop(0, 2, back_body, 0)
            rows = slice(pair * PAIR, (pair + 1) * PAIR)
            r.st[block, qkv_lanes(pair, 0)] = r.big[i, rows, Q_AT : Q_AT + BQ].T.astype(BF16)
            turn((pair, i))
        lanes = slice(pair * PAIR, (pair + 1) * PAIR)
        r.st[:, qkv_lanes(pair, 1)] = (
            r.big[:, :, K_AT + lanes.start : K_AT + lanes.stop].reshape(T, PAIR) * (1.0 / math.sqrt(HD))
        ).astype(BF16)
        r.st[:, qkv_lanes(pair, 2)] = (
            r.big[:, :, V_AT + lanes.start : V_AT + lanes.stop].reshape(T, PAIR).astype(BF16)
        )
        turn((pair,))
    for pair in range(PAIRS):
        lanes = pl.ds(pl.multiple_of(m * HW + pair * PAIR, PAIR), PAIR)
        for row, kind in ((6, 0), (7, 2)):
            r.vg[row : row + 1, lanes] = jnp.sum(
                r.st[:, qkv_lanes(pair, kind)].astype(F32), 0, keepdims=True
            )

    if fast:
        fetch_state("u")
        fetch_state("q")

    for j in range(C):
        rs[j] = rs_start(3, j, pair_flat(r.st, j), lambda lanes: (r.wqkv[lanes, :], NT))

    turn(BACK)
    if not fast:
        whole_grad(r.mix, r.g4, D, r.o_grad)
        whole_grad(r.g1, r.st, 3 * HW, r.q_grad)

    for j in range(C):
        rows = slice(j * rc, (j + 1) * rc)
        gf = rs_finish(j, rs[j])
        normed, inverse = norm_rows(r.x[rows, :].astype(F32))
        r.ig[rows, :] = r.hidden[rows, :] + norm_backward(gf, normed, inverse, r.vec[0:1, :])
        r.vg[0:1, :] += jnp.sum(gf * normed, 0, keepdims=True)
        r.vg[1:2, :] += jnp.sum(gf, 0, keepdims=True)
    ig_out = local_copy(r.ig, r.ig_hbm, r.in_sem.at[4])

    vector_send, vector_step = doubling(mp_bits + dp_bits, r.vs, r.vs_r, r.cnt_ss, r.cnt_rs)
    r.vs[0] = r.vg[...]
    vector_send(0)
    vector_out = []

    def vector_next():
        vector_step()
        late["steps"] = late.get("steps", 0) + 1
        if late["steps"] < len(bits):
            return
        vec_in.wait()
        total = r.vs[len(bits), 0 : r.vec.shape[0]]
        new = adam_step(total, r.vec_state[0], r.vec_state[1], r.vec_state[2], 0.0, token_total)
        r.v_sum[...] = total
        for k in range(3):
            r.vec_state[k] = new[k]
        r.v_copy[...] = new[0].astype(BF16)
        for k, (near, far) in enumerate(
            [(r.v_sum, r.v_grad), (r.vec_state, r.v_new), (r.v_copy, r.v_low)]
        ):
            vector_out.append(local_copy(near, far, r.in_sem.at[5 + k]))

    late["vector_next"] = vector_next
    if fast:
        turn(END)
        for name in parts:
            gather_end(name)
        for cp in local_out:
            cp.wait()
    else:
        for _ in bits:
            vector_next()
    for cp in [bo_out, ig_out] + vector_out:
        cp.wait()


Z_FIRST = ("d0",)
Y_FIRST = ("u1",)
Y, C0, C1, C2, E, F, H, G1, G2, G3, V = range(11)
D0, D1, U0, U1, O0, Q0, Q1 = range(7)
THIRD, NORM, FOURTH, BACK, END = range(5)
ORDER = {
    THIRD: ((Y, D1), (C0, D0),),
    NORM: ((C0, D1), (Y, U0), (C1, D0), (Y, U1), (C1, D1), (C2, D0),),
    FOURTH: ((C0, U0),),
    (0, 1): ((C2, D1),),
    (0, 2): ((E, D0),),
    (0,): ((Y, Q0),),
    (1, 0): ((C0, U1),),
    (1, 1): ((C1, U0),),
    (1, 2): ((C1, U1), (F, D1), (Y, O0),),
    (1, 3): ((F, D0), (C0, Q0), (C2, U1),),
    BACK: (
        (G1, D0), (Y, Q1), (C1, Q0), (G1, D1), (C2, U0), (C0, O0), (F, U1), (C2, Q0), (G2, D1),
    ),
    END: (
        (F, U0), (C1, O0), (C0, Q1), (G3, D1), (G2, D0), (F, Q0), (C2, O0), (V, None), (C1, Q1), (G1, U0),
        (H, U1), (V, None), (G1, Q0), (F, O0), (C2, Q1), (G2, U0), (G1, O0), (F, Q1), (G2, O0), (G2, Q0),
        (G3, Q0), (V, None), (G1, Q1), (G2, Q1), (G1, U1), (G3, U0), (V, None), (G3, Q1), (G2, U1), (G3, D0),
        (V, None), (G3, O0), (G3, U1),
    ),
}


def pieces(head_width, units):
    return [
        ("d0", units // 2),
        ("d1", units // 2),
        ("u0", units // 2),
        ("u1", units // 2),
        ("o0", head_width),
    ] + [("q%d" % pair, 6 * HD) for pair in range(head_width // (2 * HD))]


SHARE = 128


def block_call(sizes, x, teacher, segments, valid, vectors, copies, states):
    dp_size, mp_size = sizes
    R, D = x.shape
    T = mp_size * R
    wqkv, wout, wup, wdown = copies
    HW = wout.shape[0]
    FU = wup.shape[1]
    C = CHUNKS
    rc = R // C
    n_bits = (dp_size * mp_size).bit_length() - 1
    NZ = dp_size // 2
    PAIRS = HW // (2 * HD)
    fast = D == dp_size * SHARE
    dma = pltpu.SemaphoreType.DMA
    M = pltpu.VMEM
    S = jax.ShapeDtypeStruct
    vmem = pl.BlockSpec(memory_space=pltpu.VMEM)
    anywhere = pl.BlockSpec(memory_space=pl.ANY)

    ins = {
        "x_hbm": (x, anywhere),
        "t_hbm": (teacher, anywhere),
        "segr": (segments, vmem),
        "valid": (valid.reshape(1, R), vmem),
        "vec_low": (vectors, vmem),
        "vec_state_hbm": (states[4], anywhere),
        "wqkv_hbm": (wqkv, anywhere),
        "wout_hbm": (wout, anywhere),
        "wup_hbm": (wup, anywhere),
        "wdown_hbm": (wdown, anywhere),
    }
    outs = {
        "bo_hbm": (S((R, D), BF16), anywhere),
        "ig_hbm": (S((R, D), F32), anywhere),
        "v_grad": (S(vectors.shape, F32), anywhere),
        "v_new": (S(states[4].shape, F32), anywhere),
        "v_low": (S(vectors.shape, BF16), anywhere),
    }
    if fast:
        shard = {"q": (3, SHARE, HW), "o": (HW, SHARE), "u": (SHARE, FU), "d": (FU, SHARE)}
        whole = {"q": (3, D, HW), "o": (HW, D), "u": (D, FU), "d": (FU, D)}
        for name, state in zip("qoud", states):
            ins["s%s_hbm" % name] = (state, anywhere)
        for name in "qoud":
            outs[name + "_grad"] = (S(shard[name], F32), anywhere)
        for name in "qoud":
            outs[name + "_new"] = (S((3,) + shard[name], F32), anywhere)
        for name in "qoud":
            outs[name + "_full"] = (S(whole[name], BF16), anywhere)
    else:
        outs["q_grad"] = (S((D, 3 * HW), F32), anywhere)
        outs["o_grad"] = (S((HW, D), F32), anywhere)
        outs["u_grad"] = (S((D, FU), F32), anywhere)
        outs["d_grad"] = (S((FU, D), F32), anywhere)
    scratch = {
        "wqkv": M((D, 3 * HW), BF16),
        "wout": M((HW, D), BF16),
        "wup": M((D, FU), BF16),
        "wdown": M((FU, D), BF16),
        "w_sem": dma((3,)),
        "ow_ss": dma((3,)),
        "ow_rs": dma((3,)),
        "mix_ss": dma((4, C)),
        "mix_rs": dma((4, C)),
        "in_sem": dma((8,)),
        "x": M((R, D), BF16),
        "t": M((R, D), BF16),
        "bo": M((R, D), BF16),
        "ig": M((R, D), F32),
        "vec_state": M(states[4].shape, F32),
        "v_sum": M(vectors.shape, F32),
        "v_copy": M(vectors.shape, BF16),
        "wq_sem": dma((PAIRS, 3)),
        "vec": M(vectors.shape, F32),
        "g1": M((mp_size, R, D), BF16),
        "g2": M((mp_size, R, D), BF16),
        "g3": M((mp_size, R, D), BF16),
        "g4": M((mp_size, R, D), BF16),
        "qkv": M((T, 3 * HW), BF16),
        "qT": M((HW, T), BF16),
        "kT": M((HW, T), BF16),
        "vT": M((HW, T), BF16),
        "mixT": M((HW, BQ), BF16),
        "mix": M((T, HW), BF16),
        "lse": M((HW // HD, 1, T), F32),
        "hidden": M((R, D), F32),
        "n2": M((R, D), F32),
        "inv2": M((R, 1), F32),
        "act": M((mp_size, R, FU), BF16),
        "big": M((mp_size, R, FU), F32),
        "gup": M((mp_size, R, FU), BF16),
        "gm": M((T, HW), BF16),
        "st": M((T, 3 * HW), BF16),
        "pass_on": M((C, rc, D), F32),
        "keep": M((C, rc, D), F32),
        "rs_cs": M((C, 2, rc, D), BF16),
        "rs_cr": M((C, 2, rc, D), BF16),
        "rs_xs": M((C, rc, D), BF16),
        "rs_xr": M((C, rc, D), BF16),
        "cnt": M((n_bits + 1, 8, 128), F32),
        "cnt_r": M((n_bits, 8, 128), F32),
        "vg": M((16, D), F32),
        "vs": M((n_bits + 1, 16, D), F32),
        "vs_r": M((n_bits, 16, D), F32),
        "ag_ss": dma((4, C, 3)),
        "ag_rs": dma((4, C, 3)),
        "rs_ss": dma((3, C, 3)),
        "rs_rs": dma((3, C, 3)),
        "cnt_ss": dma((n_bits,)),
        "cnt_rs": dma((n_bits,)),
    }
    if fast:
        for name, w in pieces(HW, FU):
            shares = 1 if name in Z_FIRST else NZ
            rows = 2 * SHARE if name in Z_FIRST else SHARE
            scratch["ys" + name] = M((shares, SHARE, w), BF16)
            scratch["yr" + name] = M((shares, SHARE, w), BF16)
            scratch["zs" + name] = M((2, rows, w), BF16)
            scratch["zr" + name] = M((2, NZ - 1, rows, w), BF16)
        for name in "qoud":
            scratch["gr" + name] = M(shard[name], F32)
            scratch["nc" + name] = M(shard[name], BF16)
        scratch["sd"] = M((3,) + shard["d"], F32)
        scratch["so"] = M((3,) + shard["o"], F32)
        scratch["acc"] = M((SHARE, FU // 2), F32)
        scratch["wide"] = M((2 * SHARE, FU // 2), F32)
        n = len(pieces(HW, FU))
        scratch["s_sem"] = dma((n + 2 * PAIRS,))
        scratch["o_sem"] = dma((n, 2))
        scratch["y_ss"] = dma((n, NZ))
        scratch["y_rs"] = dma((n, NZ))
        scratch["z_ss"] = dma((n, 2))
        scratch["z_rs"] = dma((n, 2, NZ - 1))
        scratch["az_ss"] = dma((n + len(Y_FIRST), 2, NZ - 1))
        scratch["az_rs"] = dma((n + len(Y_FIRST), 2, NZ - 1))
        scratch["ay_ss"] = dma((n, NZ))
        scratch["ay_rs"] = dma((n, NZ))
    else:
        scratch["stage"] = M((TILE, D), F32)
        scratch["stage_sem"] = dma
    names = list(ins) + list(outs) + list(scratch)
    results = pl.pallas_call(
        functools.partial(block_kernel, sizes, fast, names),
        out_shape=[v[0] for v in outs.values()],
        in_specs=[v[1] for v in ins.values()],
        out_specs=[v[1] for v in outs.values()],
        scratch_shapes=list(scratch.values()),
        compiler_params=pltpu.CompilerParams(
            collective_id=0, has_side_effects=True, vmem_limit_bytes=62 << 20
        ),
        name="block",
    )(*[v[0] for v in ins.values()])
    outs = dict(zip(outs, results))
    if fast:
        names, results = list(outs), list(outs.values())
        outs = dict(zip(names, settle(results)))
    return outs, fast


def settle_kernel(count, *refs):
    sources, results, held = refs[:count], refs[count : 2 * count], refs[2 * count : 3 * count]
    in_sem, out_sem = refs[3 * count :]
    loads = [pltpu.make_async_copy(sources[i], held[i], in_sem.at[i]) for i in range(count)]
    stores = [pltpu.make_async_copy(held[i], results[i], out_sem.at[i]) for i in range(count)]
    for cp in loads:
        cp.start()
    for load, store in zip(loads, stores):
        load.wait()
        store.start()
    for cp in stores:
        cp.wait()


def settle(arrays):
    anywhere = pl.BlockSpec(memory_space=pltpu.HBM)
    dma = pltpu.SemaphoreType.DMA((len(arrays),))
    return pl.pallas_call(
        functools.partial(settle_kernel, len(arrays)),
        out_shape=[jax.ShapeDtypeStruct(a.shape, a.dtype) for a in arrays],
        in_specs=[anywhere] * len(arrays),
        out_specs=[anywhere] * len(arrays),
        scratch_shapes=[pltpu.VMEM(a.shape, a.dtype) for a in arrays] + [dma, dma],
        compiler_params=pltpu.CompilerParams(vmem_limit_bytes=62 << 20),
        name="settle",
    )(*arrays)


def adam_update(gradient, stored, decay_factor, token_total):
    new = adam_step(gradient, stored[0], stored[1], stored[2], decay_factor, token_total)
    return (jnp.stack(new), new[0].astype(jnp.bfloat16))


def shards(
    inputs,
    teacher,
    segments,
    valid_mask,
    qkv_copy,
    out_copy,
    up_copy,
    down_copy,
    vector_copy,
    qkv_state,
    out_state,
    up_state,
    down_state,
    vector_state,
):
    sizes = (lax.axis_size("dp"), lax.axis_size("mp"))
    token_total = inputs.shape[0] * sizes[0] * sizes[1]
    width = inputs.shape[1]
    head_width = qkv_copy.shape[2]
    pairs = head_width // (2 * HD)
    outs, fast = block_call(
        sizes,
        inputs,
        teacher,
        segments,
        valid_mask,
        vector_copy,
        (qkv_copy.transpose(1, 0, 2), out_copy, up_copy, down_copy),
        (qkv_state.transpose(0, 2, 1, 3), out_state, up_state, down_state, vector_state),
    )
    vector_grad, vector_new, vector_low = outs["v_grad"], outs["v_new"], outs["v_low"]
    if fast:
        qkv_grad = outs["q_grad"].transpose(1, 0, 2)
        out_grad, up_grad, down_grad = (outs[n + "_grad"] for n in "oud")
        qkv_new = outs["q_new"].transpose(0, 2, 1, 3)
        out_new, up_new, down_new = (outs[n + "_new"] for n in "oud")
        qkv_full = outs["q_full"].transpose(1, 0, 2)
        out_full, up_full, down_full = (outs[n + "_full"] for n in "oud")
    else:
        qkv_local = outs["q_grad"].reshape(width, pairs, 3, 2 * HD)
        qkv_local = qkv_local.transpose(0, 2, 1, 3).reshape(width, 3, head_width)
        qkv_grad, out_grad, up_grad, down_grad = (
            lax.psum_scatter(qkv_local, "dp", scatter_dimension=0, tiled=True),
            lax.psum_scatter(outs["o_grad"], "dp", scatter_dimension=1, tiled=True),
            lax.psum_scatter(outs["u_grad"], "dp", scatter_dimension=0, tiled=True),
            lax.psum_scatter(outs["d_grad"], "dp", scatter_dimension=1, tiled=True),
        )
        qkv_new, qkv_low = adam_update(qkv_grad, qkv_state, decay_rate, token_total)
        out_new, out_low = adam_update(out_grad, out_state, decay_rate, token_total)
        up_new, up_low = adam_update(up_grad, up_state, decay_rate, token_total)
        down_new, down_low = adam_update(down_grad, down_state, decay_rate, token_total)
        qkv_full, out_full, up_full, down_full = (
            lax.all_gather(qkv_low, "dp", axis=0, tiled=True),
            lax.all_gather(out_low, "dp", axis=1, tiled=True),
            lax.all_gather(up_low, "dp", axis=0, tiled=True),
            lax.all_gather(down_low, "dp", axis=1, tiled=True),
        )
    return (
        outs["bo_hbm"],
        outs["ig_hbm"],
        qkv_grad,
        out_grad,
        up_grad,
        down_grad,
        vector_grad,
        qkv_new,
        out_new,
        up_new,
        down_new,
        vector_new,
        qkv_full,
        out_full,
        up_full,
        down_full,
        vector_low,
    )


def solution(mesh):
    in_specs = (
        P(("dp", "mp"), None),
        P(("dp", "mp"), None),
        P("dp", None),
        P(("dp", "mp")),
        P(None, None, "mp"),
        P("mp", None),
        P(None, "mp"),
        P("mp", None),
        P(),
        P(None, "dp", None, "mp"),
        P(None, "mp", "dp"),
        P(None, "dp", "mp"),
        P(None, "mp", "dp"),
        P(),
    )
    out_specs = (
        P(("dp", "mp"), None),
        P(("dp", "mp"), None),
        P("dp", None, "mp"),
        P("mp", "dp"),
        P("dp", "mp"),
        P("mp", "dp"),
        P(),
        P(None, "dp", None, "mp"),
        P(None, "mp", "dp"),
        P(None, "dp", "mp"),
        P(None, "mp", "dp"),
        P(),
        P(None, None, "mp"),
        P("mp", None),
        P(None, "mp"),
        P("mp", None),
        P(),
    )
    return jax.shard_map(shards, mesh=mesh, in_specs=in_specs, out_specs=out_specs, check_vma=False)
```

```python
import functools
import math
import types

import jax
import jax.numpy as jnp
from jax import lax
from jax.experimental import pallas as pl
from jax.experimental.pallas import tpu as pltpu
from jax.sharding import PartitionSpec as P

HEADS = 16
HD = 64

norm_eps = 1e-05
beta_one = 0.9
beta_two = 0.95
adam_eps = 1e-08
learn_rate = 0.001
decay_rate = 0.1
correction_one = 1.0 - (0.9**10) ** 10
correction_two = 1.0 - (0.95**10) ** 10
log2_e = 1.4426950408889634

CHUNKS = 2
BQ = 256
TILE = 256
MESH = pl.DeviceIdType.MESH
F32 = jnp.float32
BF16 = jnp.bfloat16
NN = ((1,), (0,))
NT = ((1,), (1,))
TN = ((0,), (0,))


def mm(a, b, dims):
    return lax.dot_general(a, b, (dims, ((), ())), preferred_element_type=F32)


def gelu_both(v):
    c = 0.7978845608
    v2 = v * v
    th = jnp.tanh(c * (v + 0.044715 * v2 * v))
    half = 0.5 * (1.0 + th)
    back = half + 0.5 * v * (1.0 - th * th) * (c * (1.0 + 3.0 * 0.044715 * v2))
    return v * half, back


def norm_rows(v):
    centred = v - jnp.mean(v, -1, keepdims=True)
    inverse = lax.rsqrt(jnp.mean(centred * centred, -1, keepdims=True) + norm_eps)
    return centred * inverse, inverse


def norm_backward(grad_out, normed, inverse, gain_row):
    scaled = grad_out * gain_row
    return inverse * (
        scaled
        - jnp.mean(scaled, -1, keepdims=True)
        - normed * jnp.mean(scaled * normed, -1, keepdims=True)
    )


def adam_step(gradient, weight, first, second, decay_factor, token_total):
    mean_grad = gradient / token_total
    moment_one = beta_one * first + (1.0 - beta_one) * mean_grad
    moment_two = beta_two * second + (1.0 - beta_two) * mean_grad * mean_grad
    update = (
        moment_one / correction_one / (jnp.sqrt(moment_two / correction_two) + adam_eps)
        + decay_factor * weight
    )
    return weight - learn_rate * update, moment_one, moment_two


def block_kernel(sizes, fast, names, *refs):
    r = types.SimpleNamespace(**dict(zip(names, refs)))
    dp_size, mp_size = sizes
    dp = lax.axis_index("dp")
    m = lax.axis_index("mp")
    core = lax.rem(m, 2)
    chip = m // 2
    mc = m + 1 - 2 * core
    mx = lax.rem(m + 2, 4)
    md = mc + mx - m
    C = CHUNKS
    R, D = r.x.shape
    rc = R // C
    T = mp_size * R
    HW = r.wout.shape[0]
    FU = r.wup.shape[1]
    LOCAL_HEADS = HW // HD
    PAIR = 2 * HD
    PAIRS = HW // PAIR
    token_total = float(dp_size * T)

    dp_bits = [("dp", b) for b in range(dp_size.bit_length() - 1)]
    mp_bits = [("mp", b) for b in range(mp_size.bit_length() - 1)]
    bits = dp_bits + mp_bits

    def flip(v, b):
        w = 1 << b
        return v + w - 2 * w * lax.rem(v // w, 2)

    def bit_partner(item):
        axis, b = item
        if axis == "mp":
            return (dp, flip(m, b))
        return (flip(dp, b), m)

    to_core = (dp, mc)
    to_x = (dp, mx)

    NZ = dp_size // 2
    z = dp // 2
    y = lax.rem(dp, 2)
    to_y = (dp + 1 - 2 * y, m)

    def line(direction):
        place = z + direction * (NZ - 1 - 2 * z)
        return place, (dp + 2 - 4 * direction, m)

    def local_copy(src, dst, sem):
        cp = pltpu.make_async_copy(src, dst, sem)
        cp.start()
        return cp

    def qkv_lanes(pair, kind):
        return slice((3 * pair + kind) * PAIR, (3 * pair + kind + 1) * PAIR)

    x_in = local_copy(r.x_hbm, r.x, r.in_sem.at[0])
    t_in = local_copy(r.t_hbm, r.t, r.in_sem.at[1])
    qkv_weights = [
        local_copy(
            r.wqkv_hbm.at[kind, :, pair * PAIR : (pair + 1) * PAIR],
            r.wqkv.at[:, qkv_lanes(pair, kind)],
            r.wq_sem.at[pair, kind],
        )
        for pair in range(PAIRS)
        for kind in range(3)
    ]
    weights = [
        local_copy(src, dst, r.w_sem.at[i])
        for i, (src, dst) in enumerate(
            [(r.wout_hbm, r.wout), (r.wup_hbm, r.wup), (r.wdown_hbm, r.wdown)]
        )
    ]
    if fast:
        parts = {}
        for name, width in pieces(HW, FU):
            left, right = {
                "d": (r.g3, r.act),
                "u": (r.g2, r.gup),
                "o": (r.g4, r.mix),
                "q": (r.g1, r.st),
            }[name[0]]
            parts[name] = (len(parts), left, right, width)
        names_of = list(parts)
        state_in = {}

        def span(name):
            width = PAIR if name[0] == "q" else parts[name][3]
            return slice(int(name[1]) * width, (int(name[1]) + 1) * width)

        def piece(ref, name):
            at = span(name)
            if name[0] == "q":
                return ref.at[:, :, at]
            return ref.at[:, at] if name[0] == "u" else ref.at[at, :]

        def state_copies(name, out):
            far = getattr(r, name[0] + "_new") if out else getattr(r, "s%s_hbm" % name[0])
            at = span(name)
            if name[0] == "q":
                return [
                    (
                        far.at[:, kind, :, at],
                        r.big.at[0:3, SHARE : 2 * SHARE, kind * HW + at.start : kind * HW + at.stop],
                    )
                    for kind in range(3)
                ]
            if name[0] == "u":
                return [(far.at[:, :, at], r.big.at[0:3, 0:SHARE, at])]
            return [(far.at[:, at, :], getattr(r, "s" + name[0]).at[:, at, :])]

        def state_sem(name, k):
            p = parts[name][0]
            return r.s_sem.at[p + 2 * max(0, p - 5) + k]

        def fetch_state(matrix):
            for name in parts:
                if name[0] == matrix:
                    state_in[name] = [
                        local_copy(far, near, state_sem(name, k))
                        for k, (far, near) in enumerate(state_copies(name, False))
                    ]

        fetch_state("d")
        fetch_state("o")

    vec_in = local_copy(r.vec_state_hbm, r.vec_state, r.in_sem.at[2])
    barrier = pltpu.get_barrier_semaphore()
    for item in bits:
        pl.semaphore_signal(barrier, inc=1, device_id=bit_partner(item), device_id_type=MESH)
    greetings = len(bits)
    if fast:
        for direction in range(2):
            place, following = line(direction)

            @pl.when(place < NZ - 1)
            def _():
                pl.semaphore_signal(barrier, inc=1, device_id=following, device_id_type=MESH)

        greetings = greetings + (z > 0).astype(jnp.int32) + (z < NZ - 1).astype(jnp.int32)
    r.vec[...] = r.vec_low[...].astype(F32)
    x_in.wait()
    for j in range(C):
        rows = slice(j * rc, (j + 1) * rc)
        normed, inverse = norm_rows(r.x[rows, :].astype(F32))
        r.g1[m, rows, :] = (normed * r.vec[0:1, :] + r.vec[1:2, :]).astype(BF16)
    r.vg[...] = jnp.zeros(r.vg.shape, F32)
    r.cnt[0] = jnp.zeros((8, 128), F32) + jnp.sum(r.valid[...].astype(F32))
    pl.semaphore_wait(barrier, greetings)

    def doubling(order, values, received, send_sems, recv_sems):
        copies = []

        def send(step):
            cp = pltpu.make_async_remote_copy(
                src_ref=values.at[step], dst_ref=received.at[step],
                send_sem=send_sems.at[step], recv_sem=recv_sems.at[step],
                device_id=bit_partner(order[step]), device_id_type=MESH,
            )
            cp.start()
            copies.append(cp)

        def following():
            step = len(copies) - 1
            copies[step].wait()
            values[step + 1] = values[step] + received[step]
            if step + 1 < len(order):
                send(step + 1)

        return send, following

    count_send, count_next = doubling(bits, r.cnt, r.cnt_r, r.cnt_ss, r.cnt_rs)

    def ag_copy(site, j, kind, ref, block, device):
        part = ref.at[block, pl.ds(j * rc, rc)]
        return pltpu.make_async_remote_copy(
            src_ref=part, dst_ref=part, send_sem=r.ag_ss.at[site, j, kind],
            recv_sem=r.ag_rs.at[site, j, kind], device_id=device, device_id_type=MESH,
        )

    def ag_send(site, j, ref):
        cx = ag_copy(site, j, 0, ref, m, to_x)
        cx.start()
        cc = ag_copy(site, j, 1, ref, m, to_core)
        cc.start()
        return cx, cc

    def ag_start(site, j, ref, value):
        ref[m, pl.ds(j * rc, rc), :] = value
        return ag_send(site, j, ref)

    def ag_forward(site, j, ref):
        cf = ag_copy(site, j, 2, ref, mx, to_core)
        cf.start()
        return cf

    def rs_copy(site, j, kind, src, dst, device):
        return pltpu.make_async_remote_copy(
            src_ref=src, dst_ref=dst, send_sem=r.rs_ss.at[site - 1, j, kind],
            recv_sem=r.rs_rs.at[site - 1, j, kind], device_id=device, device_id_type=MESH,
        )

    def rs_product(j, lhs, rhs_of, slot, kept_ref):
        def tile_body(n, carry):
            lanes = pl.ds(pl.multiple_of(n * TILE, TILE), TILE)
            rhs, dims = rhs_of(lanes)
            both = mm(lhs, rhs, dims)
            low, high = both[:rc], both[rc:]
            r.rs_cs[j, slot, :, lanes] = jnp.where(core == 0, high, low).astype(BF16)
            kept_ref[j, :, lanes] = jnp.where(core == 0, low, high)
            return carry

        lax.fori_loop(0, D // TILE, tile_body, 0)

    def rs_core(site, j, slot):
        cp = rs_copy(site, j, slot, r.rs_cs.at[j, slot], r.rs_cr.at[j, slot], to_core)
        cp.start()
        return cp

    def rs_own(site, j, lhs_of, rhs_of):
        rs_product(j, lhs_of(2 * chip), rhs_of, 1, r.keep)
        return rs_core(site, j, 1)

    def rs_other(site, j, lhs_of, rhs_of, between=None):
        rs_product(j, lhs_of(2 * (1 - chip)), rhs_of, 0, r.pass_on)
        c0 = rs_core(site, j, 0)
        c1 = between() if between else None
        c0.wait()
        r.rs_xs[j] = (r.pass_on[j] + r.rs_cr[j, 0].astype(F32)).astype(BF16)
        cx = rs_copy(site, j, 2, r.rs_xs.at[j], r.rs_xr.at[j], to_x)
        cx.start()
        return cx, c1

    def rs_start(site, j, lhs_of, rhs_of):
        return rs_other(site, j, lhs_of, rhs_of, lambda: rs_own(site, j, lhs_of, rhs_of))

    def rs_finish(j, copies):
        for cp in copies:
            cp.wait()
        return r.keep[j] + r.rs_cr[j, 1].astype(F32) + r.rs_xr[j].astype(F32)

    def share_rows(ref, share):
        lanes = pl.ds(pl.multiple_of(share * SHARE, SHARE), SHARE)
        return ref[:, :, lanes].reshape(T, SHARE).T

    def right_tile(ref, lanes):
        if len(ref.shape) == 3:
            return ref[:, :, lanes].reshape(T, lanes.size)
        return ref[:, lanes]

    def tiles(width):
        return width if width < 2 * TILE else TILE

    def part_tile(name, n, step):
        _, _, right, width = parts[name]
        lanes = pl.ds(pl.multiple_of(n * step, 128), step)
        from_lanes = pl.ds(pl.multiple_of(int(name[1]) * width + n * step, 128), step)
        return lanes, right_tile(right, from_lanes)

    def part_product(name, lhs, put):
        width = parts[name][3]
        step = tiles(width)

        def tile_body(n, carry):
            lanes, rhs = part_tile(name, n, step)
            put(lanes, mm(lhs, rhs, NN))
            return carry

        lax.fori_loop(0, width // step, tile_body, 0)

    def y_copy(name, i):
        p = parts[name][0]
        return pltpu.make_async_remote_copy(
            src_ref=getattr(r, "ys" + name).at[i], dst_ref=getattr(r, "yr" + name).at[i],
            send_sem=r.y_ss.at[p, i], recv_sem=r.y_rs.at[p, i], device_id=to_y, device_id_type=MESH,
        )

    def y_start(name):
        left = parts[name][1]
        out = getattr(r, "ys" + name)

        def pair_body(i, carry):
            lhs = jnp.concatenate(
                [share_rows(left, 4 * i + 1 - y), share_rows(left, 4 * i + 3 - y)], 0
            )

            def put(lanes, both):
                out[2 * i, :, lanes] = both[:SHARE].astype(BF16)
                out[2 * i + 1, :, lanes] = both[SHARE:].astype(BF16)

            part_product(name, lhs, put)
            y_copy(name, 2 * i).start()
            y_copy(name, 2 * i + 1).start()
            return carry

        lax.fori_loop(0, NZ // 2, pair_body, 0)

    def share_sum(name, target):
        got = getattr(r, "yr" + name)
        y_copy(name, target).wait_recv()

        def put(lanes, value):
            r.acc[0:SHARE, lanes] = value + got[target, :, lanes].astype(F32)

        part_product(name, share_rows(parts[name][1], 2 * target + y), put)

    def both_shares(name, target):
        def put(lanes, value):
            r.wide[:, lanes] = value

        left = parts[name][1]
        lanes = pl.ds(pl.multiple_of(2 * target * SHARE, 2 * SHARE), 2 * SHARE)
        part_product(name, left[:, :, lanes].reshape(T, 2 * SHARE).T, put)

    def z_copy(name, direction, step, device):
        p = parts[name][0]
        return pltpu.make_async_remote_copy(
            src_ref=getattr(r, "zs" + name).at[direction],
            dst_ref=getattr(r, "zr" + name).at[direction, step],
            send_sem=r.z_ss.at[p, direction], recv_sem=r.z_rs.at[p, direction, step],
            device_id=device, device_id_type=MESH,
        )

    def chain_step(name, step):
        out = getattr(r, "zs" + name)
        got = getattr(r, "zr" + name)
        width = parts[name][3]
        total = (r.wide if name in Z_FIRST else r.acc).at[:, 0:width]

        def one(direction, carry):
            place, following = line(direction)

            @pl.when(place <= step)
            def _():
                mirrored = NZ - 1 - step + place
                target = mirrored + direction * (NZ - 1 - 2 * mirrored)
                (both_shares if name in Z_FIRST else share_sum)(name, target)
                if step > 0:

                    @pl.when(place < step)
                    def _():
                        z_copy(name, direction, step - 1, following).wait_send()

                    @pl.when(place > 0)
                    def _():
                        z_copy(name, direction, step - 1, following).wait_recv()
                        total[...] += got[direction, step - 1].astype(F32)

                out[direction] = total[...].astype(BF16)
                z_copy(name, direction, step, following).start()

            return carry

        lax.fori_loop(0, 2, one, 0)

    def chain_end(name):
        got = getattr(r, "zr" + name)
        width = parts[name][3]
        total = (r.wide if name in Z_FIRST else r.acc).at[:, 0:width]
        (both_shares if name in Z_FIRST else share_sum)(name, z)

        def one(direction, carry):
            place, _ = line(direction)

            @pl.when(place > 0)
            def _():
                z_copy(name, direction, NZ - 2, (dp, m)).wait_recv()
                total[...] += got[direction, NZ - 2].astype(F32)

            return carry

        lax.fori_loop(0, 2, one, 0)

    def y_exchange(name):
        chain_end(name)
        width = parts[name][3]
        theirs = pl.ds(pl.multiple_of((1 - y) * SHARE, SHARE), SHARE)
        getattr(r, "ys" + name)[0] = r.wide[theirs, 0:width].astype(BF16)
        y_copy(name, 0).start()

    def a_src(name, share):
        ref = getattr(r, name[0] + "_full")
        at = pl.ds(pl.multiple_of(share * SHARE, SHARE), SHARE)
        if name[0] == "q":
            return ref.at[:, at, span(name)]
        return ref.at[at, span(name)] if name[0] == "u" else ref.at[span(name), at]

    def az_copy(name, side, direction, step, share, src, device):
        p = len(parts) + Y_FIRST.index(name) if side else parts[name][0]
        return pltpu.make_async_remote_copy(
            src_ref=src, dst_ref=a_src(name, share), send_sem=r.az_ss.at[p, direction, step],
            recv_sem=r.az_rs.at[p, direction, step], device_id=device, device_id_type=MESH,
        )

    def ay_copy(name, place, src):
        p = parts[name][0]
        return pltpu.make_async_remote_copy(
            src_ref=src, dst_ref=a_src(name, 2 * place + y), send_sem=r.ay_ss.at[p, place],
            recv_sem=r.ay_rs.at[p, place], device_id=to_y, device_id_type=MESH,
        )

    local_out = []

    def finish_share(name):
        p, _, _, width = parts[name]
        matrix = name[0]
        at0 = span(name)
        if name in Z_FIRST:
            y_copy(name, 0).wait_recv()
            ours = pl.ds(pl.multiple_of(y * SHARE, SHARE), SHARE)
            r.acc[:, 0:width] = r.wide[ours, 0:width] + getattr(r, "yr" + name)[0].astype(F32)
        else:
            chain_end(name)
        for cp in state_in[name]:
            cp.wait()
        grad_out = getattr(r, "gr" + matrix)
        fresh = getattr(r, "nc" + matrix)

        def adam_block(cols, at, state, state_at):
            grad = r.acc[:, cols]
            if matrix in "do":
                grad = grad.T
            grad_out[at] = grad
            w, a, b = adam_step(
                grad,
                state[(0,) + state_at],
                state[(1,) + state_at],
                state[(2,) + state_at],
                decay_rate,
                token_total,
            )
            state[(0,) + state_at] = w
            state[(1,) + state_at] = a
            state[(2,) + state_at] = b
            fresh[at] = w.astype(BF16)

        if matrix == "q":
            for kind in range(3):
                adam_block(
                    slice(kind * PAIR, (kind + 1) * PAIR),
                    (kind, slice(None), at0),
                    r.big,
                    (slice(SHARE, 2 * SHARE), slice(kind * HW + at0.start, kind * HW + at0.stop)),
                )
        else:

            def adam_body(n, carry):
                cols = pl.ds(pl.multiple_of(n * SHARE, SHARE), SHARE)
                there = pl.ds(pl.multiple_of(at0.start + n * SHARE, SHARE), SHARE)
                if matrix == "u":
                    adam_block(cols, (slice(None), there), r.big, (slice(0, SHARE), there))
                else:
                    at = (there, slice(None))
                    adam_block(cols, at, getattr(r, "s" + matrix), at)
                return carry

            lax.fori_loop(0, width // SHARE, adam_body, 0)
        fresh = piece(fresh, name)
        if name in Y_FIRST:
            ay_copy(name, z, fresh).start()
        for direction in range(2):
            place, following = line(direction)

            @pl.when(place < NZ - 1)
            def _():
                az_copy(name, 0, direction, 0, 2 * z + y, fresh, following).start()

        if name not in Y_FIRST:
            ay_copy(name, z, fresh).start()
        local_out.append(local_copy(fresh, a_src(name, 2 * z + y), r.o_sem.at[p, 0]))
        local_out.append(
            local_copy(piece(grad_out, name), piece(getattr(r, matrix + "_grad"), name), r.o_sem.at[p, 1])
        )
        for k, (far, near) in enumerate(state_copies(name, True)):
            local_out.append(local_copy(near, far, state_sem(name, k)))

    def neighbour_share(name):
        part = a_src(name, 2 * z + 1 - y)
        ay_copy(name, z, part).wait_recv()
        for direction in range(2):
            place, following = line(direction)

            @pl.when(place < NZ - 1)
            def _():
                az_copy(name, 1, direction, 0, 2 * z + 1 - y, part, following).start()

    def gather_step(name, step):
        for side in range(2 if name in Y_FIRST else 1):
            for direction in range(2):
                place, following = line(direction)

                @pl.when(place >= step)
                def _():
                    source = z - step + 2 * step * direction
                    share = 2 * source + (1 - y if side else y)
                    part = a_src(name, share)
                    az_copy(name, side, direction, step - 1, share, part, following).wait_recv()
                    if step < NZ - 1:

                        @pl.when(place < NZ - 1)
                        def _():
                            az_copy(name, side, direction, step, share, part, following).start()

                    if name not in Y_FIRST:
                        ay_copy(name, source, part).start()

    def gather_end(name):
        part = a_src(name, 2 * z + y)

        def one(direction, carry):
            place, following = line(direction)

            @pl.when(place <= NZ - 2)
            def _():
                z_copy(name, direction, NZ - 2, following).wait_send()

            for step in range(NZ - 1):

                @pl.when((place >= step) & (place < NZ - 1))
                def _():
                    for side in range(2 if name in Y_FIRST else 1):
                        az_copy(name, side, direction, step, 2 * z + y, part, following).wait_send()

            return carry

        lax.fori_loop(0, 2, one, 0)
        if name in Z_FIRST:
            y_copy(name, 0).wait_send()
        if name in Y_FIRST:
            ay_copy(name, z, part).wait_send()

        def y_body(i, carry):
            if name not in Z_FIRST:
                y_copy(name, i).wait_send()
            if name not in Y_FIRST:
                there = a_src(name, 2 * i + y)
                ay_copy(name, i, there).wait_send()
                ay_copy(name, i, there).wait_recv()
            return carry

        lax.fori_loop(0, NZ, y_body, 0)

    def put_out(src, dst):
        cp = pltpu.make_async_copy(src, dst, r.stage_sem)
        cp.start()
        cp.wait()

    late = {}

    def turn(point):
        if not fast:
            return
        for kind, number in ORDER.get(point, ()):
            name = names_of[number] if number is not None else None
            if kind == V:
                late["vector_next"]()
            elif kind == Y:
                y_start(name)
            elif kind == F:
                finish_share(name)
            elif kind == E:
                y_exchange(name)
            elif kind == H:
                neighbour_share(name)
            elif kind in (C0, C1, C2):
                chain_step(name, kind - C0)
            else:
                gather_step(name, kind - G1 + 1)

    ag = {}
    for j in range(C):
        ag[j] = ag_send(0, j, r.g1)
    count_send(0)

    def w_copy(kind, src, block, device):
        return pltpu.make_async_remote_copy(
            src_ref=src, dst_ref=r.act.at[block], send_sem=r.ow_ss.at[kind],
            recv_sem=r.ow_rs.at[kind], device_id=device, device_id_type=MESH,
        )

    weights[0].wait()
    w_x = w_copy(0, r.wout, m, to_x)
    w_x.start()
    w_c = w_copy(1, r.wout, m, to_core)
    w_c.start()
    r.act[m] = r.wout[...]
    for w in qkv_weights:
        w.wait()

    def project(o):
        p = mm(r.g1[o], r.wqkv[...], NN)
        at = pl.ds(pl.multiple_of(o * R, R), R)
        for pair in range(PAIRS):
            rows = slice(pair * PAIR, (pair + 1) * PAIR)
            lanes = pl.ds(pl.multiple_of(m * HW + pair * PAIR, PAIR), PAIR)
            q, k, v = (p[:, qkv_lanes(pair, kind)] for kind in range(3))
            q = (q + r.vec[6:7, lanes]).astype(BF16)
            k = k.astype(BF16)
            v = (v + r.vec[7:8, lanes]).astype(BF16)
            for kind, value in enumerate((q, k, v)):
                r.qkv[at, qkv_lanes(pair, kind)] = value
            r.qT[rows, at] = q.T
            r.kT[rows, at] = k.T
            r.vT[rows, at] = v.T

    def make_dist(i, start):
        def one(b, carry):
            key = lax.broadcasted_iota(jnp.int32, (BQ, BQ), 0) + b * BQ
            query = lax.broadcasted_iota(jnp.int32, (BQ, BQ), 1) + i * BQ
            apart = query - key
            key_seg = r.segr[:, pl.ds(pl.multiple_of(b * BQ, BQ), BQ)]
            key_seg = jnp.broadcast_to(key_seg, (BQ, BQ)).T
            same = key_seg == r.segr[:, i * BQ : (i + 1) * BQ]
            r.big[b, :, start : start + BQ] = jnp.where((apart >= 0) & same, apart.astype(F32), jnp.inf)
            return carry

        lax.fori_loop(0, i + 1, one, 0)

    n_blocks = T // BQ
    project(m)
    for i in range(n_blocks):
        make_dist(i, i * BQ)
    count_next()
    for j in range(C):
        ag[j][1].wait()
    project(mc)
    for _ in range(1, dp_size.bit_length() - 1):
        count_next()
    fw = {}
    for j in range(C):
        ag[j][0].wait()
        fw[j] = ag_forward(0, j, r.g1)
    project(mx)
    for j in range(C):
        fw[j].wait()
    project(md)

    pair_row = lax.broadcasted_iota(jnp.int32, (2 * HD, BQ), 0) // HD
    pair_lane = lax.broadcasted_iota(jnp.int32, (BQ, 2 * HD), 1) // HD
    scale2 = log2_e / math.sqrt(HD)
    K_AT, V_AT, Q_AT, DIST = 0, HW, 2 * HW, 3 * HW

    def head_slope(h):
        head = jnp.zeros((1, BQ), jnp.int32) + (m * LOCAL_HEADS + h + 1)
        return jnp.exp2(head.astype(F32) * (-8.0 / HEADS)) * log2_e

    def pair_lanes(h, start):
        return pl.ds(pl.multiple_of(start + (h // 2) * PAIR, PAIR), PAIR)

    def kind_lanes(h, kind):
        return pl.ds(pl.multiple_of((h // 2) * 3 * PAIR + kind * PAIR, PAIR), PAIR)

    def head_scores(i, ke, h, start):
        mask = (pair_row == lax.rem(h, 2)).astype(F32).astype(BF16)
        q_cols = r.qT[pair_lanes(h, 0), i * BQ : (i + 1) * BQ] * mask
        raw = mm(r.qkv[0:ke, kind_lanes(h, 1)], q_cols, NN)
        return raw * scale2 - head_slope(h) * r.big[0 : i + 1, :, start : start + BQ].reshape(ke, BQ)

    OWN, PASSING = slice(0, HW), slice(HW, 2 * HW)

    def mix_copy(kind, j, src, dst, device):
        return pltpu.make_async_remote_copy(
            src_ref=src, dst_ref=dst, send_sem=r.mix_ss.at[kind, j], recv_sem=r.mix_rs.at[kind, j],
            device_id=device, device_id_type=MESH,
        )

    def send_mixture(i):
        for j in range(C):
            rows = slice(j * rc, (j + 1) * rc)
            src = r.mix.at[i * BQ + rows.start : i * BQ + rows.stop, :]

            @pl.when(i // 2 != chip)
            def _():
                kind = (core + i) % 2
                lanes = pl.ds(pl.multiple_of(kind * HW, HW), HW)
                mix_copy(kind, j, src, r.gup.at[m, rows, lanes], to_x).start()

            @pl.when(mc == i)
            def _():
                mix_copy(2, j, src, r.gup.at[m, rows, OWN], to_core).start()

            @pl.when(m == i)
            def _():
                r.gup[m, rows, OWN] = src[...]

    for turn_of, i in enumerate([*range(n_blocks - 2), n_blocks - 1, n_blocks - 2]):
        ke = (i + 1) * BQ
        block = slice(i * BQ, (i + 1) * BQ)

        def head_body(h, carry):
            s = head_scores(i, ke, h, i * BQ)
            top = jnp.max(s, 0, keepdims=True)
            e = jnp.exp2(s - top)
            total = jnp.sum(e, 0, keepdims=True)
            p = (e * (1.0 / total)).astype(BF16)
            r.lse[h, :, block] = top + jnp.log2(total)
            at = pl.ds(pl.multiple_of(h * HD, HD), HD)
            r.mixT[at, :] = mm(r.vT[at, 0:ke], p, NN).astype(BF16)
            return carry

        lax.fori_loop(0, LOCAL_HEADS, head_body, 0, unroll=LOCAL_HEADS if i < n_blocks // 2 else 1)
        r.mix[block, :] = r.mixT[...].T
        send_mixture(i)
        if turn_of >= n_blocks - (mp_size.bit_length() - 1):
            count_next()

    def pair_rows(ref, j):
        def of(first):
            v = ref[pl.ds(first, 2), pl.ds(j * rc, rc), :]
            return v.reshape(2 * rc, v.shape[2])

        return of

    def pair_flat(ref, j):
        def of(first):
            a = ref[pl.ds(pl.multiple_of(first * R + j * rc, rc), rc), :]
            b = ref[pl.ds(pl.multiple_of(first * R + R + j * rc, rc), rc), :]
            return jnp.concatenate([a, b], 0)

        return of

    def ag_finish(site, j, ref):
        ag[j][0].wait()
        cf = ag_forward(site, j, ref)
        ag[j][1].wait()
        cf.wait()

    w_x.wait()
    w_f = w_copy(2, r.act.at[mx], mx, to_core)
    w_f.start()
    m_f = {}
    for j in range(C):
        rows = slice(j * rc, (j + 1) * rc)
        here = r.gup.at[m, rows, OWN]
        mix_copy(1, j, here, here, to_x).wait_recv()
        m_f[j] = mix_copy(3, j, r.gup.at[mx, rows, PASSING], r.gup.at[mx, rows, OWN], to_core)
        m_f[j].start()
    w_c.wait()
    w_f.wait()
    rs = {}
    for j in range(C):
        rows = slice(j * rc, (j + 1) * rc)
        here = r.gup.at[m, rows, OWN]
        mix_copy(0, j, here, here, to_x).wait()
        mix_copy(1, j, here, here, to_x).wait_send()
        mix_copy(2, j, here, here, to_core).wait()
        m_f[j].wait()

        def out_body(n, carry):
            lanes = pl.ds(pl.multiple_of(n * TILE, TILE), TILE)
            total = mm(r.gup[0, rows, OWN], r.act[0, :, lanes], NN)
            for q in range(1, mp_size):
                total += mm(r.gup[q, rows, OWN], r.act[q, :, lanes], NN)
            r.keep[j, :, lanes] = total
            return carry

        lax.fori_loop(0, D // TILE, out_body, 0)
        hid = r.x[rows, :].astype(F32) + r.keep[j] + r.vec[2:3, :]
        r.hidden[rows, :] = hid
        normed, inverse = norm_rows(hid)
        r.n2[rows, :] = normed
        r.inv2[rows, :] = inverse
        ag[j] = ag_start(1, j, r.g2, (normed * r.vec[3:4, :] + r.vec[4:5, :]).astype(BF16))

    weights[1].wait()
    weights[2].wait()
    def up_half(j, first):
        pair = pl.ds(first, 2)
        rows = pair_rows(r.g2, j)(first)

        def up_body(n, carry):
            lanes = pl.ds(pl.multiple_of(n * TILE, TILE), TILE)
            u = mm(rows, r.wup[:, lanes], NN) + r.vec[pl.ds(8 + m, 1), lanes]
            a, b = gelu_both(u)
            r.act[pair, pl.ds(j * rc, rc), lanes] = a.astype(BF16).reshape(2, rc, TILE)
            r.big[pair, pl.ds(j * rc, rc), lanes] = b.reshape(2, rc, TILE)
            return carry

        lax.fori_loop(0, FU // TILE, up_body, 0)

    def by_halves(site, gather, ref, half, left, rhs_of):
        own = {}
        for j in range(C):
            ag[j][1].wait()
            half(j, 2 * chip)
            own[j] = rs_own(site, j, pair_rows(left, j), rhs_of)
        for j in range(C):
            ag[j][0].wait()
            ag_forward(gather, j, ref).wait()
            if site == 2 and j == C - 1:
                turn(THIRD)
            half(j, 2 * (1 - chip))
            cx, _ = rs_other(site, j, pair_rows(left, j), rhs_of)
            rs[j] = (cx, own[j])

    by_halves(1, 1, r.g2, up_half, r.act, lambda lanes: (r.wdown[:, lanes], NN))

    t_in.wait()
    loss_scale = token_total / r.cnt[len(bits), 0:1, 0:1]
    for j in range(C):
        rows = slice(j * rc, (j + 1) * rc)
        out = r.hidden[rows, :] + rs_finish(j, rs[j]) + r.vec[5:6, :]
        r.bo[rows, :] = out.astype(BF16)
        valid = jnp.broadcast_to(r.valid[:, rows].astype(F32), (SHARE, rc)).T[:, 0:1]
        grad = valid * (out - r.t[rows, :].astype(F32)) * loss_scale
        r.ig[rows, :] = grad
        ag[j] = ag_start(2, j, r.g3, grad.astype(BF16))
        r.vg[5:6, :] += jnp.sum(grad, 0, keepdims=True)
    bo_out = local_copy(r.bo, r.bo_hbm, r.in_sem.at[3])

    def act_half(j, first):
        pair = pl.ds(first, 2)
        rows = pair_rows(r.g3, j)(first)

        def act_body(n, carry):
            lanes = pl.ds(pl.multiple_of(n * TILE, TILE), TILE)
            ga = mm(rows, r.wdown[lanes, :], NT)
            gu = ga * r.big[pair, pl.ds(j * rc, rc), lanes].reshape(2 * rc, TILE)
            r.gup[pair, pl.ds(j * rc, rc), lanes] = gu.astype(BF16).reshape(2, rc, TILE)
            return carry

        lax.fori_loop(0, FU // TILE, act_body, 0)

    by_halves(2, 2, r.g3, act_half, r.gup, lambda lanes: (r.wup[lanes, :], NT))

    def whole_grad(left, right, width, dst):
        def body(n, carry):
            lanes = pl.ds(pl.multiple_of(n * TILE, TILE), TILE)
            r.stage[:, 0:width] = mm(right_tile(left, lanes), right[...].reshape(T, width), TN)
            put_out(r.stage.at[:, 0:width], dst.at[lanes, :])
            return carry

        lax.fori_loop(0, dst.shape[0] // TILE, body, 0)

    if not fast:
        whole_grad(r.act, r.g3, D, r.d_grad)

    for j in range(C):
        rows = slice(j * rc, (j + 1) * rc)
        gs = rs_finish(j, rs[j])
        gh = r.ig[rows, :] + norm_backward(gs, r.n2[rows, :], r.inv2[rows, :], r.vec[3:4, :])
        r.hidden[rows, :] = gh
        ag[j] = ag_start(3, j, r.g4, gh.astype(BF16))
        r.vg[2:3, :] += jnp.sum(gh, 0, keepdims=True)
        r.vg[3:4, :] += jnp.sum(gs * r.n2[rows, :], 0, keepdims=True)
        r.vg[4:5, :] += jnp.sum(gs, 0, keepdims=True)

    turn(NORM)
    if not fast:
        whole_grad(r.g2, r.gup, FU, r.u_grad)
    r.vg[pl.ds(8 + m, 1), :] = jnp.sum(r.gup[...].reshape(T, FU).astype(F32), 0, keepdims=True)

    for j in range(C):
        ag_finish(3, j, r.g4)

    def gm_body(o, carry):
        at = pl.ds(pl.multiple_of(o * R, R), R)
        gmx = mm(r.g4[o], r.wout[...], NT).astype(BF16)
        r.gm[at, :] = gmx
        r.vT[:, at] = gmx.T
        return carry

    lax.fori_loop(0, mp_size, gm_body, 0)
    turn(FOURTH)

    r.big[:, :, K_AT : K_AT + HW] = jnp.zeros((mp_size, R, HW), F32)
    r.big[:, :, V_AT : V_AT + HW] = jnp.zeros((mp_size, R, HW), F32)
    for pair in range(PAIRS):
        for i in range(n_blocks):
            ke = (i + 1) * BQ
            block = slice(i * BQ, (i + 1) * BQ)
            make_dist(i, DIST)

            def back_body(half, carry):
                h = 2 * pair + half
                row_mask = (pair_row == half).astype(F32).astype(BF16)
                lane_mask = (pair_lane == half).astype(F32).astype(BF16)
                lanes = slice(pair * PAIR, (pair + 1) * PAIR)
                p = jnp.exp2(head_scores(i, ke, h, DIST) - r.lse[h, :, block])
                gp = mm(r.qkv[0:ke, qkv_lanes(pair, 2)], r.vT[lanes, block] * row_mask, NN)
                inner = jnp.sum(p * gp, 0, keepdims=True)
                raw = (p * (gp - inner)).astype(BF16)
                low = p.astype(BF16)
                r.big[0 : i + 1, :, V_AT + lanes.start : V_AT + lanes.stop] += mm(
                    low, r.gm[block, lanes] * lane_mask, NN
                ).reshape(i + 1, BQ, PAIR)
                r.big[0 : i + 1, :, K_AT + lanes.start : K_AT + lanes.stop] += mm(
                    raw, r.qkv[block, qkv_lanes(pair, 0)] * lane_mask, NN
                ).reshape(i + 1, BQ, PAIR)
                at = pl.ds(pl.multiple_of(h * HD, HD), HD)
                r.big[i, at, Q_AT : Q_AT + BQ] = mm(r.kT[at, 0:ke], raw, NN) * (1.0 / math.sqrt(HD))
                return carry

            lax.fori_loop(0, 2, back_body, 0)
            rows = slice(pair * PAIR, (pair + 1) * PAIR)
            r.st[block, qkv_lanes(pair, 0)] = r.big[i, rows, Q_AT : Q_AT + BQ].T.astype(BF16)
            turn((pair, i))
        lanes = slice(pair * PAIR, (pair + 1) * PAIR)
        r.st[:, qkv_lanes(pair, 1)] = (
            r.big[:, :, K_AT + lanes.start : K_AT + lanes.stop].reshape(T, PAIR) * (1.0 / math.sqrt(HD))
        ).astype(BF16)
        r.st[:, qkv_lanes(pair, 2)] = (
            r.big[:, :, V_AT + lanes.start : V_AT + lanes.stop].reshape(T, PAIR).astype(BF16)
        )
        turn((pair,))
    for pair in range(PAIRS):
        lanes = pl.ds(pl.multiple_of(m * HW + pair * PAIR, PAIR), PAIR)
        for row, kind in ((6, 0), (7, 2)):
            r.vg[row : row + 1, lanes] = jnp.sum(
                r.st[:, qkv_lanes(pair, kind)].astype(F32), 0, keepdims=True
            )

    if fast:
        fetch_state("u")
        fetch_state("q")

    for j in range(C):
        rs[j] = rs_start(3, j, pair_flat(r.st, j), lambda lanes: (r.wqkv[lanes, :], NT))

    turn(BACK)
    if not fast:
        whole_grad(r.mix, r.g4, D, r.o_grad)
        whole_grad(r.g1, r.st, 3 * HW, r.q_grad)

    for j in range(C):
        rows = slice(j * rc, (j + 1) * rc)
        gf = rs_finish(j, rs[j])
        normed, inverse = norm_rows(r.x[rows, :].astype(F32))
        r.ig[rows, :] = r.hidden[rows, :] + norm_backward(gf, normed, inverse, r.vec[0:1, :])
        r.vg[0:1, :] += jnp.sum(gf * normed, 0, keepdims=True)
        r.vg[1:2, :] += jnp.sum(gf, 0, keepdims=True)
    ig_out = local_copy(r.ig, r.ig_hbm, r.in_sem.at[4])

    vector_send, vector_step = doubling(mp_bits + dp_bits, r.vs, r.vs_r, r.cnt_ss, r.cnt_rs)
    r.vs[0] = r.vg[...]
    vector_send(0)
    vector_out = []

    def vector_next():
        vector_step()
        late["steps"] = late.get("steps", 0) + 1
        if late["steps"] < len(bits):
            return
        vec_in.wait()
        total = r.vs[len(bits), 0 : r.vec.shape[0]]
        new = adam_step(total, r.vec_state[0], r.vec_state[1], r.vec_state[2], 0.0, token_total)
        r.v_sum[...] = total
        for k in range(3):
            r.vec_state[k] = new[k]
        r.v_copy[...] = new[0].astype(BF16)
        for k, (near, far) in enumerate(
            [(r.v_sum, r.v_grad), (r.vec_state, r.v_new), (r.v_copy, r.v_low)]
        ):
            vector_out.append(local_copy(near, far, r.in_sem.at[5 + k]))

    late["vector_next"] = vector_next
    if fast:
        turn(END)
        for name in parts:
            gather_end(name)
        for cp in local_out:
            cp.wait()
    else:
        for _ in bits:
            vector_next()
    for cp in [bo_out, ig_out] + vector_out:
        cp.wait()


Z_FIRST = ("d0",)
Y_FIRST = ("u1",)
Y, C0, C1, C2, E, F, H, G1, G2, G3, V = range(11)
D0, D1, U0, U1, O0, Q0, Q1 = range(7)
THIRD, NORM, FOURTH, BACK, END = range(5)
ORDER = {
    THIRD: ((Y, D1), (C0, D0),),
    NORM: ((C0, D1), (Y, U0), (C1, D0), (Y, U1), (C1, D1), (C2, D0),),
    FOURTH: ((C0, U0),),
    (0, 1): ((C2, D1),),
    (0, 2): ((E, D0),),
    (0,): ((Y, Q0),),
    (1, 0): ((C0, U1),),
    (1, 1): ((C1, U0),),
    (1, 2): ((C1, U1), (F, D1), (Y, O0),),
    (1, 3): ((F, D0), (C0, Q0), (C2, U1),),
    BACK: (
        (G1, D0), (Y, Q1), (C1, Q0), (G1, D1), (C2, U0), (C0, O0), (F, U1), (C2, Q0), (G2, D1),
    ),
    END: (
        (F, U0), (C1, O0), (C0, Q1), (G3, D1), (G2, D0), (F, Q0), (C2, O0), (V, None), (C1, Q1), (G1, U0),
        (H, U1), (V, None), (G1, Q0), (F, O0), (C2, Q1), (G2, U0), (G1, O0), (F, Q1), (G2, O0), (G2, Q0),
        (G3, Q0), (V, None), (G1, Q1), (G2, Q1), (G1, U1), (G3, U0), (V, None), (G3, Q1), (G2, U1), (G3, D0),
        (V, None), (G3, O0), (G3, U1),
    ),
}


def pieces(head_width, units):
    return [
        ("d0", units // 2),
        ("d1", units // 2),
        ("u0", units // 2),
        ("u1", units // 2),
        ("o0", head_width),
    ] + [("q%d" % pair, 6 * HD) for pair in range(head_width // (2 * HD))]


SHARE = 128


def block_call(sizes, x, teacher, segments, valid, vectors, copies, states):
    dp_size, mp_size = sizes
    R, D = x.shape
    T = mp_size * R
    wqkv, wout, wup, wdown = copies
    HW = wout.shape[0]
    FU = wup.shape[1]
    C = CHUNKS
    rc = R // C
    n_bits = (dp_size * mp_size).bit_length() - 1
    NZ = dp_size // 2
    PAIRS = HW // (2 * HD)
    fast = D == dp_size * SHARE
    dma = pltpu.SemaphoreType.DMA
    M = pltpu.VMEM
    S = jax.ShapeDtypeStruct
    vmem = pl.BlockSpec(memory_space=pltpu.VMEM)
    anywhere = pl.BlockSpec(memory_space=pl.ANY)

    ins = {
        "x_hbm": (x, anywhere),
        "t_hbm": (teacher, anywhere),
        "segr": (segments, vmem),
        "valid": (valid.reshape(1, R), vmem),
        "vec_low": (vectors, vmem),
        "vec_state_hbm": (states[4], anywhere),
        "wqkv_hbm": (wqkv, anywhere),
        "wout_hbm": (wout, anywhere),
        "wup_hbm": (wup, anywhere),
        "wdown_hbm": (wdown, anywhere),
    }
    outs = {
        "bo_hbm": (S((R, D), BF16), anywhere),
        "ig_hbm": (S((R, D), F32), anywhere),
        "v_grad": (S(vectors.shape, F32), anywhere),
        "v_new": (S(states[4].shape, F32), anywhere),
        "v_low": (S(vectors.shape, BF16), anywhere),
    }
    if fast:
        shard = {"q": (3, SHARE, HW), "o": (HW, SHARE), "u": (SHARE, FU), "d": (FU, SHARE)}
        whole = {"q": (3, D, HW), "o": (HW, D), "u": (D, FU), "d": (FU, D)}
        for name, state in zip("qoud", states):
            ins["s%s_hbm" % name] = (state, anywhere)
        for name in "qoud":
            outs[name + "_grad"] = (S(shard[name], F32), anywhere)
        for name in "qoud":
            outs[name + "_new"] = (S((3,) + shard[name], F32), anywhere)
        for name in "qoud":
            outs[name + "_full"] = (S(whole[name], BF16), anywhere)
    else:
        outs["q_grad"] = (S((D, 3 * HW), F32), anywhere)
        outs["o_grad"] = (S((HW, D), F32), anywhere)
        outs["u_grad"] = (S((D, FU), F32), anywhere)
        outs["d_grad"] = (S((FU, D), F32), anywhere)
    scratch = {
        "wqkv": M((D, 3 * HW), BF16),
        "wout": M((HW, D), BF16),
        "wup": M((D, FU), BF16),
        "wdown": M((FU, D), BF16),
        "w_sem": dma((3,)),
        "ow_ss": dma((3,)),
        "ow_rs": dma((3,)),
        "mix_ss": dma((4, C)),
        "mix_rs": dma((4, C)),
        "in_sem": dma((8,)),
        "x": M((R, D), BF16),
        "t": M((R, D), BF16),
        "bo": M((R, D), BF16),
        "ig": M((R, D), F32),
        "vec_state": M(states[4].shape, F32),
        "v_sum": M(vectors.shape, F32),
        "v_copy": M(vectors.shape, BF16),
        "wq_sem": dma((PAIRS, 3)),
        "vec": M(vectors.shape, F32),
        "g1": M((mp_size, R, D), BF16),
        "g2": M((mp_size, R, D), BF16),
        "g3": M((mp_size, R, D), BF16),
        "g4": M((mp_size, R, D), BF16),
        "qkv": M((T, 3 * HW), BF16),
        "qT": M((HW, T), BF16),
        "kT": M((HW, T), BF16),
        "vT": M((HW, T), BF16),
        "mixT": M((HW, BQ), BF16),
        "mix": M((T, HW), BF16),
        "lse": M((HW // HD, 1, T), F32),
        "hidden": M((R, D), F32),
        "n2": M((R, D), F32),
        "inv2": M((R, 1), F32),
        "act": M((mp_size, R, FU), BF16),
        "big": M((mp_size, R, FU), F32),
        "gup": M((mp_size, R, FU), BF16),
        "gm": M((T, HW), BF16),
        "st": M((T, 3 * HW), BF16),
        "pass_on": M((C, rc, D), F32),
        "keep": M((C, rc, D), F32),
        "rs_cs": M((C, 2, rc, D), BF16),
        "rs_cr": M((C, 2, rc, D), BF16),
        "rs_xs": M((C, rc, D), BF16),
        "rs_xr": M((C, rc, D), BF16),
        "cnt": M((n_bits + 1, 8, 128), F32),
        "cnt_r": M((n_bits, 8, 128), F32),
        "vg": M((16, D), F32),
        "vs": M((n_bits + 1, 16, D), F32),
        "vs_r": M((n_bits, 16, D), F32),
        "ag_ss": dma((4, C, 3)),
        "ag_rs": dma((4, C, 3)),
        "rs_ss": dma((3, C, 3)),
        "rs_rs": dma((3, C, 3)),
        "cnt_ss": dma((n_bits,)),
        "cnt_rs": dma((n_bits,)),
    }
    if fast:
        for name, w in pieces(HW, FU):
            shares = 1 if name in Z_FIRST else NZ
            rows = 2 * SHARE if name in Z_FIRST else SHARE
            scratch["ys" + name] = M((shares, SHARE, w), BF16)
            scratch["yr" + name] = M((shares, SHARE, w), BF16)
            scratch["zs" + name] = M((2, rows, w), BF16)
            scratch["zr" + name] = M((2, NZ - 1, rows, w), BF16)
        for name in "qoud":
            scratch["gr" + name] = M(shard[name], F32)
            scratch["nc" + name] = M(shard[name], BF16)
        scratch["sd"] = M((3,) + shard["d"], F32)
        scratch["so"] = M((3,) + shard["o"], F32)
        scratch["acc"] = M((SHARE, FU // 2), F32)
        scratch["wide"] = M((2 * SHARE, FU // 2), F32)
        n = len(pieces(HW, FU))
        scratch["s_sem"] = dma((n + 2 * PAIRS,))
        scratch["o_sem"] = dma((n, 2))
        scratch["y_ss"] = dma((n, NZ))
        scratch["y_rs"] = dma((n, NZ))
        scratch["z_ss"] = dma((n, 2))
        scratch["z_rs"] = dma((n, 2, NZ - 1))
        scratch["az_ss"] = dma((n + len(Y_FIRST), 2, NZ - 1))
        scratch["az_rs"] = dma((n + len(Y_FIRST), 2, NZ - 1))
        scratch["ay_ss"] = dma((n, NZ))
        scratch["ay_rs"] = dma((n, NZ))
    else:
        scratch["stage"] = M((TILE, D), F32)
        scratch["stage_sem"] = dma
    names = list(ins) + list(outs) + list(scratch)
    results = pl.pallas_call(
        functools.partial(block_kernel, sizes, fast, names),
        out_shape=[v[0] for v in outs.values()],
        in_specs=[v[1] for v in ins.values()],
        out_specs=[v[1] for v in outs.values()],
        scratch_shapes=list(scratch.values()),
        compiler_params=pltpu.CompilerParams(
            collective_id=0, has_side_effects=True, vmem_limit_bytes=62 << 20
        ),
        name="block",
    )(*[v[0] for v in ins.values()])
    outs = dict(zip(outs, results))
    if fast:
        names, results = list(outs), list(outs.values())
        outs = dict(zip(names, settle(results)))
    return outs, fast


def settle_kernel(count, *refs):
    sources, results, held = refs[:count], refs[count : 2 * count], refs[2 * count : 3 * count]
    in_sem, out_sem = refs[3 * count :]
    loads = [pltpu.make_async_copy(sources[i], held[i], in_sem.at[i]) for i in range(count)]
    stores = [pltpu.make_async_copy(held[i], results[i], out_sem.at[i]) for i in range(count)]
    for cp in loads:
        cp.start()
    for load, store in zip(loads, stores):
        load.wait()
        store.start()
    for cp in stores:
        cp.wait()


def settle(arrays):
    anywhere = pl.BlockSpec(memory_space=pltpu.HBM)
    dma = pltpu.SemaphoreType.DMA((len(arrays),))
    return pl.pallas_call(
        functools.partial(settle_kernel, len(arrays)),
        out_shape=[jax.ShapeDtypeStruct(a.shape, a.dtype) for a in arrays],
        in_specs=[anywhere] * len(arrays),
        out_specs=[anywhere] * len(arrays),
        scratch_shapes=[pltpu.VMEM(a.shape, a.dtype) for a in arrays] + [dma, dma],
        compiler_params=pltpu.CompilerParams(vmem_limit_bytes=62 << 20),
        name="settle",
    )(*arrays)


def adam_update(gradient, stored, decay_factor, token_total):
    new = adam_step(gradient, stored[0], stored[1], stored[2], decay_factor, token_total)
    return (jnp.stack(new), new[0].astype(jnp.bfloat16))


def shards(
    inputs,
    teacher,
    segments,
    valid_mask,
    qkv_copy,
    out_copy,
    up_copy,
    down_copy,
    vector_copy,
    qkv_state,
    out_state,
    up_state,
    down_state,
    vector_state,
):
    sizes = (lax.axis_size("dp"), lax.axis_size("mp"))
    token_total = inputs.shape[0] * sizes[0] * sizes[1]
    width = inputs.shape[1]
    head_width = qkv_copy.shape[2]
    pairs = head_width // (2 * HD)
    outs, fast = block_call(
        sizes,
        inputs,
        teacher,
        segments,
        valid_mask,
        vector_copy,
        (qkv_copy.transpose(1, 0, 2), out_copy, up_copy, down_copy),
        (qkv_state.transpose(0, 2, 1, 3), out_state, up_state, down_state, vector_state),
    )
    vector_grad, vector_new, vector_low = outs["v_grad"], outs["v_new"], outs["v_low"]
    if fast:
        qkv_grad = outs["q_grad"].transpose(1, 0, 2)
        out_grad, up_grad, down_grad = (outs[n + "_grad"] for n in "oud")
        qkv_new = outs["q_new"].transpose(0, 2, 1, 3)
        out_new, up_new, down_new = (outs[n + "_new"] for n in "oud")
        qkv_full = outs["q_full"].transpose(1, 0, 2)
        out_full, up_full, down_full = (outs[n + "_full"] for n in "oud")
    else:
        qkv_local = outs["q_grad"].reshape(width, pairs, 3, 2 * HD)
        qkv_local = qkv_local.transpose(0, 2, 1, 3).reshape(width, 3, head_width)
        qkv_grad, out_grad, up_grad, down_grad = (
            lax.psum_scatter(qkv_local, "dp", scatter_dimension=0, tiled=True),
            lax.psum_scatter(outs["o_grad"], "dp", scatter_dimension=1, tiled=True),
            lax.psum_scatter(outs["u_grad"], "dp", scatter_dimension=0, tiled=True),
            lax.psum_scatter(outs["d_grad"], "dp", scatter_dimension=1, tiled=True),
        )
        qkv_new, qkv_low = adam_update(qkv_grad, qkv_state, decay_rate, token_total)
        out_new, out_low = adam_update(out_grad, out_state, decay_rate, token_total)
        up_new, up_low = adam_update(up_grad, up_state, decay_rate, token_total)
        down_new, down_low = adam_update(down_grad, down_state, decay_rate, token_total)
        qkv_full, out_full, up_full, down_full = (
            lax.all_gather(qkv_low, "dp", axis=0, tiled=True),
            lax.all_gather(out_low, "dp", axis=1, tiled=True),
            lax.all_gather(up_low, "dp", axis=0, tiled=True),
            lax.all_gather(down_low, "dp", axis=1, tiled=True),
        )
    return (
        outs["bo_hbm"],
        outs["ig_hbm"],
        qkv_grad,
        out_grad,
        up_grad,
        down_grad,
        vector_grad,
        qkv_new,
        out_new,
        up_new,
        down_new,
        vector_new,
        qkv_full,
        out_full,
        up_full,
        down_full,
        vector_low,
    )


def solution(mesh):
    in_specs = (
        P(("dp", "mp"), None),
        P(("dp", "mp"), None),
        P("dp", None),
        P(("dp", "mp")),
        P(None, None, "mp"),
        P("mp", None),
        P(None, "mp"),
        P("mp", None),
        P(),
        P(None, "dp", None, "mp"),
        P(None, "mp", "dp"),
        P(None, "dp", "mp"),
        P(None, "mp", "dp"),
        P(),
    )
    out_specs = (
        P(("dp", "mp"), None),
        P(("dp", "mp"), None),
        P("dp", None, "mp"),
        P("mp", "dp"),
        P("dp", "mp"),
        P("mp", "dp"),
        P(),
        P(None, "dp", None, "mp"),
        P(None, "mp", "dp"),
        P(None, "dp", "mp"),
        P(None, "mp", "dp"),
        P(),
        P(None, None, "mp"),
        P("mp", None),
        P(None, "mp"),
        P("mp", None),
        P(),
    )
    return jax.shard_map(shards, mesh=mesh, in_specs=in_specs, out_specs=out_specs, check_vma=False)
```
